128 devices in a mesh: dev: 128 (over z, y, x, core).
Axes of the slice: x: 4, y: 4, z: 4, core: 2. Of those that a mesh axis runs over, the one named last changes fastest.
Arguments:
- params: float32 [59, 524288], P(None, 'dev'), may hold values from -7000 to 7000, as said below
- cameras: float32 [2, 4, 8], replicated, may hold values from -200 to 3600
- send_lists: int32 [2, 128, 128, 32], P(None, 'dev'), may hold values from 0 to 4095, as said below
- tile_slots: int32 [2, 4096, 256], P(None, 'dev'), may hold values from 0 to 4095, as said below
- tile_ids: int32 [2, 4096], P(None, 'dev'), may hold values from 0 to 129599, as said below
- tile_len: int32 [2, 128, 32], P(None, 'dev'), may hold values from 1 to 256, 4096 in all within a row
- targets: float32 [2, 4096, 3, 256], P(None, 'dev'), may hold values from -4.5 to 5.5
Outputs:
- param_grads: float32 [59, 524288], P(None, 'dev')
- mean_error: float32 [], replicated
The draws below stay inside these ranges and needn't reach their ends.
Inputs may be any that keep to these rules, and one draw needn't show every extreme that they name: `send_lists`: in each batch, the lists of one owner name each of its 4096 Gaussians exactly once. `tile_slots`: in one batch, the 32 lists of one renderer together name each of its 4096 slots exactly twice, both times in tiles of one view; the first tile_len entries of a list are live. `tile_ids`: the tiles of one batch are distinct. `params`: every Gaussian lies at a depth of 500 or more in front of every camera of both batches; quaternions have a first component of 1 to 2.
All inputs are finite; a program needn't handle non-finite values.
Results may differ from the reference program's by a relative error of at most 0.0003.
Values sent between devices are 32-bit elements; how exact they have to be, the bound alone decides.
No kernel may reach another device: no remote copies, remote signals or barrier semaphores. Data moves between devices by JAX's collectives and lax.ppermute only.
A program may use at most 128 MiB of HBM per device.

```python
import math
import jax
import jax.numpy as jnp
import numpy as np
from jax import lax

PARAMS = 59
VIEWS = 4
BATCHES = 2
TILE = 16
IMG_W = 3840
IMG_H = 2160
PAIRS = 256
TILES_DEV = 32
OWNERS = 128
TILE_PX = 256
TILES_X = 240
TILES_VIEW = 32400
RTILES = 4096
SLOTS = 4096
CAP = 32
G_DEV = 4096
GAUSS = 524288


def camera_frame_drawn(camera):
    cos_yaw = jnp.cos(camera[0])
    sin_yaw = jnp.sin(camera[0])
    cos_pitch = jnp.cos(camera[1])
    sin_pitch = jnp.sin(camera[1])
    return ((cos_yaw, 0.0 * cos_yaw, sin_yaw), (sin_pitch * sin_yaw, cos_pitch, -sin_pitch * cos_yaw), (-cos_pitch * sin_yaw, sin_pitch, cos_pitch * cos_yaw))


def pick_pairs(sub_key):
    pair_total = VIEWS * TILES_VIEW // 2
    pair_count = RTILES // 2
    shuffled = jax.random.permutation(sub_key, pair_total).astype(jnp.int32)
    ranking = jnp.where(shuffled == pair_total - 1, -2, jnp.where(shuffled == 0, -1, jnp.arange(pair_total, dtype=jnp.int32)))
    chosen = shuffled[jnp.argsort(ranking)][:pair_count]
    chosen = chosen[jax.random.permutation(jax.random.fold_in(sub_key, 5), pair_count)]
    half_view = TILES_VIEW // 2
    view_no = chosen // half_view
    within = chosen % half_view
    row_no = within // (TILES_X // 2)
    col_no = 2 * (within % (TILES_X // 2))
    return (view_no * TILES_VIEW + row_no * TILES_X + col_no).astype(jnp.int32)


def perm_of(size_n):

    def make(sub_key):
        return jax.random.permutation(sub_key, size_n).astype(jnp.int32)
    return make


def layout(key):
    key_own = jax.random.fold_in(key, 101)
    key_group = jax.random.fold_in(key, 102)
    key_pair = jax.random.fold_in(key, 103)
    key_cam = jax.random.fold_in(key, 104)
    key_rend = jax.random.fold_in(key, 105)
    key_cap = jax.random.fold_in(key, 106)
    key_loc = jax.random.fold_in(key, 107)
    key_jit = jax.random.fold_in(key, 108)
    pair_dev = TILES_DEV // 2
    owner_perm = jax.vmap(perm_of(G_DEV))(jax.random.split(key_own, OWNERS))
    group_order = jax.vmap(perm_of(SLOTS))(jax.random.split(key_group, OWNERS))
    pair_left = pick_pairs(key_pair).reshape(OWNERS, pair_dev)
    group_rend = jax.vmap(perm_of(OWNERS))(jax.random.split(key_rend, BATCHES))
    cap_perm = jax.vmap(perm_of(CAP))(jax.random.split(key_cap, BATCHES * OWNERS * OWNERS)).reshape(BATCHES, OWNERS, OWNERS, CAP)
    loc_perm = jax.vmap(perm_of(TILES_DEV))(jax.random.split(key_loc, BATCHES * OWNERS)).reshape(BATCHES, OWNERS, TILES_DEV)
    lower_end = jnp.array([-0.15, -0.15, -198.0, -198.0, -198.0, 3000.0, 0.5 * IMG_W - 18.0, 0.5 * IMG_H - 18.0], jnp.float32)
    upper_end = jnp.array([0.15, 0.15, 198.0, 198.0, 198.0, 3590.0, 0.5 * IMG_W + 18.0, 0.5 * IMG_H + 18.0], jnp.float32)
    jitter_size = jnp.array([0.0005, 0.0005, 2.0, 2.0, 2.0, 10.0, 2.0, 2.0], jnp.float32)
    cam_unit = jax.random.uniform(key_cam, (VIEWS, 8), jnp.float32)
    base_cams = lower_end + (upper_end - lower_end) * cam_unit
    jitter = jax.random.uniform(key_jit, (BATCHES, VIEWS, 8), jnp.float32, -1.0, 1.0) * jitter_size
    later = (jnp.arange(BATCHES) > 0).astype(jnp.float32)[:, None, None]
    cameras = base_cams[None, :, :] + jitter * later
    return (owner_perm, group_order, pair_left, group_rend, cap_perm, loc_perm, cameras)


def draw_cameras(key, part):
    owner_perm, group_order, pair_left, group_rend, cap_perm, loc_perm, cameras = layout(key)
    return cameras


def draw_send_lists(key, part):
    owner_perm, group_order, pair_left, group_rend, cap_perm, loc_perm, cameras = layout(key)
    owner_grouped = owner_perm.reshape(OWNERS, OWNERS, CAP)
    owner_idx = jnp.arange(OWNERS)[None, :, None, None]
    group_idx = jnp.arange(OWNERS)[None, None, :, None]
    source = owner_grouped[owner_idx, group_idx, cap_perm]
    inv_rend = jnp.argsort(group_rend, axis=1).astype(jnp.int32)
    batch_idx = jnp.arange(BATCHES)[:, None, None, None]
    return source[batch_idx, jnp.arange(OWNERS)[None, :, None, None], inv_rend[:, None, :, None], jnp.arange(CAP)[None, None, None, :]]


def draw_tile_slots(key, part):
    owner_perm, group_order, pair_left, group_rend, cap_perm, loc_perm, cameras = layout(key)
    cap_inv = jnp.argsort(cap_perm, axis=3).astype(jnp.int32)
    group_lists = group_order.reshape(OWNERS, TILES_DEV // 2, PAIRS)
    batch_idx = jnp.arange(BATCHES)[:, None, None, None]
    group_idx = jnp.arange(OWNERS)[None, :, None, None]
    entries = group_lists[group_idx, (loc_perm // 2)[:, :, :, None], jnp.arange(PAIRS)[None, None, None, :]]
    owner_no = entries // CAP
    slot_no = owner_no * CAP + cap_inv[batch_idx, owner_no, group_idx, entries % CAP]
    inv_rend = jnp.argsort(group_rend, axis=1).astype(jnp.int32)
    placed = slot_no[jnp.arange(BATCHES)[:, None], inv_rend]
    return placed.reshape(BATCHES, RTILES, PAIRS)


def draw_tile_ids(key, part):
    owner_perm, group_order, pair_left, group_rend, cap_perm, loc_perm, cameras = layout(key)
    group_idx = jnp.arange(OWNERS)[None, :, None]
    ids = pair_left[group_idx, loc_perm // 2] + loc_perm % 2
    inv_rend = jnp.argsort(group_rend, axis=1).astype(jnp.int32)
    placed = ids[jnp.arange(BATCHES)[:, None], inv_rend]
    return placed.reshape(BATCHES, RTILES)


def draw_params(key, part):
    owner_perm, group_order, pair_left, group_rend, cap_perm, loc_perm, cameras = layout(key)
    key = jax.random.fold_in(key, 7)
    inverse_own = jnp.argsort(owner_perm, axis=1).astype(jnp.int32).reshape(GAUSS)
    owner_of = jnp.arange(GAUSS, dtype=jnp.int32) // G_DEV
    group_of = inverse_own // CAP
    entry_of = owner_of * CAP + inverse_own % CAP
    inverse_group = jnp.argsort(group_order, axis=1).astype(jnp.int32)
    position = inverse_group[group_of, entry_of]
    pair_of = position // PAIRS
    depth_rank = (position % PAIRS).astype(jnp.float32)
    tile_id = pair_left[group_of, pair_of]
    cam_cols = cameras[0, tile_id // TILES_VIEW].T
    in_view = tile_id % TILES_VIEW
    unit_draw = jax.random.uniform(key, (10, GAUSS), jnp.float32)
    screen_u = ((in_view % TILES_X).astype(jnp.float32) + 0.5 + unit_draw[0]) * TILE
    screen_v = ((in_view // TILES_X).astype(jnp.float32) + 1.5 * unit_draw[1] - 0.25) * TILE
    depth = 3000.0 + 3000.0 * (depth_rank + unit_draw[2]) / PAIRS
    focal_len = cam_cols[5]
    cam_pt = ((screen_u - cam_cols[6]) * depth / focal_len, (screen_v - cam_cols[7]) * depth / focal_len, depth)
    cam_frame = camera_frame_drawn(cam_cols)
    cam_shift = (cam_cols[2], cam_cols[3], cam_cols[4])
    world = [cam_frame[0][row_i] * (cam_pt[0] - cam_shift[0]) + cam_frame[1][row_i] * (cam_pt[1] - cam_shift[1]) + cam_frame[2][row_i] * (cam_pt[2] - cam_shift[2]) for row_i in range(3)]
    log_scale = [jnp.log(depth / focal_len) + jnp.log(1.5) + jnp.log(4.0) * unit_draw[3 + axis_k] for axis_k in range(3)]
    quats = [1.0 + unit_draw[6], 2.0 * unit_draw[7] - 1.0, 2.0 * unit_draw[8] - 1.0, 2.0 * unit_draw[9] - 1.0]
    key_opac = jax.random.fold_in(key, 1)
    key_shade = jax.random.fold_in(key, 2)
    dc_factor = jnp.where((jnp.arange(48) % 16 == 0)[:, None], 1.0, 0.5)
    opacity_logit = -4.5 + 2.5 * jax.random.uniform(key_opac, (GAUSS,), jnp.float32)
    sh_rows = jnp.clip(jax.random.normal(key_shade, (48, GAUSS), jnp.float32), -4.0, 4.0) * dc_factor
    head = jnp.stack(world + log_scale + quats + [opacity_logit])
    return jnp.concatenate([head, sh_rows], axis=0).astype(jnp.float32)


def draw_targets(key, part):
    key = jax.random.fold_in(key, 9)
    row_pos = jnp.arange(RTILES, dtype=jnp.float32) / RTILES
    noise = jnp.clip(jax.random.normal(key, (BATCHES, RTILES, 3, TILE_PX), jnp.float32), -4.0, 4.0)
    row_scale = 0.3 + 0.9 * row_pos
    base_level = 0.5
    return (base_level + noise * row_scale[None, :, None, None]).astype(jnp.float32)


def split_up(amount, total, most, skew):
    portions = [(1 << 20) // math.isqrt(rank ** skew) + 1 for rank in range(2, amount + 1)]
    surplus, given = total - most - (amount - 1), [1] * (amount - 1)
    while surplus > 0:
        candidates = [i for i in range(amount - 1) if given[i] < most]
        pool, left = sum([portions[i] for i in candidates]), surplus
        for i in candidates:
            more = min(most - given[i], max(1, left * portions[i] // pool), surplus)
            given[i] = given[i] + more
            surplus = surplus - more
    return np.array([most] + given)


def ragged_sizes(rng, count, total, bound, lean):
    if count == 2:
        one = jax.random.randint(rng, (), max(1, total - bound), min(bound, total - 1) + 1)
        return jnp.stack([one, total - one])
    tallies = jnp.asarray(split_up(count, total, bound, lean), jnp.int32)
    pairs = (count - 1) // 2
    giver, taker = tallies[1:1 + 2 * pairs:2], tallies[2:2 + 2 * pairs:2]
    slack = jnp.minimum(giver - 1, bound - taker)
    moved = jax.random.randint(jax.random.fold_in(rng, 1), (pairs,), 0, 1 << 20) % (slack + 1)
    tallies = tallies.at[1:1 + 2 * pairs:2].set(giver - moved).at[2:2 + 2 * pairs:2].set(taker + moved)
    return tallies[jax.random.permutation(jax.random.fold_in(rng, 2), count)]


def setup_inputs(seed: int = 0) -> dict:
    seeds = jax.random.split(jax.random.key(seed), 8)
    params = draw_params(jax.random.fold_in(seeds[7], 71), 0)
    cameras = draw_cameras(jax.random.fold_in(seeds[7], 71), 0)
    send_lists = draw_send_lists(jax.random.fold_in(seeds[7], 71), 0)
    tile_slots = draw_tile_slots(jax.random.fold_in(seeds[7], 71), 0)
    tile_ids = draw_tile_ids(jax.random.fold_in(seeds[7], 71), 0)
    tile_len = jax.vmap(lambda own: ragged_sizes(own, TILES_DEV, TILES_DEV * PAIRS // 2, PAIRS, 2))(jax.random.split(seeds[5], BATCHES * OWNERS)).reshape((BATCHES, OWNERS, TILES_DEV)).astype(jnp.int32)
    targets = draw_targets(jax.random.fold_in(seeds[7], 71), 0)
    return dict(params=params, cameras=cameras, send_lists=send_lists, tile_slots=tile_slots, tile_ids=tile_ids, tile_len=tile_len, targets=targets)


SH_ZERO = 0.28209479177387814
SH_ONE = 0.4886025119029199
SH_TWO = (1.0925484305920792, -1.0925484305920792, 0.31539156525252005, -1.0925484305920792, 0.5462742152960396)
SH_THREE = (-0.5900435899266435, 2.890611442640554, -0.4570457994644658, 0.3731763325901154, -0.4570457994644658, 1.445305721320277, -0.5900435899266435)

def camera_frame(camera):
    cos_yaw = jnp.cos(camera[0])
    sin_yaw = jnp.sin(camera[0])
    cos_pitch = jnp.cos(camera[1])
    sin_pitch = jnp.sin(camera[1])
    return ((cos_yaw, 0.0 * cos_yaw, sin_yaw), (sin_pitch * sin_yaw, cos_pitch, -sin_pitch * cos_yaw), (-cos_pitch * sin_yaw, sin_pitch, cos_pitch * cos_yaw))

def sh_basis(dir_x, dir_y, dir_z):
    square_x = dir_x * dir_x
    square_y = dir_y * dir_y
    square_z = dir_z * dir_z
    unit_row = jnp.ones_like(dir_x)
    return [SH_ZERO * unit_row, -SH_ONE * dir_y, SH_ONE * dir_z, -SH_ONE * dir_x, SH_TWO[0] * dir_x * dir_y, SH_TWO[1] * dir_y * dir_z, SH_TWO[2] * (2.0 * square_z - square_x - square_y), SH_TWO[3] * dir_x * dir_z, SH_TWO[4] * (square_x - square_y), SH_THREE[0] * dir_y * (3.0 * square_x - square_y), SH_THREE[1] * dir_x * dir_y * dir_z, SH_THREE[2] * dir_y * (4.0 * square_z - square_x - square_y), SH_THREE[3] * dir_z * (2.0 * square_z - 3.0 * square_x - 3.0 * square_y), SH_THREE[4] * dir_x * (4.0 * square_z - square_x - square_y), SH_THREE[5] * dir_z * (square_x - square_y), SH_THREE[6] * dir_x * (square_x - 3.0 * square_y)]

def project(columns, camera):
    cam_frame = camera_frame(camera)
    cam_shift = (camera[2], camera[3], camera[4])
    focal_len = camera[5]
    world_pt = (columns[0], columns[1], columns[2])
    viewed = [cam_frame[row_i][0] * world_pt[0] + cam_frame[row_i][1] * world_pt[1] + cam_frame[row_i][2] * world_pt[2] + cam_shift[row_i] for row_i in range(3)]
    inv_depth = 1.0 / viewed[2]
    screen_u = focal_len * viewed[0] * inv_depth + camera[6]
    screen_v = focal_len * viewed[1] * inv_depth + camera[7]
    quat_len = jnp.sqrt(columns[6] * columns[6] + columns[7] * columns[7] + columns[8] * columns[8] + columns[9] * columns[9])
    quat_w = columns[6] / quat_len
    quat_x = columns[7] / quat_len
    quat_y = columns[8] / quat_len
    quat_z = columns[9] / quat_len
    rotation = ((1.0 - 2.0 * (quat_y * quat_y + quat_z * quat_z), 2.0 * (quat_x * quat_y - quat_w * quat_z), 2.0 * (quat_x * quat_z + quat_w * quat_y)), (2.0 * (quat_x * quat_y + quat_w * quat_z), 1.0 - 2.0 * (quat_x * quat_x + quat_z * quat_z), 2.0 * (quat_y * quat_z - quat_w * quat_x)), (2.0 * (quat_x * quat_z - quat_w * quat_y), 2.0 * (quat_y * quat_z + quat_w * quat_x), 1.0 - 2.0 * (quat_x * quat_x + quat_y * quat_y)))
    spread = (jnp.exp(columns[3]), jnp.exp(columns[4]), jnp.exp(columns[5]))
    shaped = [[(cam_frame[row_i][0] * rotation[0][col_j] + cam_frame[row_i][1] * rotation[1][col_j] + cam_frame[row_i][2] * rotation[2][col_j]) * spread[col_j] for col_j in range(3)] for row_i in range(3)]
    jac_main = focal_len * inv_depth
    jac_u = -focal_len * viewed[0] * inv_depth * inv_depth
    jac_v = -focal_len * viewed[1] * inv_depth * inv_depth
    along_u = [jac_main * shaped[0][col_j] + jac_u * shaped[2][col_j] for col_j in range(3)]
    along_v = [jac_main * shaped[1][col_j] + jac_v * shaped[2][col_j] for col_j in range(3)]
    cov_uu = along_u[0] * along_u[0] + along_u[1] * along_u[1] + along_u[2] * along_u[2] + 0.3
    cov_uv = along_u[0] * along_v[0] + along_u[1] * along_v[1] + along_u[2] * along_v[2]
    cov_vv = along_v[0] * along_v[0] + along_v[1] * along_v[1] + along_v[2] * along_v[2] + 0.3
    determinant = cov_uu * cov_vv - cov_uv * cov_uv
    centre = [-(cam_frame[0][row_i] * cam_shift[0] + cam_frame[1][row_i] * cam_shift[1] + cam_frame[2][row_i] * cam_shift[2]) for row_i in range(3)]
    ray_dir = [world_pt[row_i] - centre[row_i] for row_i in range(3)]
    ray_len = jnp.sqrt(ray_dir[0] * ray_dir[0] + ray_dir[1] * ray_dir[1] + ray_dir[2] * ray_dir[2])
    sh_values = sh_basis(ray_dir[0] / ray_len, ray_dir[1] / ray_len, ray_dir[2] / ray_len)
    colors = []
    for channel in range(3):
        shaded = 0.5
        for sh_term in range(16):
            shaded = shaded + sh_values[sh_term] * columns[11 + 16 * channel + sh_term]
        colors.append(shaded)
    return jnp.stack([screen_u, screen_v, cov_vv / determinant, -cov_uv / determinant, cov_uu / determinant, jax.nn.sigmoid(columns[10])] + colors)

def tile_pixels(tile_id):
    in_view = tile_id % TILES_VIEW
    row_t = in_view // TILES_X
    col_t = in_view % TILES_X
    pixel_no = jnp.arange(TILE_PX, dtype=jnp.int32)
    pix_u = (col_t * TILE + pixel_no % TILE).astype(jnp.float32) + 0.5
    pix_v = (row_t * TILE + pixel_no // TILE).astype(jnp.float32) + 0.5
    return (pix_u, pix_v)

def tile_error(features, live_mask, pix_u, pix_v, target):
    off_u = pix_u[:, None] - features[0][None, :]
    off_v = pix_v[:, None] - features[1][None, :]
    exponent = -0.5 * (features[2] * off_u * off_u + features[4] * off_v * off_v) - features[3] * off_u * off_v
    alphas = features[5] * jnp.exp(exponent) * live_mask
    keep_log = jnp.log1p(-alphas)
    running = jnp.cumsum(keep_log, axis=1)
    before = jnp.concatenate([jnp.zeros_like(running[:, :1]), running[:, :-1]], axis=1)
    weight = jnp.exp(before) * alphas
    pixel_color = jnp.einsum('cp,xp->cx', features[6:9], weight, precision=lax.Precision.HIGHEST)
    residual = pixel_color - target
    return jnp.sum(residual * residual)

def reference(params, cameras, send_lists, tile_slots, tile_ids, tile_len, targets):
    grad_sum = jnp.zeros(params.shape, jnp.float32)
    error_sum = jnp.zeros((), jnp.float32)
    valid_pos = jnp.arange(PAIRS, dtype=jnp.int32)
    renderer = (jnp.arange(RTILES, dtype=jnp.int32) // TILES_DEV)[:, None]
    for batch_no in range(BATCHES):
        pair_slots = tile_slots[batch_no]
        source = pair_slots // CAP
        local_idx = send_lists[batch_no][source, renderer, pair_slots % CAP]
        gauss_of = source * G_DEV + local_idx
        lengths = tile_len[batch_no].reshape(RTILES)
        batch_cams = cameras[batch_no]

        def one_tile(tile_items):
            gauss_idx, tile_id, length, target = tile_items
            camera = batch_cams[tile_id // TILES_VIEW]
            pix_u, pix_v = tile_pixels(tile_id)
            live_mask = (valid_pos < length).astype(jnp.float32)

            def tile_loss(columns):
                return tile_error(project(columns, camera), live_mask, pix_u, pix_v, target)
            return jax.value_and_grad(tile_loss)(params[:, gauss_idx])
        errors, row_grads = lax.map(one_tile, (gauss_of, tile_ids[batch_no], lengths, targets[batch_no]))
        error_sum = error_sum + jnp.sum(errors)
        flat_grads = jnp.transpose(row_grads, (1, 0, 2)).reshape(PARAMS, RTILES * PAIRS)
        grad_sum = grad_sum.at[:, gauss_of.reshape(RTILES * PAIRS)].add(flat_grads)
    mean_error = error_sum / (BATCHES * RTILES * 3 * TILE_PX)
    return (grad_sum, mean_error)
```

```python
import functools

import jax
import jax.numpy as jnp
from jax import lax
from jax.experimental import pallas as pl
from jax.experimental.pallas import tpu as pltpu
from jax.sharding import PartitionSpec as P

BATCHES = 2
TILE = 16
PAIRS = 256
TILE_PX = 256
TILES_X = 240
TILES_VIEW = 32400
VIEWS = 4
PARAMS = 59
TILES_DEV = 32
OWNERS = 128
CAP = 32
SLOTS = 4096
GROUPS = 4
LOG2_E = 1.4426950408889634
VMEM_BYTES = 56 * 1024 * 1024

SH_ZERO = 0.28209479177387814
SH_ONE = 0.4886025119029199
SH_TWO = (
    1.0925484305920792,
    -1.0925484305920792,
    0.31539156525252005,
    -1.0925484305920792,
    0.5462742152960396,
)
SH_THREE = (
    -0.5900435899266435,
    2.890611442640554,
    -0.4570457994644658,
    0.3731763325901154,
    -0.4570457994644658,
    1.445305721320277,
    -0.5900435899266435,
)

F32 = jnp.float32
BF16 = jnp.bfloat16
NN = (((1,), (0,)), ((), ()))
NT = (((1,), (1,)), ((), ()))
TN = (((0,), (0,)), ((), ()))


def dot(lhs, rhs, dims):
    return lax.dot_general(lhs, rhs, dims, preferred_element_type=F32)


def split2(value):
    high = value.astype(BF16).astype(F32)
    return high, value - high


def camera_table(cameras):
    cos_yaw = jnp.cos(cameras[:, :, 0])
    sin_yaw = jnp.sin(cameras[:, :, 0])
    cos_pitch = jnp.cos(cameras[:, :, 1])
    sin_pitch = jnp.sin(cameras[:, :, 1])
    frame = [
        cos_yaw,
        sin_yaw,
        sin_pitch * sin_yaw,
        cos_pitch,
        -sin_pitch * cos_yaw,
        -cos_pitch * sin_yaw,
        sin_pitch,
        cos_pitch * cos_yaw,
    ]
    shift = [cameras[:, :, 2], cameras[:, :, 3], cameras[:, :, 4]]
    centre = [
        -(frame[0] * shift[0] + frame[2] * shift[1] + frame[5] * shift[2]),
        -(frame[3] * shift[1] + frame[6] * shift[2]),
        -(frame[1] * shift[0] + frame[4] * shift[1] + frame[7] * shift[2]),
    ]
    rest = [cameras[:, :, 5], cameras[:, :, 6], cameras[:, :, 7]]
    return jnp.stack(frame + shift + centre + rest)


CAM_ROWS = 17


def sh_basis(dir_x, dir_y, dir_z):
    square_x = dir_x * dir_x
    square_y = dir_y * dir_y
    square_z = dir_z * dir_z
    return [
        SH_ZERO * jnp.ones_like(dir_x),
        -SH_ONE * dir_y,
        SH_ONE * dir_z,
        -SH_ONE * dir_x,
        SH_TWO[0] * dir_x * dir_y,
        SH_TWO[1] * dir_y * dir_z,
        SH_TWO[2] * (2.0 * square_z - square_x - square_y),
        SH_TWO[3] * dir_x * dir_z,
        SH_TWO[4] * (square_x - square_y),
        SH_THREE[0] * dir_y * (3.0 * square_x - square_y),
        SH_THREE[1] * dir_x * dir_y * dir_z,
        SH_THREE[2] * dir_y * (4.0 * square_z - square_x - square_y),
        SH_THREE[3] * dir_z * (2.0 * square_z - 3.0 * square_x - 3.0 * square_y),
        SH_THREE[4] * dir_x * (4.0 * square_z - square_x - square_y),
        SH_THREE[5] * dir_z * (square_x - square_y),
        SH_THREE[6] * dir_x * (square_x - 3.0 * square_y),
    ]


def project_geometry(cols, cam):
    zero = jnp.zeros_like(cam[0])
    frame = ((cam[0], zero, cam[1]), (cam[2], cam[3], cam[4]), (cam[5], cam[6], cam[7]))
    shift = cam[8:11]
    focal = cam[14]
    viewed = [
        frame[0][0] * cols[0] + frame[0][2] * cols[2] + shift[0],
        frame[1][0] * cols[0] + frame[1][1] * cols[1] + frame[1][2] * cols[2] + shift[1],
        frame[2][0] * cols[0] + frame[2][1] * cols[1] + frame[2][2] * cols[2] + shift[2],
    ]
    inv_depth = 1.0 / viewed[2]
    screen_u = focal * viewed[0] * inv_depth + cam[15]
    screen_v = focal * viewed[1] * inv_depth + cam[16]
    inv_quat = 1.0 / jnp.sqrt(
        cols[6] * cols[6] + cols[7] * cols[7] + cols[8] * cols[8] + cols[9] * cols[9]
    )
    quat_w, quat_x, quat_y, quat_z = [cols[6 + i] * inv_quat for i in range(4)]
    rotation = (
        (
            1.0 - 2.0 * (quat_y * quat_y + quat_z * quat_z),
            2.0 * (quat_x * quat_y - quat_w * quat_z),
            2.0 * (quat_x * quat_z + quat_w * quat_y),
        ),
        (
            2.0 * (quat_x * quat_y + quat_w * quat_z),
            1.0 - 2.0 * (quat_x * quat_x + quat_z * quat_z),
            2.0 * (quat_y * quat_z - quat_w * quat_x),
        ),
        (
            2.0 * (quat_x * quat_z - quat_w * quat_y),
            2.0 * (quat_y * quat_z + quat_w * quat_x),
            1.0 - 2.0 * (quat_x * quat_x + quat_y * quat_y),
        ),
    )
    spread = [jnp.exp(cols[3 + i]) for i in range(3)]
    jac_main = focal * inv_depth
    jac_u = -jac_main * viewed[0] * inv_depth
    jac_v = -jac_main * viewed[1] * inv_depth
    row_u = [
        jac_main * frame[0][0] + jac_u * frame[2][0],
        jac_u * frame[2][1],
        jac_main * frame[0][2] + jac_u * frame[2][2],
    ]
    row_v = [jac_main * frame[1][i] + jac_v * frame[2][i] for i in range(3)]
    along_u = [
        (row_u[0] * rotation[0][j] + row_u[1] * rotation[1][j] + row_u[2] * rotation[2][j])
        * spread[j]
        for j in range(3)
    ]
    along_v = [
        (row_v[0] * rotation[0][j] + row_v[1] * rotation[1][j] + row_v[2] * rotation[2][j])
        * spread[j]
        for j in range(3)
    ]
    cov_uu = along_u[0] * along_u[0] + along_u[1] * along_u[1] + along_u[2] * along_u[2] + 0.3
    cov_uv = along_u[0] * along_v[0] + along_u[1] * along_v[1] + along_u[2] * along_v[2]
    cov_vv = along_v[0] * along_v[0] + along_v[1] * along_v[1] + along_v[2] * along_v[2] + 0.3
    inv_det = 1.0 / (cov_uu * cov_vv - cov_uv * cov_uv)
    return screen_u, screen_v, cov_vv * inv_det, -cov_uv * inv_det, cov_uu * inv_det


def ray_basis(position, cam):
    ray = [position[i] - cam[11 + i] for i in range(3)]
    inv_len = 1.0 / jnp.sqrt(ray[0] * ray[0] + ray[1] * ray[1] + ray[2] * ray[2])
    return sh_basis(ray[0] * inv_len, ray[1] * inv_len, ray[2] * inv_len)


def pick_camera(cam_ref, batch_no, view):
    picked = []
    for row in range(CAM_ROWS):
        value = jnp.full(view.shape, cam_ref[row, batch_no, VIEWS - 1], F32)
        for view_no in range(VIEWS - 2, -1, -1):
            value = jnp.where(view == view_no, cam_ref[row, batch_no, view_no], value)
        picked.append(value)
    return picked


def view_kernel(ids_ref, slots_ref, out_ref):
    row_own = lax.broadcasted_iota(jnp.int32, (OWNERS, PAIRS), 0)
    row_cap = lax.broadcasted_iota(jnp.int32, (CAP, PAIRS), 0)

    def step(tile_no, sums):
        out = []
        for batch_no in range(BATCHES):
            view = (ids_ref[batch_no, tile_no] // TILES_VIEW).astype(F32) * 0.5
            slots = slots_ref[batch_no, pl.ds(tile_no, 1), :]
            lhs = jnp.where(row_own == (slots >> 5), view, 0.0).astype(BF16)
            rhs = jnp.where(row_cap == (slots & 31), 1.0, 0.0).astype(BF16)
            out.append(sums[batch_no] + dot(lhs, rhs, NT))
        return tuple(out)

    zero = jnp.zeros((OWNERS, CAP), F32)
    sums = lax.fori_loop(0, TILES_DEV, step, (zero, zero))
    for batch_no in range(BATCHES):
        out_ref[:, batch_no * CAP : (batch_no + 1) * CAP] = sums[batch_no]


def scatter_rhs(index):
    row = lax.broadcasted_iota(jnp.int32, (256, index.shape[1]), 0)
    return jnp.where(row == (index & 255), 1.0, 0.0).astype(BF16)


def project_kernel(cam_ref, params_ref, view_ref, send_ref, out_ref, vg_ref, tab_ref):
    row_a = lax.broadcasted_iota(jnp.int32, (16, 256), 0)

    for batch_no in range(BATCHES):

        def place(chunk, total, batch_no=batch_no):
            index = send_ref[batch_no, pl.ds(chunk, 1), :]
            view = view_ref[batch_no, pl.ds(chunk, 1), :]
            lhs = jnp.where(row_a == (index >> 8), view, 0.0).astype(BF16)
            return total + dot(lhs, scatter_rhs(index), NT)

        vg_ref[batch_no] = lax.fori_loop(0, 16, place, jnp.zeros((16, 256), F32))

    def block(block_no, carry):
        row0 = pl.multiple_of((block_no // 2) * 8, 8)
        half = block_no % 2
        lane0 = pl.multiple_of(half * 128, 128)
        cols = [params_ref[p, pl.ds(row0, 8), pl.ds(lane0, 128)] for p in range(PARAMS)]
        opac = -(jnp.maximum(-cols[10], 0.0) + jnp.log1p(jnp.exp(-jnp.abs(cols[10]))))
        for batch_no in range(BATCHES):
            view = vg_ref[batch_no, pl.ds(row0, 8), pl.ds(lane0, 128)]
            cam = pick_camera(cam_ref, batch_no, view)
            feats = list(project_geometry(cols, cam)) + [opac]
            basis = ray_basis(cols[0:3], cam)
            for channel in range(3):
                shade = 0.5
                for term in range(16):
                    shade = shade + basis[term] * cols[11 + 16 * channel + term]
                feats.append(shade)
            for f, value in enumerate(feats):
                start = (2 * row0 + half) * 16 + f
                tab_ref[batch_no, pl.ds(start, 8, stride=32), :] = value
        return carry

    lax.fori_loop(0, 4, block, 0)

    for batch_no in range(BATCHES):

        def pick(chunk, carry, batch_no=batch_no):
            both = send_ref[batch_no, pl.ds(chunk, 1), :]
            for half in range(2):
                index = jnp.broadcast_to(both[:, half * 128 : half * 128 + 128], (8, 128))
                low = index & 127
                high = index >> 7
                acc0 = jnp.zeros((8, 128), F32)
                acc1 = jnp.zeros((8, 128), F32)
                for h in range(32):
                    hit = high == h
                    got0 = jnp.take_along_axis(
                        tab_ref[batch_no, h * 16 : h * 16 + 8, :], low, axis=1,
                        mode="promise_in_bounds",
                    )
                    got1 = jnp.take_along_axis(
                        tab_ref[batch_no, h * 16 + 8 : h * 16 + 16, :], low, axis=1,
                        mode="promise_in_bounds",
                    )
                    acc0 = jnp.where(hit, got0, acc0)
                    acc1 = jnp.where(hit, got1, acc1)
                lane = pl.multiple_of(chunk * 256 + half * 128, 128)
                out_ref[batch_no, 0:8, pl.ds(lane, 128)] = acc0
                out_ref[batch_no, 8:9, pl.ds(lane, 128)] = acc1[0:1]
            return carry

        lax.fori_loop(0, 16, pick, 0)


def blend_kernel(
    order_ref, ids_ref, len_ref, feat_ref, slots_ref, target_ref, out_ref,
    sl_ref, tg_ref, fe_ref, cm_ref, ix_ref, al_ref, w_ref, wh_ref, wl_ref,
):
    lane = lax.broadcasted_iota(jnp.int32, (8, 128), 1)
    sub = lax.broadcasted_iota(jnp.int32, (8, 128), 0)
    diag = sub == (lane & 7)
    lane_k = lane >> 3
    row_a = lax.broadcasted_iota(jnp.int32, (16, 128), 0)
    pix = lax.broadcasted_iota(jnp.int32, (8, 256), 1)
    term = lax.broadcasted_iota(jnp.int32, (8, 256), 0)
    px = (pix & 15).astype(F32) - 7.5
    py = (pix >> 4).astype(F32) - 7.5
    basis = jnp.where(
        term == 0, px * px,
        jnp.where(
            term == 1, px * py,
            jnp.where(
                term == 2, py * py,
                jnp.where(term == 3, px, jnp.where(term == 4, py, jnp.where(term == 5, 1.0, 0.0))),
            ),
        ),
    )
    basis_b = jnp.concatenate([basis] * 4, axis=0).astype(BF16)
    basis_2 = jnp.concatenate([jnp.concatenate([basis, basis], axis=1)] * 2, axis=0).astype(BF16)
    zero8 = jnp.zeros((8, 128), F32)

    for batch_no in range(BATCHES):
        out_ref[batch_no] = jnp.zeros((160, 256), F32)

        def group(group_no, err, batch_no=batch_no):
            longest = jnp.int32(0)
            cx = zero8
            cy = zero8
            length = jnp.zeros((8, 128), jnp.int32)
            for t in range(8):
                tile = order_ref[batch_no, group_no * 8 + t]
                in_view = lax.rem(ids_ref[batch_no, tile], TILES_VIEW)
                row_t = lax.div(in_view, TILES_X)
                col_t = in_view - row_t * TILES_X
                tile_len = len_ref[batch_no, tile]
                longest = jnp.maximum(longest, tile_len)
                here = (lane & 7) == t
                cx = jnp.where(here, (col_t * TILE + 8).astype(F32), cx)
                cy = jnp.where(here, (row_t * TILE + 8).astype(F32), cy)
                length = jnp.where(here, tile_len, length)
                sl_ref[t : t + 1, :] = slots_ref[batch_no, pl.ds(tile, 1), :]
                for channel in range(3):
                    tg_ref[channel * 8 + t : channel * 8 + t + 1, :] = target_ref[
                        batch_no, pl.ds(tile, 1), channel, :
                    ]
            chunks = (longest + 15) // 16

            def forward(j, carry):
                through, colour = carry
                half = pl.multiple_of((j // 8) * 128, 128)
                picked = jnp.take_along_axis(
                    sl_ref[:, pl.ds(half, 128)], lane_k + (j % 8) * 16, axis=1,
                    mode="promise_in_bounds",
                )
                picked = jnp.sum(jnp.where(diag, picked.astype(F32), 0.0), axis=0, keepdims=True)
                index = jnp.broadcast_to(picked.astype(jnp.int32), (8, 128))
                low = index & 127
                high = index >> 7
                acc0 = zero8
                acc1 = zero8
                for h in range(32):
                    hit = high == h
                    got0 = jnp.take_along_axis(
                        feat_ref[batch_no, 0:8, h * 128 : h * 128 + 128], low, axis=1,
                        mode="promise_in_bounds",
                    )
                    got1 = jnp.take_along_axis(
                        feat_ref[batch_no, 8:16, h * 128 : h * 128 + 128], low, axis=1,
                        mode="promise_in_bounds",
                    )
                    acc0 = jnp.where(hit, got0, acc0)
                    acc1 = jnp.where(hit, got1, acc1)
                ix_ref[pl.ds(j, 1), :] = index[0:1]
                u = acc0[0:1] - cx[0:1]
                v = acc0[1:2] - cy[0:1]
                con_a = acc0[2:3]
                con_b = acc0[3:4]
                con_c = acc0[4:5]
                live = (lane_k[0:1] + j * 16) < length[0:1]
                coefs = [
                    con_a * (-0.5 * LOG2_E),
                    con_b * -LOG2_E,
                    con_c * (-0.5 * LOG2_E),
                    (con_a * u + con_b * v) * LOG2_E,
                    (con_b * u + con_c * v) * LOG2_E,
                    jnp.where(
                        live,
                        (acc0[5:6] - 0.5 * (con_a * u * u + con_c * v * v) - con_b * u * v) * LOG2_E,
                        -1e30,
                    ),
                ]
                fe_ref[j] = jnp.concatenate(
                    [u, v, con_a, con_b, con_c, acc0[5:6], jnp.zeros((2, 128), F32)], axis=0
                )
                coef = jnp.concatenate(coefs + [jnp.zeros((2, 128), F32)], axis=0)
                hi, rest = split2(coef)
                mid, lo = split2(rest)
                lhs = jnp.concatenate([hi, mid, lo, zero8], axis=0).astype(BF16)
                alphas = jnp.exp2(dot(lhs, basis_b, TN))
                row0 = pl.multiple_of(j * 128, 128)
                al_ref[pl.ds(row0, 128), :] = alphas
                weights = []
                for k in range(16):
                    weight = through * alphas[k * 8 : k * 8 + 8]
                    through = through - weight
                    weights.append(weight)
                weight = jnp.concatenate(weights, axis=0)
                w_ref[pl.ds(row0, 128), :] = weight
                w_hi, w_lo = split2(weight)
                w_hi = w_hi.astype(BF16)
                w_lo = w_lo.astype(BF16)
                wh_ref[pl.ds(row0, 128), :] = w_hi
                wl_ref[pl.ds(row0, 128), :] = w_lo
                cmat = jnp.concatenate(
                    [
                        jnp.where(diag, acc0[6:7], 0.0),
                        jnp.where(diag, acc0[7:8], 0.0),
                        jnp.where(diag, acc1[0:1], 0.0),
                    ],
                    axis=0,
                )
                c_hi, c_lo = split2(cmat)
                c_two = jnp.concatenate([c_hi, c_lo], axis=0).astype(BF16)
                cm_ref[j] = c_two
                prod = dot(c_two, w_hi, NN)
                prod_lo = dot(c_two, w_lo, NN)
                colour = colour + prod[0:24] + prod[24:48] + prod_lo[0:24] + prod_lo[24:48]
                return through, colour

            _, colour = lax.fori_loop(
                0, chunks, forward, (jnp.ones((8, 256), F32), jnp.zeros((24, 256), F32))
            )
            resid = colour - tg_ref[...]
            err = err + jnp.sum(resid * resid, axis=0, keepdims=True)
            r_hi, r_lo = split2(2.0 * resid)
            r_two = jnp.concatenate([r_hi, r_lo], axis=0).astype(BF16)
            r_four = jnp.concatenate([r_hi, r_hi, r_lo, r_lo], axis=0).astype(BF16)

            def backward(i, behind):
                j = chunks - 1 - i
                row0 = pl.multiple_of(j * 128, 128)
                c_two = cm_ref[j]
                pull = dot(jnp.concatenate([c_two, c_two], axis=0), r_four, TN)
                alphas = al_ref[pl.ds(row0, 128), :]
                weight = w_ref[pl.ds(row0, 128), :]
                parts = []
                for k in range(15, -1, -1):
                    diff = pull[k * 8 : k * 8 + 8] - behind
                    parts.append(weight[k * 8 : k * 8 + 8] * diff)
                    behind = behind + alphas[k * 8 : k * 8 + 8] * diff
                d_exp = jnp.concatenate(parts[::-1], axis=0)
                d_hi, d_lo = split2(d_exp)
                d_two = jnp.concatenate([d_hi.astype(BF16), d_lo.astype(BF16)], axis=1)
                mom = dot(basis_2, d_two, NT)
                shade_hi = dot(r_two, wh_ref[pl.ds(row0, 128), :], NT)
                shade_lo = dot(r_two, wl_ref[pl.ds(row0, 128), :], NT)
                shade = shade_hi[0:24] + shade_hi[24:48] + shade_lo[0:24] + shade_lo[24:48]
                d_col = [
                    jnp.sum(
                        jnp.where(diag, shade[h * 8 : h * 8 + 8], 0.0), axis=0, keepdims=True
                    )
                    for h in range(3)
                ]
                feats = fe_ref[j]
                u = feats[0:1]
                v = feats[1:2]
                con_a = feats[2:3]
                con_b = feats[3:4]
                con_c = feats[4:5]
                m_xx = mom[0:1]
                m_xy = mom[1:2]
                m_yy = mom[2:3]
                m_x = mom[3:4]
                m_y = mom[4:5]
                m_1 = mom[5:6]
                s_x = m_x - u * m_1
                s_y = m_y - v * m_1
                grads = [
                    con_a * s_x + con_b * s_y,
                    con_b * s_x + con_c * s_y,
                    -0.5 * (m_xx - u * (m_x + s_x)),
                    -(m_xy - u * m_y - v * s_x),
                    -0.5 * (m_yy - v * (m_y + s_y)),
                    m_1,
                ] + d_col
                index = ix_ref[pl.ds(j, 1), :]
                hit = row_a == (index >> 8)
                rhs = scatter_rhs(index)
                rows = []
                for value in grads:
                    g_hi, g_lo = split2(value)
                    rows.append(
                        jnp.concatenate(
                            [jnp.where(hit, g_hi, 0.0), jnp.where(hit, g_lo, 0.0)], axis=1
                        )
                    )
                lhs = jnp.concatenate(rows, axis=0).astype(BF16)
                out_ref[batch_no, 0:144, :] += dot(
                    lhs, jnp.concatenate([rhs, rhs], axis=1), NT
                )
                return behind

            lax.fori_loop(0, chunks, backward, jnp.zeros((8, 256), F32))
            return err

        err = lax.fori_loop(0, GROUPS, group, jnp.zeros((1, 256), F32))
        out_ref[batch_no, 144:160, :] = jnp.broadcast_to(
            jnp.sum(err, axis=1, keepdims=True), (16, 256)
        )


def grads_kernel(cam_ref, params_ref, view_ref, send_ref, grad_ref, out_ref, err_ref, vg_ref, gg_ref):
    row_a = lax.broadcasted_iota(jnp.int32, (16, 256), 0)

    for batch_no in range(BATCHES):
        gg_ref[batch_no] = jnp.zeros((160, 256), F32)

        def place(chunk, carry, batch_no=batch_no):
            index = send_ref[batch_no, pl.ds(chunk, 1), :]
            view = view_ref[batch_no, pl.ds(chunk, 1), :]
            hit = row_a == (index >> 8)
            rhs = scatter_rhs(index)
            high = []
            low = []
            for f in range(9):
                g_hi, g_lo = split2(grad_ref[batch_no, f, pl.ds(chunk, 1), :])
                high.append(jnp.where(hit, g_hi, 0.0))
                low.append(jnp.where(hit, g_lo, 0.0))
            high.append(jnp.where(hit, view, 0.0))
            low.append(jnp.zeros((16, 256), F32))
            gg_ref[batch_no] += dot(jnp.concatenate(high, axis=0).astype(BF16), rhs, NT) + dot(
                jnp.concatenate(low, axis=0).astype(BF16), rhs, NT
            )
            return carry

        lax.fori_loop(0, 16, place, 0)

    def block(block_no, carry):
        row0 = pl.multiple_of((block_no // 2) * 8, 8)
        lane0 = pl.multiple_of((block_no % 2) * 128, 128)
        cols = [params_ref[p, pl.ds(row0, 8), pl.ds(lane0, 128)] for p in range(PARAMS)]
        geo = [0.0] * 10
        opac = 0.0
        shade = [0.0] * 48
        for batch_no in range(BATCHES):

            def feat(f, batch_no=batch_no):
                return gg_ref[batch_no, pl.ds(f * 16 + row0, 8), pl.ds(lane0, 128)]

            cam = pick_camera(cam_ref, batch_no, feat(9))
            _, pull_geo = jax.vjp(lambda c: project_geometry(c, cam), cols[0:10])
            (d_geo,) = pull_geo(tuple(feat(f) for f in range(5)))
            basis, pull_ray = jax.vjp(lambda c: ray_basis(c, cam), cols[0:3])
            d_col = [feat(6 + h) for h in range(3)]
            (d_ray,) = pull_ray(
                [
                    d_col[0] * cols[11 + k] + d_col[1] * cols[27 + k] + d_col[2] * cols[43 + k]
                    for k in range(16)
                ]
            )
            for i in range(10):
                geo[i] = geo[i] + d_geo[i]
            for i in range(3):
                geo[i] = geo[i] + d_ray[i]
            opac = opac + feat(5)
            for h in range(3):
                for k in range(16):
                    shade[16 * h + k] = shade[16 * h + k] + d_col[h] * basis[k]
        opac = opac / (1.0 + jnp.exp(cols[10]))
        for p, value in enumerate(geo + [opac] + shade):
            out_ref[p, pl.ds(row0, 8), pl.ds(lane0, 128)] = value
        return carry

    lax.fori_loop(0, 4, block, 0)
    total = grad_ref[0, 9] + grad_ref[1, 9]
    total = jnp.sum(jnp.sum(total, axis=0, keepdims=True), axis=1, keepdims=True)
    err_ref[...] = total * (1.0 / (CAP * BATCHES * OWNERS * TILES_DEV * 3 * TILE_PX))


def exchange(values):
    return lax.all_to_all(values, "dev", split_axis=1, concat_axis=1, tiled=True)


SMEM = pl.BlockSpec(memory_space=pltpu.SMEM)
VMEM = pl.BlockSpec(memory_space=pltpu.VMEM)
CALL = pltpu.CompilerParams(vmem_limit_bytes=VMEM_BYTES)


def local(params, cameras, send_lists, tile_slots, tile_ids, tile_len, targets):
    cams = camera_table(cameras)
    lengths = tile_len[:, 0]
    tile_no = jnp.arange(TILES_DEV, dtype=jnp.int32)
    ahead = (lengths[:, None, :] > lengths[:, :, None]) | (
        (lengths[:, None, :] == lengths[:, :, None]) & (tile_no[None, None, :] < tile_no[None, :, None])
    )
    rank = jnp.sum(ahead.astype(jnp.int32), axis=2)
    order = jnp.sum(
        jnp.where(rank[:, None, :] == tile_no[None, :, None], tile_no[None, None, :], 0), axis=2
    )
    send = send_lists[:, 0].reshape(BATCHES, 16, 256)
    blocks = params.reshape(PARAMS, 16, 256)

    views = pl.pallas_call(
        view_kernel,
        out_shape=jax.ShapeDtypeStruct((OWNERS, BATCHES * CAP), F32),
        in_specs=[SMEM, VMEM],
        out_specs=VMEM,
        compiler_params=CALL,
        name="slot_views",
    )(tile_ids, tile_slots)
    views = lax.all_to_all(views, "dev", split_axis=0, concat_axis=0, tiled=True)
    views = jnp.transpose(views.reshape(OWNERS, BATCHES, CAP), (1, 0, 2)).reshape(BATCHES, 16, 256)

    feats = pl.pallas_call(
        project_kernel,
        out_shape=jax.ShapeDtypeStruct((BATCHES, 9, SLOTS), F32),
        in_specs=[SMEM, VMEM, VMEM, VMEM],
        out_specs=VMEM,
        scratch_shapes=[
            pltpu.VMEM((BATCHES, 16, 256), F32),
            pltpu.VMEM((BATCHES, 512, 128), F32),
        ],
        compiler_params=CALL,
        name="project",
    )(cams, blocks, views, send)
    feats = exchange(feats.reshape(BATCHES * 9, OWNERS, CAP)).reshape(BATCHES, 9, SLOTS)
    feats = jnp.pad(feats, ((0, 0), (0, 7), (0, 0)))

    rows = TILES_DEV // GROUPS * PAIRS
    slot_grads = pl.pallas_call(
        blend_kernel,
        out_shape=jax.ShapeDtypeStruct((BATCHES, 160, 256), F32),
        in_specs=[SMEM, SMEM, SMEM, VMEM, VMEM, VMEM],
        out_specs=VMEM,
        scratch_shapes=[
            pltpu.VMEM((8, 256), jnp.int32),
            pltpu.VMEM((24, 256), F32),
            pltpu.VMEM((16, 8, 128), F32),
            pltpu.VMEM((16, 48, 128), BF16),
            pltpu.VMEM((16, 128), jnp.int32),
            pltpu.VMEM((rows, 256), F32),
            pltpu.VMEM((rows, 256), F32),
            pltpu.VMEM((rows, 256), BF16),
            pltpu.VMEM((rows, 256), BF16),
        ],
        compiler_params=CALL,
        name="blend",
    )(order, tile_ids, lengths, feats, tile_slots, targets)
    slot_grads = exchange(slot_grads.reshape(BATCHES * 10, OWNERS, CAP)).reshape(
        BATCHES, 10, 16, 256
    )

    grads, err = pl.pallas_call(
        grads_kernel,
        out_shape=(
            jax.ShapeDtypeStruct((PARAMS, 16, 256), F32),
            jax.ShapeDtypeStruct((1, 1), F32),
        ),
        in_specs=[SMEM, VMEM, VMEM, VMEM, VMEM],
        out_specs=(VMEM, VMEM),
        scratch_shapes=[
            pltpu.VMEM((BATCHES, 16, 256), F32),
            pltpu.VMEM((BATCHES, 160, 256), F32),
        ],
        compiler_params=CALL,
        name="param_grads",
    )(cams, blocks, views, send, slot_grads)
    return (grads.reshape(PARAMS, 4096), err[0, 0])


def solution(mesh):
    placed = (
        P(None, "dev"),
        P(),
        P(None, "dev", None, None),
        P(None, "dev", None),
        P(None, "dev"),
        P(None, "dev", None),
        P(None, "dev", None, None),
    )
    return jax.shard_map(
        local, mesh=mesh, in_specs=placed, out_specs=(P(None, "dev"), P()), check_vma=False
    )
```

```python
import jax
import jax.numpy as jnp
from jax import lax
from jax.experimental import pallas as pl
from jax.experimental.pallas import tpu as pltpu
from jax.sharding import PartitionSpec as P

BATCHES = 2
TILE = 16
PAIRS = 256
TILE_PX = 256
TILES_X = 240
TILES_VIEW = 32400
VIEWS = 4
PARAMS = 59
TILES_DEV = 32
OWNERS = 128
CAP = 32
SLOTS = 4096
GROUPS = 4
UNROLL = 2
LOG2_E = 1.4426950408889634
VMEM_BYTES = 56 * 1024 * 1024

SH_ZERO = 0.28209479177387814
SH_ONE = 0.4886025119029199
SH_TWO = (
    1.0925484305920792,
    -1.0925484305920792,
    0.31539156525252005,
    -1.0925484305920792,
    0.5462742152960396,
)
SH_THREE = (
    -0.5900435899266435,
    2.890611442640554,
    -0.4570457994644658,
    0.3731763325901154,
    -0.4570457994644658,
    1.445305721320277,
    -0.5900435899266435,
)

F32 = jnp.float32
BF16 = jnp.bfloat16
NN = (((1,), (0,)), ((), ()))
NT = (((1,), (1,)), ((), ()))
TN = (((0,), (0,)), ((), ()))


def dot(lhs, rhs, dims):
    return lax.dot_general(lhs, rhs, dims, preferred_element_type=F32)


def split2(value):
    high = value.astype(BF16).astype(F32)
    return high, value - high


def camera_table(cameras):
    cos_yaw = jnp.cos(cameras[:, :, 0])
    sin_yaw = jnp.sin(cameras[:, :, 0])
    cos_pitch = jnp.cos(cameras[:, :, 1])
    sin_pitch = jnp.sin(cameras[:, :, 1])
    frame = [
        cos_yaw,
        sin_yaw,
        sin_pitch * sin_yaw,
        cos_pitch,
        -sin_pitch * cos_yaw,
        -cos_pitch * sin_yaw,
        sin_pitch,
        cos_pitch * cos_yaw,
    ]
    shift = [cameras[:, :, 2], cameras[:, :, 3], cameras[:, :, 4]]
    centre = [
        -(frame[0] * shift[0] + frame[2] * shift[1] + frame[5] * shift[2]),
        -(frame[3] * shift[1] + frame[6] * shift[2]),
        -(frame[1] * shift[0] + frame[4] * shift[1] + frame[7] * shift[2]),
    ]
    rest = [cameras[:, :, 5], cameras[:, :, 6], cameras[:, :, 7]]
    return jnp.stack(frame + shift + centre + rest)


CAM_ROWS = 17


def sh_basis(dir_x, dir_y, dir_z):
    square_x = dir_x * dir_x
    square_y = dir_y * dir_y
    square_z = dir_z * dir_z
    return [
        SH_ZERO * jnp.ones_like(dir_x),
        -SH_ONE * dir_y,
        SH_ONE * dir_z,
        -SH_ONE * dir_x,
        SH_TWO[0] * dir_x * dir_y,
        SH_TWO[1] * dir_y * dir_z,
        SH_TWO[2] * (2.0 * square_z - square_x - square_y),
        SH_TWO[3] * dir_x * dir_z,
        SH_TWO[4] * (square_x - square_y),
        SH_THREE[0] * dir_y * (3.0 * square_x - square_y),
        SH_THREE[1] * dir_x * dir_y * dir_z,
        SH_THREE[2] * dir_y * (4.0 * square_z - square_x - square_y),
        SH_THREE[3] * dir_z * (2.0 * square_z - 3.0 * square_x - 3.0 * square_y),
        SH_THREE[4] * dir_x * (4.0 * square_z - square_x - square_y),
        SH_THREE[5] * dir_z * (square_x - square_y),
        SH_THREE[6] * dir_x * (square_x - 3.0 * square_y),
    ]


def shape_terms(cols):
    inv_quat = 1.0 / jnp.sqrt(
        cols[6] * cols[6] + cols[7] * cols[7] + cols[8] * cols[8] + cols[9] * cols[9]
    )
    return [jnp.exp(cols[3 + i]) for i in range(3)] + [cols[6 + i] * inv_quat for i in range(4)]


def screen_terms(position, shape, cam):
    spread = shape[0:3]
    quat_w, quat_x, quat_y, quat_z = shape[3:7]
    frame = ((cam[0], None, cam[1]), (cam[2], cam[3], cam[4]), (cam[5], cam[6], cam[7]))
    shift = cam[8:11]
    focal = cam[14]
    viewed = [
        frame[0][0] * position[0] + frame[0][2] * position[2] + shift[0],
        frame[1][0] * position[0]
        + frame[1][1] * position[1]
        + frame[1][2] * position[2]
        + shift[1],
        frame[2][0] * position[0]
        + frame[2][1] * position[1]
        + frame[2][2] * position[2]
        + shift[2],
    ]
    inv_depth = 1.0 / viewed[2]
    screen_u = focal * viewed[0] * inv_depth + cam[15]
    screen_v = focal * viewed[1] * inv_depth + cam[16]
    rotation = (
        (
            1.0 - 2.0 * (quat_y * quat_y + quat_z * quat_z),
            2.0 * (quat_x * quat_y - quat_w * quat_z),
            2.0 * (quat_x * quat_z + quat_w * quat_y),
        ),
        (
            2.0 * (quat_x * quat_y + quat_w * quat_z),
            1.0 - 2.0 * (quat_x * quat_x + quat_z * quat_z),
            2.0 * (quat_y * quat_z - quat_w * quat_x),
        ),
        (
            2.0 * (quat_x * quat_z - quat_w * quat_y),
            2.0 * (quat_y * quat_z + quat_w * quat_x),
            1.0 - 2.0 * (quat_x * quat_x + quat_y * quat_y),
        ),
    )
    jac_main = focal * inv_depth
    jac_u = -jac_main * viewed[0] * inv_depth
    jac_v = -jac_main * viewed[1] * inv_depth
    row_u = [
        jac_main * frame[0][0] + jac_u * frame[2][0],
        jac_u * frame[2][1],
        jac_main * frame[0][2] + jac_u * frame[2][2],
    ]
    row_v = [jac_main * frame[1][i] + jac_v * frame[2][i] for i in range(3)]
    along_u = [
        (row_u[0] * rotation[0][j] + row_u[1] * rotation[1][j] + row_u[2] * rotation[2][j])
        * spread[j]
        for j in range(3)
    ]
    along_v = [
        (row_v[0] * rotation[0][j] + row_v[1] * rotation[1][j] + row_v[2] * rotation[2][j])
        * spread[j]
        for j in range(3)
    ]
    cov_uu = along_u[0] * along_u[0] + along_u[1] * along_u[1] + along_u[2] * along_u[2] + 0.3
    cov_uv = along_u[0] * along_v[0] + along_u[1] * along_v[1] + along_u[2] * along_v[2]
    cov_vv = along_v[0] * along_v[0] + along_v[1] * along_v[1] + along_v[2] * along_v[2] + 0.3
    inv_det = 1.0 / (cov_uu * cov_vv - cov_uv * cov_uv)
    return screen_u, screen_v, cov_vv * inv_det, -cov_uv * inv_det, cov_uu * inv_det


def ray_basis(position, cam):
    ray = [position[i] - cam[11 + i] for i in range(3)]
    inv_len = 1.0 / jnp.sqrt(ray[0] * ray[0] + ray[1] * ray[1] + ray[2] * ray[2])
    return sh_basis(ray[0] * inv_len, ray[1] * inv_len, ray[2] * inv_len)


def pick_camera(cam_ref, batch_no, view):
    picked = []
    for row in range(CAM_ROWS):
        value = jnp.full(view.shape, cam_ref[row, batch_no, VIEWS - 1], F32)
        for view_no in range(VIEWS - 2, -1, -1):
            value = jnp.where(view == view_no, cam_ref[row, batch_no, view_no], value)
        picked.append(value)
    return picked


def take_lanes(table, index):
    return jnp.take_along_axis(table, index, axis=1, mode="promise_in_bounds")


def by_quarter(quarter, values):
    out = values[0]
    for q in range(1, len(values)):
        out = jnp.where(quarter == q, values[q], out)
    return out


def turn(value, quarters):
    quarters = quarters % 4
    return value if quarters == 0 else pltpu.roll(value, 32 * quarters, 1)


def scatter_rhs(index):
    row = lax.broadcasted_iota(jnp.int32, (256, index.shape[1]), 0)
    return jnp.where(row == (index & 255), 1.0, 0.0).astype(BF16)


def offer_kernel(cam_ref, params_ref, send_ref, out_ref, tab_ref):
    quarter = lax.broadcasted_iota(jnp.int32, (8, 128), 1) >> 5

    def block(block_no, carry):
        row0 = pl.multiple_of((block_no // 2) * 8, 8)
        half = block_no % 2
        lane0 = pl.multiple_of(half * 128, 128)
        cols = [params_ref[p, pl.ds(row0, 8), pl.ds(lane0, 128)] for p in range(PARAMS)]
        opac = -(jnp.maximum(-cols[10], 0.0) + jnp.log1p(jnp.exp(-jnp.abs(cols[10]))))
        shared = cols[0:3] + shape_terms(cols) + [opac]
        for batch_no in range(BATCHES):
            feats = list(shared)
            for view_no in range(VIEWS):
                cam = [cam_ref[row, batch_no, view_no] for row in range(CAM_ROWS)]
                basis = ray_basis(cols[0:3], cam)
                for channel in range(3):
                    shade = 0.5
                    for term in range(16):
                        shade = shade + basis[term] * cols[11 + 16 * channel + term]
                    feats.append(shade)
            for f, value in enumerate(feats):
                start = (2 * row0 + half) * 24 + f
                tab_ref[batch_no, pl.ds(start, 8, stride=48), :] = value
            tab_ref[batch_no, pl.ds((2 * row0 + half) * 24 + 23, 8, stride=48), :] = cols[0]
        return carry

    lax.fori_loop(0, 4, block, 0)

    def pick(chunk, carry):
        for batch_no in range(BATCHES):
            both = send_ref[batch_no, pl.ds(chunk, 1), :]
            for half in range(2):
                index = jnp.broadcast_to(both[:, half * 128 : half * 128 + 128], (8, 128))
                low = index & 127
                high = index >> 7
                acc = [jnp.zeros((8, 128), F32)] * 3
                for h in range(32):
                    hit = high == h
                    for q in range(3):
                        row = h * 24 + q * 8
                        got = take_lanes(tab_ref[batch_no, row : row + 8, :], low)
                        acc[q] = jnp.where(hit, got, acc[q])
                for r in range(4):
                    out_ref[(chunk * 2 + half) * 4 + r, batch_no * 8 : batch_no * 8 + 8, :] = (
                        by_quarter(quarter, [turn(acc[q], q - r) for q in range(3)])
                    )
        return carry

    lax.fori_loop(0, 16, pick, 0)


def blend_kernel(
    order_ref, ids_ref, len_ref, cam_ref, feat_ref, slots_ref, target_ref, out_ref,
    tab_ref, sl_ref, tg_ref, fr_ref, ix_ref, ft_ref, co_ref, cc_ref,
    al_ref, w_ref, wh_ref, wl_ref, mo_ref, gr_ref, sg_ref, err_ref,
):
    lane = lax.broadcasted_iota(jnp.int32, (8, 128), 1)
    sub = lax.broadcasted_iota(jnp.int32, (8, 128), 0)
    quarter = lane >> 5
    diag = sub == (lane & 7)
    lane_k = lane >> 3
    row_a = lax.broadcasted_iota(jnp.int32, (16, 128), 0)
    pix = lax.broadcasted_iota(jnp.int32, (8, 256), 1)
    term = lax.broadcasted_iota(jnp.int32, (8, 256), 0)
    px = (pix & 15).astype(F32) - 7.5
    py = (pix >> 4).astype(F32) - 7.5
    basis = jnp.where(
        term == 0, px * px,
        jnp.where(
            term == 1, px * py,
            jnp.where(
                term == 2, py * py,
                jnp.where(term == 3, px, jnp.where(term == 4, py, jnp.where(term == 5, 1.0, 0.0))),
            ),
        ),
    )
    basis_b = jnp.concatenate([basis] * 4, axis=0).astype(BF16)
    basis_2 = jnp.concatenate([jnp.concatenate([basis, basis], axis=1)] * 2, axis=0).astype(BF16)
    zero8 = jnp.zeros((8, 128), F32)
    both = range(BATCHES)

    sg_ref[...] = jnp.zeros(sg_ref.shape, F32)
    co_ref[...] = jnp.zeros(co_ref.shape, F32)
    err_ref[...] = jnp.zeros(err_ref.shape, F32)

    def table(high, carry):
        for b in both:
            tiles = [feat_ref[high * 4 + i, b * 8 : b * 8 + 8, :] for i in range(4)]
            for q in range(3):
                row = pl.multiple_of(high * 8, 8)
                tab_ref[b, q, pl.ds(row, 8), :] = by_quarter(
                    quarter, [turn(tiles[i], i - q) for i in range(4)]
                )
        return carry

    lax.fori_loop(0, 32, table, 0)

    def group(group_no, carry):
        longest = jnp.int32(0)
        centre = []
        lengths = []
        views = []
        for b in both:
            cx = zero8
            cy = zero8
            length = jnp.zeros((8, 128), jnp.int32)
            view = jnp.zeros((8, 128), jnp.int32)
            for t in range(8):
                tile = order_ref[b, group_no * 8 + t]
                tile_id = ids_ref[b, tile]
                view_t = lax.div(tile_id, TILES_VIEW)
                in_view = tile_id - view_t * TILES_VIEW
                row_t = lax.div(in_view, TILES_X)
                col_t = in_view - row_t * TILES_X
                tile_len = len_ref[b, tile]
                longest = jnp.maximum(longest, tile_len)
                here = (lane & 7) == t
                cx = jnp.where(here, (col_t * TILE + 8).astype(F32), cx)
                cy = jnp.where(here, (row_t * TILE + 8).astype(F32), cy)
                length = jnp.where(here, tile_len, length)
                view = jnp.where(here, view_t, view)
                sl_ref[b, t : t + 1, :] = slots_ref[b, pl.ds(tile, 1), :]
                for channel in range(3):
                    tg_ref[b, channel * 8 + t : channel * 8 + t + 1, :] = target_ref[
                        b, pl.ds(tile, 1), channel, :
                    ]
            centre.append((cx, cy))
            lengths.append(length)
            views.append(view)
        chunks = lax.div(longest + (16 * UNROLL - 1), 16 * UNROLL)

        def gather(i, carry):
            for b in both:
                for n in range(UNROLL):
                    j = i * UNROLL + n
                    half = pl.multiple_of(lax.div(j, 8) * 128, 128)
                    picked = take_lanes(
                        sl_ref[b, :, pl.ds(half, 128)], lane_k + lax.rem(j, 8) * 16
                    )
                    picked = jnp.sum(
                        jnp.where(diag, picked.astype(F32), 0.0), axis=0, keepdims=True
                    )
                    index = jnp.broadcast_to(picked.astype(jnp.int32), (8, 128))
                    low = index & 127
                    high = index >> 7
                    acc = [zero8] * 3
                    for h in range(32):
                        hit = high == h
                        for q in range(3):
                            got = take_lanes(tab_ref[b, q, h * 8 : h * 8 + 8, :], low)
                            acc[q] = jnp.where(hit, got, acc[q])
                    ix_ref[b, pl.ds(j, 1), :] = index[0:1]
                    for q in range(3):
                        fr_ref[b, pl.ds(q * 128 + j, 8, stride=16), :] = acc[q]
            return carry

        lax.fori_loop(0, chunks, gather, 0)

        for b in both:
            cx, cy = centre[b]
            packed = [take_lanes(cam_ref[b, r * 8 : r * 8 + 8, :], views[b]) for r in range(3)]
            cam = [packed[r // 8][r % 8 : r % 8 + 1] for r in range(CAM_ROWS)]
            cam = [jnp.broadcast_to(c, (8, 128)) for c in cam]
            for part in range(2):
                c0 = part * 8

                def raw(f, b=b, c0=c0):
                    return fr_ref[b, f * 16 + c0 : f * 16 + c0 + 8, :]

                u, v, con_a, con_b, con_c = screen_terms(
                    [raw(f) for f in range(3)], [raw(f) for f in range(3, 10)], cam
                )
                u = u - cx
                v = v - cy
                for f, value in enumerate((u, v, con_a, con_b, con_c)):
                    ft_ref[b, f * 16 + c0 : f * 16 + c0 + 8, :] = value
                live = (lane_k + (sub + c0) * 16) < lengths[b]
                coefs = [
                    con_a * (-0.5 * LOG2_E),
                    con_b * -LOG2_E,
                    con_c * (-0.5 * LOG2_E),
                    (con_a * u + con_b * v) * LOG2_E,
                    (con_b * u + con_c * v) * LOG2_E,
                    jnp.where(
                        live,
                        (raw(10) - 0.5 * (con_a * u * u + con_c * v * v) - con_b * u * v) * LOG2_E,
                        -1e30,
                    ),
                ]
                for f, value in enumerate(coefs):
                    hi, rest = split2(value)
                    mid, lo = split2(rest)
                    for p, piece in enumerate((hi, mid, lo)):
                        co_ref[b, pl.ds(c0 * 32 + p * 8 + f, 8, stride=32), :] = piece
                for channel in range(3):
                    shade = raw(11 + channel)
                    for view_no in range(1, VIEWS):
                        shade = jnp.where(
                            views[b] == view_no, raw(11 + 3 * view_no + channel), shade
                        )
                    hi, lo = split2(shade)
                    cc_ref[b, pl.ds(c0 * 8 + channel, 8, stride=8), :] = hi
                    cc_ref[b, pl.ds(c0 * 8 + 3 + channel, 8, stride=8), :] = lo

        def colours_of(b, j):
            rows = cc_ref[b, pl.ds(pl.multiple_of(j * 8, 8), 8), :]
            return jnp.concatenate(
                [jnp.where(diag, rows[r : r + 1], 0.0) for r in range(6)], axis=0
            ).astype(BF16)

        def forward(i, carry):
            carry = list(carry)
            for b in both:
                through, colour = carry[b]
                for n in range(UNROLL):
                    j = i * UNROLL + n
                    lhs = co_ref[b, pl.ds(pl.multiple_of(j * 32, 32), 32), :].astype(BF16)
                    alphas = jnp.exp2(dot(lhs, basis_b, TN))
                    row0 = pl.multiple_of(j * 128, 128)
                    al_ref[b, pl.ds(row0, 128), :] = alphas
                    weights = []
                    for k in range(16):
                        weight = through * alphas[k * 8 : k * 8 + 8]
                        through = through - weight
                        weights.append(weight)
                    weight = jnp.concatenate(weights, axis=0)
                    w_ref[b, pl.ds(row0, 128), :] = weight
                    w_hi, w_lo = split2(weight)
                    w_hi = w_hi.astype(BF16)
                    w_lo = w_lo.astype(BF16)
                    wh_ref[b, pl.ds(row0, 128), :] = w_hi
                    wl_ref[b, pl.ds(row0, 128), :] = w_lo
                    c_two = colours_of(b, j)
                    prod = dot(c_two, w_hi, NN)
                    prod_lo = dot(c_two, w_lo, NN)
                    colour = colour + prod[0:24] + prod[24:48] + prod_lo[0:24] + prod_lo[24:48]
                carry[b] = (through, colour)
            return tuple(carry)

        start = (jnp.ones((8, 256), F32), jnp.zeros((24, 256), F32))
        done = lax.fori_loop(0, chunks, forward, (start, start))
        r_two = []
        r_four = []
        for b in both:
            resid = done[b][1] - tg_ref[b]
            err_ref[b] += resid * resid
            r_hi, r_lo = split2(2.0 * resid)
            r_two.append(jnp.concatenate([r_hi, r_lo], axis=0).astype(BF16))
            r_four.append(jnp.concatenate([r_hi, r_hi, r_lo, r_lo], axis=0).astype(BF16))

        def backward(i, carry):
            carry = list(carry)
            for b in both:
                behind = carry[b]
                for n in range(UNROLL):
                    j = (chunks - 1 - i) * UNROLL + (UNROLL - 1 - n)
                    row0 = pl.multiple_of(j * 128, 128)
                    c_two = colours_of(b, j)
                    pull = dot(jnp.concatenate([c_two, c_two], axis=0), r_four[b], TN)
                    alphas = al_ref[b, pl.ds(row0, 128), :]
                    weight = w_ref[b, pl.ds(row0, 128), :]
                    parts = []
                    for k in range(15, -1, -1):
                        diff = pull[k * 8 : k * 8 + 8] - behind
                        parts.append(weight[k * 8 : k * 8 + 8] * diff)
                        behind = behind + alphas[k * 8 : k * 8 + 8] * diff
                    d_exp = jnp.concatenate(parts[::-1], axis=0)
                    d_hi, d_lo = split2(d_exp)
                    d_two = jnp.concatenate([d_hi.astype(BF16), d_lo.astype(BF16)], axis=1)
                    mom = dot(basis_2, d_two, NT)
                    shade_hi = dot(r_two[b], wh_ref[b, pl.ds(row0, 128), :], NT)
                    shade_lo = dot(r_two[b], wl_ref[b, pl.ds(row0, 128), :], NT)
                    shade = shade_hi[0:24] + shade_hi[24:48] + shade_lo[0:24] + shade_lo[24:48]
                    mo_ref[b, pl.ds(j, 8, stride=16), :] = mom[0:8]
                    for h in range(3):
                        mo_ref[b, pl.ds((8 + h) * 16 + j, 1), :] = jnp.sum(
                            jnp.where(diag, shade[h * 8 : h * 8 + 8], 0.0), axis=0, keepdims=True
                        )
                carry[b] = behind
            return tuple(carry)

        zero = jnp.zeros((8, 256), F32)
        lax.fori_loop(0, chunks, backward, (zero, zero))

        for b in both:
            for part in range(2):
                c0 = part * 8

                def moment(f, b=b, c0=c0):
                    return mo_ref[b, f * 16 + c0 : f * 16 + c0 + 8, :]

                u, v, con_a, con_b, con_c = [
                    ft_ref[b, f * 16 + c0 : f * 16 + c0 + 8, :] for f in range(5)
                ]
                m_xx, m_xy, m_yy, m_x, m_y, m_1 = [moment(f) for f in range(6)]
                s_x = m_x - u * m_1
                s_y = m_y - v * m_1
                live = (lane_k + (sub + c0) * 16) < lengths[b]
                code = jnp.where(live, 8.0 + views[b].astype(F32), 0.0)
                grads = [
                    con_a * s_x + con_b * s_y,
                    con_b * s_x + con_c * s_y,
                    -0.5 * (m_xx - u * (m_x + s_x)),
                    -(m_xy - u * m_y - v * s_x),
                    -0.5 * (m_yy - v * (m_y + s_y)),
                    m_1,
                    moment(8),
                    moment(9),
                    moment(10),
                    code,
                ]
                for f, value in enumerate(grads):
                    hi, lo = split2(value)
                    gr_ref[b, f * 16 + c0 : f * 16 + c0 + 8, :] = hi
                    gr_ref[b, 160 + f * 16 + c0 : 160 + f * 16 + c0 + 8, :] = lo

        def scatter(i, carry):
            for b in both:
                for n in range(UNROLL):
                    j = i * UNROLL + n
                    index = ix_ref[b, pl.ds(j, 1), :]
                    hit = row_a == (index >> 8)
                    rhs = scatter_rhs(index)
                    rows = []
                    for f in range(10):
                        g_hi = gr_ref[b, pl.ds(f * 16 + j, 1), :]
                        g_lo = gr_ref[b, pl.ds(160 + f * 16 + j, 1), :]
                        rows.append(
                            jnp.concatenate(
                                [jnp.where(hit, g_hi, 0.0), jnp.where(hit, g_lo, 0.0)], axis=1
                            )
                        )
                    lhs = jnp.concatenate(rows, axis=0).astype(BF16)
                    add = dot(lhs, jnp.concatenate([rhs, rhs], axis=1), NT)
                    for half in range(2):
                        sg_ref[b, half, 0:160, :] += add[:, half * 128 : half * 128 + 128]
            return carry

        lax.fori_loop(0, chunks, scatter, 0)
        return carry

    lax.fori_loop(0, GROUPS, group, 0)
    for b in both:
        total = jnp.sum(jnp.sum(err_ref[b], axis=0, keepdims=True), axis=1, keepdims=True)
        for half in range(2):
            sg_ref[b, half, 240:256, :] = jnp.broadcast_to(total, (16, 128))

    for a in range(16):
        for half in range(2):
            parts = [
                sg_ref[b, half, pl.ds(q * 128 + a, 8, stride=16), :]
                for b in both
                for q in range(2)
            ]
            for r in range(4):
                out_ref[(a * 2 + half) * 4 + r] = by_quarter(
                    quarter, [turn(parts[q], q - r) for q in range(4)]
                )


def grads_kernel(cam_ref, params_ref, send_ref, grad_ref, out_ref, err_ref, gg_ref):
    row_a = lax.broadcasted_iota(jnp.int32, (16, 256), 0)
    quarter = lax.broadcasted_iota(jnp.int32, (8, 128), 1) >> 5
    gg_ref[...] = jnp.zeros(gg_ref.shape, F32)

    def place(chunk, total):
        tiles = [grad_ref[chunk * 8 + i] for i in range(8)]
        for tile in tiles:
            total = total + tile
        for batch_no in range(BATCHES):
            index = send_ref[batch_no, pl.ds(chunk, 1), :]
            hit = row_a == (index >> 8)
            rhs = scatter_rhs(index)
            high = []
            low = []
            for q in range(2):
                values = jnp.concatenate(
                    [
                        by_quarter(
                            quarter,
                            [turn(tiles[4 * n + i], i - 2 * batch_no - q) for i in range(4)],
                        )
                        for n in range(2)
                    ],
                    axis=1,
                )
                g_hi, g_lo = split2(values)
                for f in range(8 if q == 0 else 2):
                    high.append(jnp.where(hit, g_hi[f : f + 1], 0.0))
                    low.append(jnp.where(hit, g_lo[f : f + 1], 0.0))
            gg_ref[batch_no] += dot(jnp.concatenate(high, axis=0).astype(BF16), rhs, NT) + dot(
                jnp.concatenate(low, axis=0).astype(BF16), rhs, NT
            )
        return total

    total = lax.fori_loop(0, 16, place, jnp.zeros((8, 128), F32))

    def block(block_no, carry):
        row0 = pl.multiple_of((block_no // 2) * 8, 8)
        lane0 = pl.multiple_of((block_no % 2) * 128, 128)
        cols = [params_ref[p, pl.ds(row0, 8), pl.ds(lane0, 128)] for p in range(PARAMS)]
        geo = [0.0] * 10
        opac = 0.0
        shade = [0.0] * 48
        for batch_no in range(BATCHES):

            def feat(f, batch_no=batch_no):
                return gg_ref[batch_no, pl.ds(f * 16 + row0, 8), pl.ds(lane0, 128)]

            code = feat(9)
            view = jnp.where(code >= 12.0, (code - 16.0) * 0.5, code - 8.0)
            view = jnp.maximum(view, 0.0)
            cam = pick_camera(cam_ref, batch_no, view)
            _, pull_geo = jax.vjp(
                lambda c: screen_terms(c[0:3], shape_terms(c), cam), cols[0:10]
            )
            (d_geo,) = pull_geo(tuple(feat(f) for f in range(5)))
            basis, pull_ray = jax.vjp(lambda c: ray_basis(c, cam), cols[0:3])
            d_col = [feat(6 + h) for h in range(3)]
            (d_ray,) = pull_ray(
                [
                    d_col[0] * cols[11 + k] + d_col[1] * cols[27 + k] + d_col[2] * cols[43 + k]
                    for k in range(16)
                ]
            )
            for i in range(10):
                geo[i] = geo[i] + d_geo[i]
            for i in range(3):
                geo[i] = geo[i] + d_ray[i]
            opac = opac + feat(5)
            for h in range(3):
                for k in range(16):
                    shade[16 * h + k] = shade[16 * h + k] + d_col[h] * basis[k]
        opac = opac / (1.0 + jnp.exp(cols[10]))
        for p, value in enumerate(geo + [opac] + shade):
            out_ref[p, pl.ds(row0, 8), pl.ds(lane0, 128)] = value
        return carry

    lax.fori_loop(0, 4, block, 0)
    lane = lax.broadcasted_iota(jnp.int32, (1, 128), 1)
    errors = jnp.sum(
        jnp.where((lane == 32) | (lane == 96), total[7:8], 0.0), axis=1, keepdims=True
    )
    err_ref[...] = errors * (1.0 / (BATCHES * OWNERS * TILES_DEV * 3 * TILE_PX))


def exchange(values):
    return lax.all_to_all(values, "dev", split_axis=0, concat_axis=0, tiled=True)


SMEM = pl.BlockSpec(memory_space=pltpu.SMEM)
VMEM = pl.BlockSpec(memory_space=pltpu.VMEM)
CALL = pltpu.CompilerParams(vmem_limit_bytes=VMEM_BYTES)


def local(params, cameras, send_lists, tile_slots, tile_ids, tile_len, targets):
    cams = camera_table(cameras)
    lengths = tile_len[:, 0]
    tile_no = jnp.arange(TILES_DEV, dtype=jnp.int32)
    ahead = (lengths[:, None, :] > lengths[:, :, None]) | (
        (lengths[:, None, :] == lengths[:, :, None]) & (tile_no[None, None, :] < tile_no[None, :, None])
    )
    rank = jnp.sum(ahead.astype(jnp.int32), axis=2)
    order = jnp.sum(
        jnp.where(rank[:, None, :] == tile_no[None, :, None], tile_no[None, None, :], 0), axis=2
    )
    send = send_lists[:, 0].reshape(BATCHES, 16, 256)
    blocks = params.reshape(PARAMS, 16, 256)
    cam_lanes = jnp.pad(
        jnp.transpose(cams, (1, 0, 2)), ((0, 0), (0, 24 - CAM_ROWS), (0, 128 - VIEWS))
    )

    feats = pl.pallas_call(
        offer_kernel,
        out_shape=jax.ShapeDtypeStruct((OWNERS, 16, 128), F32),
        in_specs=[SMEM, VMEM, VMEM],
        out_specs=VMEM,
        scratch_shapes=[pltpu.VMEM((BATCHES, 768, 128), F32)],
        compiler_params=CALL,
        name="offer",
    )(cams, blocks, send)
    feats = exchange(feats)

    rows = TILES_DEV // GROUPS * PAIRS
    slot_grads = pl.pallas_call(
        blend_kernel,
        out_shape=jax.ShapeDtypeStruct((OWNERS, 8, 128), F32),
        in_specs=[SMEM, SMEM, SMEM, VMEM, VMEM, VMEM, VMEM],
        out_specs=VMEM,
        scratch_shapes=[
            pltpu.VMEM((BATCHES, 3, 256, 128), F32),
            pltpu.VMEM((BATCHES, 8, 256), jnp.int32),
            pltpu.VMEM((BATCHES, 24, 256), F32),
            pltpu.VMEM((BATCHES, 384, 128), F32),
            pltpu.VMEM((BATCHES, 16, 128), jnp.int32),
            pltpu.VMEM((BATCHES, 80, 128), F32),
            pltpu.VMEM((BATCHES, 512, 128), F32),
            pltpu.VMEM((BATCHES, 128, 128), F32),
            pltpu.VMEM((BATCHES, rows, 256), F32),
            pltpu.VMEM((BATCHES, rows, 256), F32),
            pltpu.VMEM((BATCHES, rows, 256), BF16),
            pltpu.VMEM((BATCHES, rows, 256), BF16),
            pltpu.VMEM((BATCHES, 176, 128), F32),
            pltpu.VMEM((BATCHES, 320, 128), F32),
            pltpu.VMEM((BATCHES, 2, 256, 128), F32),
            pltpu.VMEM((BATCHES, 24, 256), F32),
        ],
        compiler_params=CALL,
        name="blend",
    )(order, tile_ids, lengths, cam_lanes, feats, tile_slots, targets)
    slot_grads = exchange(slot_grads)

    grads, err = pl.pallas_call(
        grads_kernel,
        out_shape=(
            jax.ShapeDtypeStruct((PARAMS, 16, 256), F32),
            jax.ShapeDtypeStruct((1, 1), F32),
        ),
        in_specs=[SMEM, VMEM, VMEM, VMEM],
        out_specs=(VMEM, VMEM),
        scratch_shapes=[pltpu.VMEM((BATCHES, 160, 256), F32)],
        compiler_params=CALL,
        name="param_grads",
    )(cams, blocks, send, slot_grads)
    return (grads.reshape(PARAMS, 4096), err[0, 0])


def solution(mesh):
    placed = (
        P(None, "dev"),
        P(),
        P(None, "dev", None, None),
        P(None, "dev", None),
        P(None, "dev"),
        P(None, "dev", None),
        P(None, "dev", None, None),
    )
    return jax.shard_map(
        local, mesh=mesh, in_specs=placed, out_specs=(P(None, "dev"), P()), check_vma=False
    )
```

```python
import jax
import jax.numpy as jnp
from jax import lax
from jax.experimental import pallas as pl
from jax.experimental.pallas import tpu as pltpu
from jax.sharding import PartitionSpec as P

BATCHES = 2
TILE = 16
PAIRS = 256
TILE_PX = 256
TILES_X = 240
TILES_VIEW = 32400
VIEWS = 4
PARAMS = 59
TILES_DEV = 32
OWNERS = 128
CAP = 32
SLOTS = 4096
GROUPS = 4
UNROLL = 2
PITCH = 72
LOG2_E = 1.4426950408889634
VMEM_BYTES = 56 * 1024 * 1024

SH_ZERO = 0.28209479177387814
SH_ONE = 0.4886025119029199
SH_TWO = (
    1.0925484305920792,
    -1.0925484305920792,
    0.31539156525252005,
    -1.0925484305920792,
    0.5462742152960396,
)
SH_THREE = (
    -0.5900435899266435,
    2.890611442640554,
    -0.4570457994644658,
    0.3731763325901154,
    -0.4570457994644658,
    1.445305721320277,
    -0.5900435899266435,
)

F32 = jnp.float32
BF16 = jnp.bfloat16
NN = (((1,), (0,)), ((), ()))
NT = (((1,), (1,)), ((), ()))
TN = (((0,), (0,)), ((), ()))


def dot(lhs, rhs, dims):
    return lax.dot_general(lhs, rhs, dims, preferred_element_type=F32)


def split2(value):
    high = value.astype(BF16).astype(F32)
    return high, value - high


def camera_table(cameras):
    cos_yaw = jnp.cos(cameras[:, :, 0])
    sin_yaw = jnp.sin(cameras[:, :, 0])
    cos_pitch = jnp.cos(cameras[:, :, 1])
    sin_pitch = jnp.sin(cameras[:, :, 1])
    frame = [
        cos_yaw,
        sin_yaw,
        sin_pitch * sin_yaw,
        cos_pitch,
        -sin_pitch * cos_yaw,
        -cos_pitch * sin_yaw,
        sin_pitch,
        cos_pitch * cos_yaw,
    ]
    shift = [cameras[:, :, 2], cameras[:, :, 3], cameras[:, :, 4]]
    centre = [
        -(frame[0] * shift[0] + frame[2] * shift[1] + frame[5] * shift[2]),
        -(frame[3] * shift[1] + frame[6] * shift[2]),
        -(frame[1] * shift[0] + frame[4] * shift[1] + frame[7] * shift[2]),
    ]
    rest = [cameras[:, :, 5], cameras[:, :, 6], cameras[:, :, 7]]
    return jnp.stack(frame + shift + centre + rest)


CAM_ROWS = 17


def sh_basis(dir_x, dir_y, dir_z):
    square_x = dir_x * dir_x
    square_y = dir_y * dir_y
    square_z = dir_z * dir_z
    return [
        SH_ZERO * jnp.ones_like(dir_x),
        -SH_ONE * dir_y,
        SH_ONE * dir_z,
        -SH_ONE * dir_x,
        SH_TWO[0] * dir_x * dir_y,
        SH_TWO[1] * dir_y * dir_z,
        SH_TWO[2] * (2.0 * square_z - square_x - square_y),
        SH_TWO[3] * dir_x * dir_z,
        SH_TWO[4] * (square_x - square_y),
        SH_THREE[0] * dir_y * (3.0 * square_x - square_y),
        SH_THREE[1] * dir_x * dir_y * dir_z,
        SH_THREE[2] * dir_y * (4.0 * square_z - square_x - square_y),
        SH_THREE[3] * dir_z * (2.0 * square_z - 3.0 * square_x - 3.0 * square_y),
        SH_THREE[4] * dir_x * (4.0 * square_z - square_x - square_y),
        SH_THREE[5] * dir_z * (square_x - square_y),
        SH_THREE[6] * dir_x * (square_x - 3.0 * square_y),
    ]


def shape_terms(cols):
    inv_quat = 1.0 / jnp.sqrt(
        cols[6] * cols[6] + cols[7] * cols[7] + cols[8] * cols[8] + cols[9] * cols[9]
    )
    return [jnp.exp(cols[3 + i]) for i in range(3)] + [cols[6 + i] * inv_quat for i in range(4)]


def screen_terms(position, shape, cam):
    spread = shape[0:3]
    quat_w, quat_x, quat_y, quat_z = shape[3:7]
    frame = ((cam[0], None, cam[1]), (cam[2], cam[3], cam[4]), (cam[5], cam[6], cam[7]))
    shift = cam[8:11]
    focal = cam[14]
    viewed = [
        frame[0][0] * position[0] + frame[0][2] * position[2] + shift[0],
        frame[1][0] * position[0]
        + frame[1][1] * position[1]
        + frame[1][2] * position[2]
        + shift[1],
        frame[2][0] * position[0]
        + frame[2][1] * position[1]
        + frame[2][2] * position[2]
        + shift[2],
    ]
    inv_depth = 1.0 / viewed[2]
    screen_u = focal * viewed[0] * inv_depth + cam[15]
    screen_v = focal * viewed[1] * inv_depth + cam[16]
    rotation = (
        (
            1.0 - 2.0 * (quat_y * quat_y + quat_z * quat_z),
            2.0 * (quat_x * quat_y - quat_w * quat_z),
            2.0 * (quat_x * quat_z + quat_w * quat_y),
        ),
        (
            2.0 * (quat_x * quat_y + quat_w * quat_z),
            1.0 - 2.0 * (quat_x * quat_x + quat_z * quat_z),
            2.0 * (quat_y * quat_z - quat_w * quat_x),
        ),
        (
            2.0 * (quat_x * quat_z - quat_w * quat_y),
            2.0 * (quat_y * quat_z + quat_w * quat_x),
            1.0 - 2.0 * (quat_x * quat_x + quat_y * quat_y),
        ),
    )
    jac_main = focal * inv_depth
    jac_u = -jac_main * viewed[0] * inv_depth
    jac_v = -jac_main * viewed[1] * inv_depth
    row_u = [
        jac_main * frame[0][0] + jac_u * frame[2][0],
        jac_u * frame[2][1],
        jac_main * frame[0][2] + jac_u * frame[2][2],
    ]
    row_v = [jac_main * frame[1][i] + jac_v * frame[2][i] for i in range(3)]
    along_u = [
        (row_u[0] * rotation[0][j] + row_u[1] * rotation[1][j] + row_u[2] * rotation[2][j])
        * spread[j]
        for j in range(3)
    ]
    along_v = [
        (row_v[0] * rotation[0][j] + row_v[1] * rotation[1][j] + row_v[2] * rotation[2][j])
        * spread[j]
        for j in range(3)
    ]
    cov_uu = along_u[0] * along_u[0] + along_u[1] * along_u[1] + along_u[2] * along_u[2] + 0.3
    cov_uv = along_u[0] * along_v[0] + along_u[1] * along_v[1] + along_u[2] * along_v[2]
    cov_vv = along_v[0] * along_v[0] + along_v[1] * along_v[1] + along_v[2] * along_v[2] + 0.3
    inv_det = 1.0 / (cov_uu * cov_vv - cov_uv * cov_uv)
    return screen_u, screen_v, cov_vv * inv_det, -cov_uv * inv_det, cov_uu * inv_det


def ray_basis(position, cam):
    ray = [position[i] - cam[11 + i] for i in range(3)]
    inv_len = 1.0 / jnp.sqrt(ray[0] * ray[0] + ray[1] * ray[1] + ray[2] * ray[2])
    return sh_basis(ray[0] * inv_len, ray[1] * inv_len, ray[2] * inv_len)


def pick_camera(cam_ref, batch_no, view):
    picked = []
    for row in range(CAM_ROWS):
        value = jnp.full(view.shape, cam_ref[row, batch_no, VIEWS - 1], F32)
        for view_no in range(VIEWS - 2, -1, -1):
            value = jnp.where(view == view_no, cam_ref[row, batch_no, view_no], value)
        picked.append(value)
    return picked


def take_lanes(table, index):
    return jnp.take_along_axis(table, index, axis=1, mode="promise_in_bounds")


def by_quarter(quarter, values):
    out = values[0]
    for q in range(1, len(values)):
        out = jnp.where(quarter == q, values[q], out)
    return out


def turn(value, quarters):
    quarters = quarters % 4
    return value if quarters == 0 else pltpu.roll(value, 32 * quarters, 1)


def scatter_rhs(index):
    row = lax.broadcasted_iota(jnp.int32, (256, index.shape[1]), 0)
    return jnp.where(row == (index & 255), 1.0, 0.0).astype(BF16)


def fetch_params(params_ref, flat_ref, sems):
    copies = [
        pltpu.make_async_copy(
            params_ref.at[:, pl.ds(j * 128, 128)],
            flat_ref.at[pl.ds(j * PITCH, PARAMS), :],
            sems.at[j],
        )
        for j in range(32)
    ]
    for copy in copies:
        copy.start()
    return copies


def param_rows(flat_ref, row0, half, param):
    return flat_ref[pl.ds((2 * row0 + half) * PITCH + param, 8, stride=2 * PITCH), :]


def offer_kernel(
    cam_ref, params_ref, send_ref, out_ref, flat_ref, tab_ref, two_ref, third_ref, sems
):
    copies = fetch_params(params_ref, flat_ref, sems)
    quarter = lax.broadcasted_iota(jnp.int32, (8, 128), 1) >> 5
    row_low = lax.broadcasted_iota(jnp.int32, (128, 256), 0)
    is_place = lax.broadcasted_iota(jnp.int32, (8, 128), 0) < 3
    for copy in copies:
        copy.wait()

    def block(block_no, carry):
        row0 = (block_no // 2) * 8
        half = block_no % 2
        cols = [param_rows(flat_ref, row0, half, p) for p in range(PARAMS)]
        opac = -(jnp.maximum(-cols[10], 0.0) + jnp.log1p(jnp.exp(-jnp.abs(cols[10]))))
        shared = cols[0:3] + shape_terms(cols) + [opac]
        for batch_no in range(BATCHES):
            feats = list(shared)
            for view_no in range(VIEWS):
                cam = [cam_ref[row, batch_no, view_no] for row in range(CAM_ROWS)]
                basis = ray_basis(cols[0:3], cam)
                for channel in range(3):
                    shade = 0.5
                    for term in range(16):
                        shade = shade + basis[term] * cols[11 + 16 * channel + term]
                    feats.append(shade)
            feats.append(jnp.zeros((8, 128), F32))
            for f, value in enumerate(feats):
                start = (2 * row0 + half) * 24 + f
                tab_ref[batch_no, pl.ds(start, 8, stride=48), :] = value
        return carry

    lax.fori_loop(0, 4, block, 0)

    def pieces(step, carry):
        for batch_no in range(BATCHES):
            row0 = pl.multiple_of(step * 192, 192)
            value = tab_ref[batch_no, pl.ds(row0, 192), :]
            hi, rest = split2(value)
            mid, lo = split2(rest)
            two_ref[batch_no, pl.ds(row0, 192), 0:128] = hi.astype(BF16)
            two_ref[batch_no, pl.ds(row0, 192), 128:256] = mid.astype(BF16)
            low = jnp.concatenate(
                [jnp.where(is_place, lo[n * 24 : n * 24 + 8], 0.0) for n in range(8)], axis=0
            )
            row1 = pl.multiple_of(step * 64, 64)
            third_ref[batch_no, pl.ds(row1, 64), 0:128] = low.astype(BF16)
            third_ref[batch_no, pl.ds(row1, 64), 128:256] = jnp.zeros((64, 128), BF16)
        return carry

    lax.fori_loop(0, 4, pieces, 0)

    def pick(chunk, carry):
        for batch_no in range(BATCHES):
            index = send_ref[batch_no, pl.ds(chunk, 1), :]
            high = jnp.broadcast_to(index >> 7, (8, 256))
            one = jnp.where(row_low == (index & 127), 1.0, 0.0).astype(BF16)
            one = jnp.concatenate([one, one], axis=0)
            acc = [jnp.zeros((8, 256), F32)] * 4
            for part in range(4):
                got = dot(two_ref[batch_no, part * 192 : part * 192 + 192, :], one, NN)
                low = dot(third_ref[batch_no, part * 64 : part * 64 + 64, :], one, NN)
                for h in range(8):
                    hit = high == part * 8 + h
                    for q in range(3):
                        row = h * 24 + q * 8
                        acc[q] = jnp.where(hit, got[row : row + 8], acc[q])
                    acc[3] = jnp.where(hit, low[h * 8 : h * 8 + 8], acc[3])
            acc[0] = acc[0] + acc[3]
            for half in range(2):
                cut = [acc[q][:, half * 128 : half * 128 + 128] for q in range(3)]
                for r in range(4):
                    out_ref[(chunk * 2 + half) * 4 + r, batch_no * 8 : batch_no * 8 + 8, :] = (
                        by_quarter(quarter, [turn(cut[q], q - r) for q in range(3)])
                    )
        return carry

    lax.fori_loop(0, 16, pick, 0)


def views_kernel(ids_ref, slots_ref, out_ref):
    row_high = lax.broadcasted_iota(jnp.int32, (32, PAIRS), 0)
    row_low = lax.broadcasted_iota(jnp.int32, (128, PAIRS), 0)

    def step(tile_no, sums):
        out = []
        for b in range(BATCHES):
            view = lax.div(ids_ref[b, tile_no], TILES_VIEW).astype(F32) * 0.5
            slots = slots_ref[b, pl.ds(tile_no, 1), :]
            lhs = jnp.where(row_high == (slots >> 7), view, 0.0).astype(BF16)
            rhs = jnp.where(row_low == (slots & 127), 1.0, 0.0).astype(BF16)
            out.append(sums[b] + dot(lhs, rhs, NT))
        return tuple(out)

    zero = jnp.zeros((32, 128), F32)
    sums = lax.fori_loop(0, TILES_DEV, step, (zero, zero))
    for b in range(BATCHES):
        out_ref[b] = sums[b]


def blend_kernel(
    order_ref, ids_ref, len_ref, cam_ref, feat_ref, view_ref, slots_ref, target_ref, out_ref,
    sf_ref, tab_ref, last_ref, sl_ref, tg_ref, fr_ref, ix_ref, co_ref, cc_ref,
    al_ref, w_ref, ww_ref, pl_ref, dd_ref, rt_ref, mo_ref, gr_ref, sg_ref, err_ref,
):
    lane = lax.broadcasted_iota(jnp.int32, (8, 128), 1)
    sub = lax.broadcasted_iota(jnp.int32, (8, 128), 0)
    quarter = lane >> 5
    diag = sub == (lane & 7)
    lane_k = lane >> 3
    row_a = lax.broadcasted_iota(jnp.int32, (16, 256), 0)
    pix = lax.broadcasted_iota(jnp.int32, (8, 256), 1)
    term = lax.broadcasted_iota(jnp.int32, (8, 256), 0)
    px = (pix & 15).astype(F32) - 7.5
    py = (pix >> 4).astype(F32) - 7.5
    basis = jnp.where(
        term == 0, px * px,
        jnp.where(
            term == 1, px * py,
            jnp.where(
                term == 2, py * py,
                jnp.where(term == 3, px, jnp.where(term == 4, py, jnp.where(term == 5, 1.0, 0.0))),
            ),
        ),
    )
    basis_b = jnp.concatenate([basis] * 4, axis=0).astype(BF16)
    basis_t = jnp.transpose(
        jnp.concatenate([basis, jnp.zeros((120, 256), F32)], axis=0)
    ).astype(BF16)
    row_t = lax.broadcasted_iota(jnp.int32, (256, 128), 0) & 7
    lane_t = lax.broadcasted_iota(jnp.int32, (256, 128), 1)
    own = (lane_t < 8) | ((lane_t & 7) == row_t)
    zero8 = jnp.zeros((8, 128), F32)
    both = range(BATCHES)

    sg_ref[...] = jnp.zeros(sg_ref.shape, F32)
    co_ref[...] = jnp.zeros(co_ref.shape, F32)
    err_ref[...] = jnp.zeros(err_ref.shape, F32)
    for b in both:
        rt_ref[b, 0:256, :] = basis_t
        rt_ref[b, 256:512, :] = basis_t

    def table(step, carry):
        for n in range(4):
            high = step * 4 + n
            for b in both:
                tiles = [feat_ref[high * 4 + i, b * 8 : b * 8 + 8, :] for i in range(4)]
                for q in range(3):
                    sf_ref[b, pl.ds(q * 256 + high, 8, stride=32), :] = by_quarter(
                        quarter, [turn(tiles[i], i - q) for i in range(4)]
                    )
        return carry

    lax.fori_loop(0, 8, table, 0)

    def screen(block, carry):
        row0 = pl.multiple_of(block * 8, 8)
        for b in both:

            def raw(f, b=b):
                return sf_ref[b, pl.ds(f * 32 + row0, 8), :]

            view = view_ref[b, pl.ds(row0, 8), :]
            cam = pick_camera(cam_ref, b, view)
            feats = list(
                screen_terms([raw(f) for f in range(3)], [raw(f) for f in range(3, 10)], cam)
            ) + [raw(10)]
            for channel in range(3):
                shade = raw(11 + channel)
                for view_no in range(1, VIEWS):
                    shade = jnp.where(view == view_no, raw(11 + 3 * view_no + channel), shade)
                feats.append(shade)
            for f in range(8):
                tab_ref[b, pl.ds(row0 * 8 + f, 8, stride=8), :] = feats[f]
            last_ref[b, pl.ds(row0, 8), :] = feats[8]
        return carry

    lax.fori_loop(0, 4, screen, 0)

    def group(group_no, carry):
        longest = jnp.int32(0)
        centre = []
        lengths = []
        for b in both:
            cx = zero8
            cy = zero8
            length = jnp.zeros((8, 128), jnp.int32)
            for t in range(8):
                tile = order_ref[b, group_no * 8 + t]
                tile_id = ids_ref[b, tile]
                in_view = lax.rem(tile_id, TILES_VIEW)
                row_t = lax.div(in_view, TILES_X)
                col_t = in_view - row_t * TILES_X
                tile_len = len_ref[b, tile]
                longest = jnp.maximum(longest, tile_len)
                here = (lane & 7) == t
                cx = jnp.where(here, (col_t * TILE + 8).astype(F32), cx)
                cy = jnp.where(here, (row_t * TILE + 8).astype(F32), cy)
                length = jnp.where(here, tile_len, length)
                sl_ref[b, t : t + 1, :] = slots_ref[b, pl.ds(tile, 1), :]
                for channel in range(3):
                    tg_ref[b, channel * 8 + t : channel * 8 + t + 1, :] = target_ref[
                        b, pl.ds(tile, 1), channel, :
                    ]
            centre.append((cx, cy))
            lengths.append(length)
        chunks = lax.div(longest + (16 * UNROLL - 1), 16 * UNROLL)

        def gather(i, carry):
            for b in both:
                for n in range(UNROLL):
                    j = i * UNROLL + n
                    half = pl.multiple_of(lax.div(j, 8) * 128, 128)
                    picked = take_lanes(
                        sl_ref[b, :, pl.ds(half, 128)], lane_k + lax.rem(j, 8) * 16
                    )
                    picked = jnp.sum(
                        jnp.where(diag, picked.astype(F32), 0.0), axis=0, keepdims=True
                    )
                    index = jnp.broadcast_to(picked.astype(jnp.int32), (8, 128))
                    low = index & 127
                    high = index >> 7
                    acc = zero8
                    for h in range(32):
                        got = take_lanes(tab_ref[b, h * 8 : h * 8 + 8, :], low)
                        acc = jnp.where(high == h, got, acc)
                    ix_ref[b, pl.ds(j, 1), :] = index[0:1]
                    fr_ref[b, pl.ds(j, 8, stride=16), :] = acc
            return carry

        lax.fori_loop(0, chunks, gather, 0)

        for b in both:
            cx, cy = centre[b]
            for part in range(2):
                c0 = part * 8

                def got(f, b=b, c0=c0):
                    return fr_ref[b, f * 16 + c0 : f * 16 + c0 + 8, :]

                index = ix_ref[b, c0 : c0 + 8, :]
                low = index & 127
                high = index >> 7
                last = zero8
                for h in range(32):
                    row = jnp.broadcast_to(last_ref[b, h : h + 1, :], (8, 128))
                    last = jnp.where(high == h, take_lanes(row, low), last)
                u = got(0) - cx
                v = got(1) - cy
                con_a, con_b, con_c = [got(f) for f in range(2, 5)]
                fr_ref[b, c0 : c0 + 8, :] = u
                fr_ref[b, 16 + c0 : 16 + c0 + 8, :] = v
                live = (lane_k + (sub + c0) * 16) < lengths[b]
                coefs = [
                    con_a * (-0.5 * LOG2_E),
                    con_b * -LOG2_E,
                    con_c * (-0.5 * LOG2_E),
                    (con_a * u + con_b * v) * LOG2_E,
                    (con_b * u + con_c * v) * LOG2_E,
                    jnp.where(
                        live,
                        (got(5) - 0.5 * (con_a * u * u + con_c * v * v) - con_b * u * v) * LOG2_E,
                        -1e30,
                    ),
                ]
                for f, value in enumerate(coefs):
                    hi, rest = split2(value)
                    mid, lo = split2(rest)
                    for p, piece in enumerate((hi, mid, lo)):
                        co_ref[b, pl.ds(c0 * 32 + p * 8 + f, 8, stride=32), :] = piece
                for channel, shade in enumerate((got(6), got(7), last)):
                    hi, lo = split2(shade)
                    cc_ref[b, pl.ds(c0 * 8 + channel, 8, stride=8), :] = hi
                    cc_ref[b, pl.ds(c0 * 8 + 3 + channel, 8, stride=8), :] = lo

        def colours_of(b, i):
            rows = cc_ref[b, pl.ds(pl.multiple_of(i * 16, 16), 16), :]
            return jnp.concatenate(
                [
                    jnp.concatenate(
                        [jnp.where(diag, rows[n * 8 + r : n * 8 + r + 1], 0.0) for r in range(6)],
                        axis=0,
                    )
                    for n in range(2)
                ],
                axis=1,
            ).astype(BF16)

        def fade(b, i):
            row0 = pl.multiple_of(i * 256, 256)
            pair = co_ref[b, pl.ds(pl.multiple_of(i * 64, 64), 64), :].astype(BF16)
            lhs = jnp.concatenate([pair[0:32], pair[32:64]], axis=1)
            al_ref[b, pl.ds(row0, 256), :] = jnp.exp2(dot(lhs, basis_b, TN))

        def weigh(b, i, through):
            row0 = pl.multiple_of(i * 256, 256)
            alphas = al_ref[b, pl.ds(row0, 256), :]
            weights = []
            for k in range(32):
                weight = through * alphas[k * 8 : k * 8 + 8]
                through = through - weight
                weights.append(weight)
            weight = jnp.concatenate(weights, axis=0)
            w_hi, w_lo = split2(weight)
            w_ref[b, pl.ds(row0, 256), :] = weight
            ww_ref[b, pl.ds(row0, 256), 0:256] = w_hi.astype(BF16)
            ww_ref[b, pl.ds(row0, 256), 256:512] = w_lo.astype(BF16)
            return through

        def shade(b, i, colour):
            row0 = pl.multiple_of(i * 256, 256)
            c_two = colours_of(b, i)
            prod = dot(c_two, ww_ref[b, pl.ds(row0, 256), 0:256], NN)
            prod_lo = dot(c_two, ww_ref[b, pl.ds(row0, 256), 256:512], NN)
            return colour + prod[0:24] + prod[24:48] + prod_lo[0:24] + prod_lo[24:48]

        def forward(i, carry):
            carry = list(carry)
            colours = [shade(b, i - 1, carry[b][1]) for b in both]
            through = [weigh(b, i, carry[b][0]) for b in both]
            for b in both:
                fade(b, i + 1)
            return tuple((through[b], colours[b]) for b in both)

        for b in both:
            fade(b, 0)
        start = [weigh(b, 0, jnp.ones((8, 256), F32)) for b in both]
        for b in both:
            fade(b, 1)
        dark = jnp.zeros((24, 256), F32)
        done = lax.fori_loop(1, chunks, forward, tuple((start[b], dark) for b in both))
        done = [(None, shade(b, chunks - 1, done[b][1])) for b in both]
        r_four = []
        for b in both:
            resid = done[b][1] - tg_ref[b]
            err_ref[b] += resid * resid
            r_hi, r_lo = split2(2.0 * resid)
            r_four.append(jnp.concatenate([r_hi, r_hi, r_lo, r_lo], axis=0).astype(BF16))
            r_t = jnp.transpose(
                jnp.concatenate(
                    [jnp.zeros((8, 256), F32), r_hi, r_lo, jnp.zeros((72, 256), F32)], axis=0
                )
            ).astype(BF16)
            rt_ref[b, 512:768, :] = r_t
            rt_ref[b, 768:1024, :] = r_t

        def pull(b, i):
            c_two = colours_of(b, i)
            pl_ref[b] = dot(jnp.concatenate([c_two, c_two], axis=0), r_four[b], TN)

        def slope(b, i, behind):
            row0 = pl.multiple_of(i * 256, 256)
            pulls = pl_ref[b]
            alphas = al_ref[b, pl.ds(row0, 256), :]
            weight = w_ref[b, pl.ds(row0, 256), :]
            parts = []
            for k in range(31, -1, -1):
                diff = pulls[k * 8 : k * 8 + 8] - behind
                parts.append(weight[k * 8 : k * 8 + 8] * diff)
                behind = behind + alphas[k * 8 : k * 8 + 8] * diff
            d_hi, d_lo = split2(jnp.concatenate(parts[::-1], axis=0))
            dd_ref[b, :, 0:256] = d_hi.astype(BF16)
            dd_ref[b, :, 256:512] = d_lo.astype(BF16)
            return behind

        def collect(b, i):
            row0 = pl.multiple_of(i * 256, 256)
            lhs = jnp.concatenate([dd_ref[b], ww_ref[b, pl.ds(row0, 256), :]], axis=1)
            sums = jnp.where(own, dot(lhs, rt_ref[b], NN), 0.0)
            for n in range(2):
                flip = jnp.transpose(sums[n * 128 : n * 128 + 128])
                j = i * 2 + n
                mo_ref[b, pl.ds(j, 8, stride=16), :] = flip[0:8]
                for h in range(3):
                    mo_ref[b, pl.ds((8 + h) * 16 + j, 1), :] = jnp.sum(
                        flip[8 + h * 8 : 16 + h * 8] + flip[32 + h * 8 : 40 + h * 8],
                        axis=0,
                        keepdims=True,
                    )

        def backward(step, carry):
            i = chunks - 1 - step
            for b in both:
                collect(b, i + 1)
            carry = tuple(slope(b, i, carry[b]) for b in both)
            for b in both:
                pull(b, jnp.maximum(i - 1, 0))
            return carry

        for b in both:
            pull(b, chunks - 1)
        start = tuple(slope(b, chunks - 1, jnp.zeros((8, 256), F32)) for b in both)
        for b in both:
            pull(b, jnp.maximum(chunks - 2, 0))
        lax.fori_loop(1, chunks, backward, start)
        for b in both:
            collect(b, 0)

        for b in both:
            for part in range(2):
                c0 = part * 8

                def moment(f, b=b, c0=c0):
                    return mo_ref[b, f * 16 + c0 : f * 16 + c0 + 8, :]

                u, v, con_a, con_b, con_c = [
                    fr_ref[b, f * 16 + c0 : f * 16 + c0 + 8, :] for f in range(5)
                ]
                m_xx, m_xy, m_yy, m_x, m_y, m_1 = [moment(f) for f in range(6)]
                s_x = m_x - u * m_1
                s_y = m_y - v * m_1
                grads = [
                    con_a * s_x + con_b * s_y,
                    con_b * s_x + con_c * s_y,
                    -0.5 * (m_xx - u * (m_x + s_x)),
                    -(m_xy - u * m_y - v * s_x),
                    -0.5 * (m_yy - v * (m_y + s_y)),
                    m_1,
                    moment(8),
                    moment(9),
                    moment(10),
                ]
                for f, value in enumerate(grads):
                    hi, lo = split2(value)
                    gr_ref[b, f * 16 + c0 : f * 16 + c0 + 8, :] = hi
                    gr_ref[b, 144 + f * 16 + c0 : 144 + f * 16 + c0 + 8, :] = lo

        def scatter(i, carry):
            j = i * 2
            for b in both:
                index = jnp.concatenate(
                    [ix_ref[b, pl.ds(j, 1), :], ix_ref[b, pl.ds(j + 1, 1), :]], axis=1
                )
                hit = row_a == (index >> 8)
                rows = []
                for f in range(18):
                    row = f * 16 + j
                    value = jnp.concatenate(
                        [gr_ref[b, pl.ds(row, 1), :], gr_ref[b, pl.ds(row + 1, 1), :]], axis=1
                    )
                    rows.append(jnp.where(hit, value, 0.0))
                add = dot(jnp.concatenate(rows, axis=0).astype(BF16), scatter_rhs(index), NT)
                add = add[0:144] + add[144:288]
                for half in range(2):
                    sg_ref[b, half, 0:144, :] += add[:, half * 128 : half * 128 + 128]
            return carry

        lax.fori_loop(0, chunks, scatter, 0)
        return carry

    lax.fori_loop(0, GROUPS, group, 0)
    for b in both:
        total = jnp.sum(jnp.sum(err_ref[b], axis=0, keepdims=True), axis=1, keepdims=True)
        for half in range(2):
            sg_ref[b, half, 144:160, :] = view_ref[b, pl.ds(half, 16, stride=2), :]
            sg_ref[b, half, 240:256, :] = jnp.broadcast_to(total, (16, 128))

    for a in range(16):
        for half in range(2):
            parts = [
                sg_ref[b, half, pl.ds(q * 128 + a, 8, stride=16), :]
                for b in both
                for q in range(2)
            ]
            for r in range(4):
                out_ref[(a * 2 + half) * 4 + r] = by_quarter(
                    quarter, [turn(parts[q], q - r) for q in range(4)]
                )


def grads_kernel(
    cam_ref, params_ref, send_ref, grad_ref, out_ref, err_ref, flat_ref, res_ref, gg_ref, sems
):
    copies = fetch_params(params_ref, flat_ref, sems)
    row_a = lax.broadcasted_iota(jnp.int32, (16, 256), 0)
    quarter = lax.broadcasted_iota(jnp.int32, (8, 128), 1) >> 5
    gg_ref[...] = jnp.zeros(gg_ref.shape, F32)

    def place(chunk, total):
        tiles = [grad_ref[chunk * 8 + i] for i in range(8)]
        for tile in tiles:
            total = total + tile
        for batch_no in range(BATCHES):
            index = send_ref[batch_no, pl.ds(chunk, 1), :]
            hit = row_a == (index >> 8)
            rhs = scatter_rhs(index)
            high = []
            low = []
            for q in range(2):
                values = jnp.concatenate(
                    [
                        by_quarter(
                            quarter,
                            [turn(tiles[4 * n + i], i - 2 * batch_no - q) for i in range(4)],
                        )
                        for n in range(2)
                    ],
                    axis=1,
                )
                g_hi, g_lo = split2(values)
                for f in range(8 if q == 0 else 2):
                    high.append(jnp.where(hit, g_hi[f : f + 1], 0.0))
                    low.append(jnp.where(hit, g_lo[f : f + 1], 0.0))
            add = dot(jnp.concatenate(high + low, axis=0).astype(BF16), rhs, NT)
            gg_ref[batch_no] += add[0:160] + add[160:320]
        return total

    total = lax.fori_loop(0, 16, place, jnp.zeros((8, 128), F32))
    for copy in copies:
        copy.wait()

    def block(block_no, carry):
        row0 = pl.multiple_of((block_no // 2) * 8, 8)
        half = block_no % 2
        lane0 = pl.multiple_of(half * 128, 128)
        cols = [param_rows(flat_ref, row0, half, p) for p in range(PARAMS)]
        geo = [0.0] * 10
        opac = 0.0
        shade = [0.0] * 48
        for batch_no in range(BATCHES):

            def feat(f, batch_no=batch_no):
                return gg_ref[batch_no, pl.ds(f * 16 + row0, 8), pl.ds(lane0, 128)]

            cam = pick_camera(cam_ref, batch_no, feat(9))
            _, pull_geo = jax.vjp(
                lambda c: screen_terms(c[0:3], shape_terms(c), cam), cols[0:10]
            )
            (d_geo,) = pull_geo(tuple(feat(f) for f in range(5)))
            basis, pull_ray = jax.vjp(lambda c: ray_basis(c, cam), cols[0:3])
            d_col = [feat(6 + h) for h in range(3)]
            (d_ray,) = pull_ray(
                [
                    d_col[0] * cols[11 + k] + d_col[1] * cols[27 + k] + d_col[2] * cols[43 + k]
                    for k in range(16)
                ]
            )
            for i in range(10):
                geo[i] = geo[i] + d_geo[i]
            for i in range(3):
                geo[i] = geo[i] + d_ray[i]
            opac = opac + feat(5)
            for h in range(3):
                for k in range(16):
                    shade[16 * h + k] = shade[16 * h + k] + d_col[h] * basis[k]
        opac = opac / (1.0 + jnp.exp(cols[10]))
        for p, value in enumerate(geo + [opac] + shade):
            res_ref[pl.ds((2 * row0 + half) * PITCH + p, 8, stride=2 * PITCH), :] = value
        return carry

    lax.fori_loop(0, 4, block, 0)
    copies = [
        pltpu.make_async_copy(
            res_ref.at[pl.ds(j * PITCH, PARAMS), :],
            out_ref.at[:, pl.ds(j * 128, 128)],
            sems.at[j],
        )
        for j in range(32)
    ]
    for copy in copies:
        copy.start()
    lane = lax.broadcasted_iota(jnp.int32, (1, 128), 1)
    errors = jnp.sum(
        jnp.where((lane == 32) | (lane == 96), total[7:8], 0.0), axis=1, keepdims=True
    )
    err_ref[...] = errors * (1.0 / (BATCHES * OWNERS * TILES_DEV * 3 * TILE_PX))
    for copy in copies:
        copy.wait()


def exchange(values):
    return lax.all_to_all(values, "dev", split_axis=0, concat_axis=0, tiled=True)


SMEM = pl.BlockSpec(memory_space=pltpu.SMEM)
VMEM = pl.BlockSpec(memory_space=pltpu.VMEM)
HBM = pl.BlockSpec(memory_space=pl.ANY)
CALL = pltpu.CompilerParams(vmem_limit_bytes=VMEM_BYTES)


def local(params, cameras, send_lists, tile_slots, tile_ids, tile_len, targets):
    cams = camera_table(cameras)
    lengths = tile_len[:, 0]
    tile_no = jnp.arange(TILES_DEV, dtype=jnp.int32)
    ahead = (lengths[:, None, :] > lengths[:, :, None]) | (
        (lengths[:, None, :] == lengths[:, :, None]) & (tile_no[None, None, :] < tile_no[None, :, None])
    )
    rank = jnp.sum(ahead.astype(jnp.int32), axis=2)
    order = jnp.sum(
        jnp.where(rank[:, None, :] == tile_no[None, :, None], tile_no[None, None, :], 0), axis=2
    )
    send = send_lists[:, 0].reshape(BATCHES, 16, 256)

    feats = pl.pallas_call(
        offer_kernel,
        out_shape=jax.ShapeDtypeStruct((OWNERS, 16, 128), F32),
        in_specs=[SMEM, HBM, VMEM],
        out_specs=VMEM,
        scratch_shapes=[
            pltpu.VMEM((32 * PITCH, 128), F32),
            pltpu.VMEM((BATCHES, 768, 128), F32),
            pltpu.VMEM((BATCHES, 768, 256), BF16),
            pltpu.VMEM((BATCHES, 256, 256), BF16),
            pltpu.SemaphoreType.DMA((32,)),
        ],
        compiler_params=CALL,
        name="offer",
    )(cams, params, send)
    feats = exchange(feats)

    views = pl.pallas_call(
        views_kernel,
        out_shape=jax.ShapeDtypeStruct((BATCHES, 32, 128), F32),
        in_specs=[SMEM, VMEM],
        out_specs=VMEM,
        compiler_params=CALL,
        name="slot_views",
    )(tile_ids, tile_slots)

    rows = TILES_DEV // GROUPS * PAIRS
    slot_grads = pl.pallas_call(
        blend_kernel,
        out_shape=jax.ShapeDtypeStruct((OWNERS, 8, 128), F32),
        in_specs=[SMEM, SMEM, SMEM, SMEM, VMEM, VMEM, VMEM, VMEM],
        out_specs=VMEM,
        scratch_shapes=[
            pltpu.VMEM((BATCHES, 768, 128), F32),
            pltpu.VMEM((BATCHES, 256, 128), F32),
            pltpu.VMEM((BATCHES, 32, 128), F32),
            pltpu.VMEM((BATCHES, 8, 256), jnp.int32),
            pltpu.VMEM((BATCHES, 24, 256), F32),
            pltpu.VMEM((BATCHES, 128, 128), F32),
            pltpu.VMEM((BATCHES, 16, 128), jnp.int32),
            pltpu.VMEM((BATCHES, 576, 128), F32),
            pltpu.VMEM((BATCHES, 128, 128), F32),
            pltpu.VMEM((BATCHES, rows + 256, 256), F32),
            pltpu.VMEM((BATCHES, rows, 256), F32),
            pltpu.VMEM((BATCHES, rows, 512), BF16),
            pltpu.VMEM((BATCHES, 256, 256), F32),
            pltpu.VMEM((BATCHES, 256, 512), BF16),
            pltpu.VMEM((BATCHES, 1024, 128), BF16),
            pltpu.VMEM((BATCHES, 176, 128), F32),
            pltpu.VMEM((BATCHES, 288, 128), F32),
            pltpu.VMEM((BATCHES, 2, 256, 128), F32),
            pltpu.VMEM((BATCHES, 24, 256), F32),
        ],
        compiler_params=CALL,
        name="blend",
    )(order, tile_ids, lengths, cams, feats, views, tile_slots, targets)
    slot_grads = exchange(slot_grads)

    grads, err = pl.pallas_call(
        grads_kernel,
        out_shape=(
            jax.ShapeDtypeStruct((PARAMS, 4096), F32),
            jax.ShapeDtypeStruct((1, 1), F32),
        ),
        in_specs=[SMEM, HBM, VMEM, VMEM],
        out_specs=(HBM, VMEM),
        scratch_shapes=[
            pltpu.VMEM((32 * PITCH, 128), F32),
            pltpu.VMEM((32 * PITCH, 128), F32),
            pltpu.VMEM((BATCHES, 160, 256), F32),
            pltpu.SemaphoreType.DMA((32,)),
        ],
        compiler_params=CALL,
        name="param_grads",
    )(cams, params, send, slot_grads)
    return (grads, err[0, 0])


def solution(mesh):
    placed = (
        P(None, "dev"),
        P(),
        P(None, "dev", None, None),
        P(None, "dev", None),
        P(None, "dev"),
        P(None, "dev", None),
        P(None, "dev", None, None),
    )
    return jax.shard_map(
        local, mesh=mesh, in_specs=placed, out_specs=(P(None, "dev"), P()), check_vma=False
    )
```

```python
import jax
import jax.numpy as jnp
from jax import lax
from jax.experimental import pallas as pl
from jax.experimental.pallas import tpu as pltpu
from jax.sharding import PartitionSpec as P

BATCHES = 2
TILE = 16
PAIRS = 256
TILE_PX = 256
TILES_X = 240
TILES_VIEW = 32400
VIEWS = 4
PARAMS = 59
TILES_DEV = 32
OWNERS = 128
CAP = 32
SLOTS = 4096
GROUPS = 4
PITCH = 72
LOG2_E = 1.4426950408889634
VMEM_BYTES = 56 * 1024 * 1024

SH_ZERO = 0.28209479177387814
SH_ONE = 0.4886025119029199
SH_TWO = (
    1.0925484305920792,
    -1.0925484305920792,
    0.31539156525252005,
    -1.0925484305920792,
    0.5462742152960396,
)
SH_THREE = (
    -0.5900435899266435,
    2.890611442640554,
    -0.4570457994644658,
    0.3731763325901154,
    -0.4570457994644658,
    1.445305721320277,
    -0.5900435899266435,
)

F32 = jnp.float32
BF16 = jnp.bfloat16
NN = (((1,), (0,)), ((), ()))
NT = (((1,), (1,)), ((), ()))
TN = (((0,), (0,)), ((), ()))


def dot(lhs, rhs, dims):
    return lax.dot_general(lhs, rhs, dims, preferred_element_type=F32)


def split2(value):
    high = value.astype(BF16).astype(F32)
    return high, value - high


def camera_table(cameras):
    cos_yaw = jnp.cos(cameras[:, :, 0])
    sin_yaw = jnp.sin(cameras[:, :, 0])
    cos_pitch = jnp.cos(cameras[:, :, 1])
    sin_pitch = jnp.sin(cameras[:, :, 1])
    frame = [
        cos_yaw,
        sin_yaw,
        sin_pitch * sin_yaw,
        cos_pitch,
        -sin_pitch * cos_yaw,
        -cos_pitch * sin_yaw,
        sin_pitch,
        cos_pitch * cos_yaw,
    ]
    shift = [cameras[:, :, 2], cameras[:, :, 3], cameras[:, :, 4]]
    centre = [
        -(frame[0] * shift[0] + frame[2] * shift[1] + frame[5] * shift[2]),
        -(frame[3] * shift[1] + frame[6] * shift[2]),
        -(frame[1] * shift[0] + frame[4] * shift[1] + frame[7] * shift[2]),
    ]
    rest = [cameras[:, :, 5], cameras[:, :, 6], cameras[:, :, 7]]
    return jnp.stack(frame + shift + centre + rest)


CAM_ROWS = 17


def sh_basis(dir_x, dir_y, dir_z):
    square_x = dir_x * dir_x
    square_y = dir_y * dir_y
    square_z = dir_z * dir_z
    return [
        SH_ZERO * jnp.ones_like(dir_x),
        -SH_ONE * dir_y,
        SH_ONE * dir_z,
        -SH_ONE * dir_x,
        SH_TWO[0] * dir_x * dir_y,
        SH_TWO[1] * dir_y * dir_z,
        SH_TWO[2] * (2.0 * square_z - square_x - square_y),
        SH_TWO[3] * dir_x * dir_z,
        SH_TWO[4] * (square_x - square_y),
        SH_THREE[0] * dir_y * (3.0 * square_x - square_y),
        SH_THREE[1] * dir_x * dir_y * dir_z,
        SH_THREE[2] * dir_y * (4.0 * square_z - square_x - square_y),
        SH_THREE[3] * dir_z * (2.0 * square_z - 3.0 * square_x - 3.0 * square_y),
        SH_THREE[4] * dir_x * (4.0 * square_z - square_x - square_y),
        SH_THREE[5] * dir_z * (square_x - square_y),
        SH_THREE[6] * dir_x * (square_x - 3.0 * square_y),
    ]


def shape_terms(cols):
    inv_quat = 1.0 / jnp.sqrt(
        cols[6] * cols[6] + cols[7] * cols[7] + cols[8] * cols[8] + cols[9] * cols[9]
    )
    return [jnp.exp(cols[3 + i]) for i in range(3)] + [cols[6 + i] * inv_quat for i in range(4)]


def screen_terms(position, shape, cam):
    spread = shape[0:3]
    quat_w, quat_x, quat_y, quat_z = shape[3:7]
    frame = ((cam[0], None, cam[1]), (cam[2], cam[3], cam[4]), (cam[5], cam[6], cam[7]))
    shift = cam[8:11]
    focal = cam[14]
    viewed = [
        frame[0][0] * position[0] + frame[0][2] * position[2] + shift[0],
        frame[1][0] * position[0]
        + frame[1][1] * position[1]
        + frame[1][2] * position[2]
        + shift[1],
        frame[2][0] * position[0]
        + frame[2][1] * position[1]
        + frame[2][2] * position[2]
        + shift[2],
    ]
    inv_depth = 1.0 / viewed[2]
    screen_u = focal * viewed[0] * inv_depth + cam[15]
    screen_v = focal * viewed[1] * inv_depth + cam[16]
    rotation = (
        (
            1.0 - 2.0 * (quat_y * quat_y + quat_z * quat_z),
            2.0 * (quat_x * quat_y - quat_w * quat_z),
            2.0 * (quat_x * quat_z + quat_w * quat_y),
        ),
        (
            2.0 * (quat_x * quat_y + quat_w * quat_z),
            1.0 - 2.0 * (quat_x * quat_x + quat_z * quat_z),
            2.0 * (quat_y * quat_z - quat_w * quat_x),
        ),
        (
            2.0 * (quat_x * quat_z - quat_w * quat_y),
            2.0 * (quat_y * quat_z + quat_w * quat_x),
            1.0 - 2.0 * (quat_x * quat_x + quat_y * quat_y),
        ),
    )
    jac_main = focal * inv_depth
    jac_u = -jac_main * viewed[0] * inv_depth
    jac_v = -jac_main * viewed[1] * inv_depth
    row_u = [
        jac_main * frame[0][0] + jac_u * frame[2][0],
        jac_u * frame[2][1],
        jac_main * frame[0][2] + jac_u * frame[2][2],
    ]
    row_v = [jac_main * frame[1][i] + jac_v * frame[2][i] for i in range(3)]
    along_u = [
        (row_u[0] * rotation[0][j] + row_u[1] * rotation[1][j] + row_u[2] * rotation[2][j])
        * spread[j]
        for j in range(3)
    ]
    along_v = [
        (row_v[0] * rotation[0][j] + row_v[1] * rotation[1][j] + row_v[2] * rotation[2][j])
        * spread[j]
        for j in range(3)
    ]
    cov_uu = along_u[0] * along_u[0] + along_u[1] * along_u[1] + along_u[2] * along_u[2] + 0.3
    cov_uv = along_u[0] * along_v[0] + along_u[1] * along_v[1] + along_u[2] * along_v[2]
    cov_vv = along_v[0] * along_v[0] + along_v[1] * along_v[1] + along_v[2] * along_v[2] + 0.3
    inv_det = 1.0 / (cov_uu * cov_vv - cov_uv * cov_uv)
    return screen_u, screen_v, cov_vv * inv_det, -cov_uv * inv_det, cov_uu * inv_det


def ray_basis(position, cam):
    ray = [position[i] - cam[11 + i] for i in range(3)]
    inv_len = 1.0 / jnp.sqrt(ray[0] * ray[0] + ray[1] * ray[1] + ray[2] * ray[2])
    return sh_basis(ray[0] * inv_len, ray[1] * inv_len, ray[2] * inv_len)


def pick_camera(cam_ref, batch_no, view):
    picked = []
    for row in range(CAM_ROWS):
        value = jnp.full(view.shape, cam_ref[row, batch_no, VIEWS - 1], F32)
        for view_no in range(VIEWS - 2, -1, -1):
            value = jnp.where(view == view_no, cam_ref[row, batch_no, view_no], value)
        picked.append(value)
    return picked


def take_lanes(table, index):
    return jnp.take_along_axis(table, index, axis=1, mode="promise_in_bounds")


def by_quarter(quarter, values):
    out = values[0]
    for q in range(1, len(values)):
        out = jnp.where(quarter == q, values[q], out)
    return out


def turn(value, quarters):
    quarters = quarters % 4
    return value if quarters == 0 else pltpu.roll(value, 32 * quarters, 1)


def scatter_rhs(index):
    row = lax.broadcasted_iota(jnp.int32, (256, index.shape[1]), 0)
    return jnp.where(row == (index & 255), 1.0, 0.0).astype(BF16)


def fetch_params(params_ref, flat_ref, sems):
    copies = [
        pltpu.make_async_copy(
            params_ref.at[:, pl.ds(j * 128, 128)],
            flat_ref.at[pl.ds(j * PITCH, PARAMS), :],
            sems.at[j],
        )
        for j in range(32)
    ]
    for copy in copies:
        copy.start()
    return copies


def param_rows(flat_ref, row0, half, param):
    return flat_ref[pl.ds((2 * row0 + half) * PITCH + param, 8, stride=2 * PITCH), :]


def offer_kernel(
    cam_ref, params_ref, send_ref, out_ref, flat_ref, tab_ref, two_ref, sems
):
    copies = fetch_params(params_ref, flat_ref, sems)
    quarter = lax.broadcasted_iota(jnp.int32, (8, 128), 1) >> 5
    row_low = lax.broadcasted_iota(jnp.int32, (128, 256), 0)
    for copy in copies:
        copy.wait()

    def block(block_no, carry):
        row0 = (block_no // 2) * 8
        half = block_no % 2
        cols = [param_rows(flat_ref, row0, half, p) for p in range(PARAMS)]
        opac = -(jnp.maximum(-cols[10], 0.0) + jnp.log1p(jnp.exp(-jnp.abs(cols[10]))))
        shared = cols[0:3] + shape_terms(cols) + [opac]
        for batch_no in range(BATCHES):
            feats = list(shared)
            for view_no in range(VIEWS):
                cam = [cam_ref[row, batch_no, view_no] for row in range(CAM_ROWS)]
                basis = ray_basis(cols[0:3], cam)
                for channel in range(3):
                    shade = 0.5
                    for term in range(16):
                        shade = shade + basis[term] * cols[11 + 16 * channel + term]
                    feats.append(shade)
            feats.append(jnp.zeros((8, 128), F32))
            for f, value in enumerate(feats):
                start = (2 * row0 + half) * 24 + f
                tab_ref[batch_no, pl.ds(start, 8, stride=48), :] = value
        return carry

    lax.fori_loop(0, 4, block, 0)

    def pieces(step, carry):
        for batch_no in range(BATCHES):
            for n in range(8):
                h = step * 8 + n
                hi, mid = split2(tab_ref[batch_no, pl.ds(pl.multiple_of(h * 24 + 8, 8), 16), :])
                row = pl.multiple_of(h * 16, 16)
                two_ref[batch_no, pl.ds(row, 16), 0:128] = hi.astype(BF16)
                two_ref[batch_no, pl.ds(row, 16), 128:256] = mid.astype(BF16)
        return carry

    lax.fori_loop(0, 4, pieces, 0)

    def pick(chunk, carry):
        for batch_no in range(BATCHES):
            index = send_ref[batch_no, pl.ds(chunk, 1), :]
            high = jnp.broadcast_to(index >> 7, (8, 256))
            low = jnp.broadcast_to(index & 127, (8, 256))
            one = jnp.where(row_low == (index & 127), 1.0, 0.0).astype(BF16)
            one = jnp.concatenate([one, one], axis=0)
            exact = [jnp.zeros((8, 128), F32)] * 2
            acc = [jnp.zeros((8, 256), F32)] * 2
            for part in range(4):
                got = dot(two_ref[batch_no, part * 128 : part * 128 + 128, :], one, NN)
                for n in range(8):
                    h = part * 8 + n
                    hit = high == h
                    for q in range(2):
                        row = n * 16 + q * 8
                        acc[q] = jnp.where(hit, got[row : row + 8], acc[q])
                    rows = tab_ref[batch_no, h * 24 : h * 24 + 8, :]
                    for half in range(2):
                        lanes = slice(half * 128, half * 128 + 128)
                        exact[half] = jnp.where(
                            hit[:, lanes], take_lanes(rows, low[:, lanes]), exact[half]
                        )
            for half in range(2):
                lanes = slice(half * 128, half * 128 + 128)
                cut = [exact[half], acc[0][:, lanes], acc[1][:, lanes]]
                for r in range(4):
                    out_ref[(chunk * 2 + half) * 4 + r, batch_no * 8 : batch_no * 8 + 8, :] = (
                        by_quarter(quarter, [turn(cut[q], q - r) for q in range(3)])
                    )
        return carry

    lax.fori_loop(0, 16, pick, 0)


def plan_kernel(
    order_ref, ids_ref, len_ref, slots_ref, target_ref,
    out_ref, ix_ref, tile_ref, aim_ref, sl_ref,
):
    lane = lax.broadcasted_iota(jnp.int32, (8, 128), 1)
    sub = lax.broadcasted_iota(jnp.int32, (8, 128), 0)
    diag = sub == (lane & 7)

    def group(group_no, carry):
        for b in range(BATCHES):
            cx = jnp.zeros((1, 128), F32)
            cy = jnp.zeros((1, 128), F32)
            length = jnp.zeros((1, 128), F32)
            for t in range(8):
                tile = order_ref[b, group_no * 8 + t]
                in_view = lax.rem(ids_ref[b, tile], TILES_VIEW)
                row_t = lax.div(in_view, TILES_X)
                col_t = in_view - row_t * TILES_X
                here = (lane[0:1] & 7) == t
                cx = jnp.where(here, (col_t * TILE + 8).astype(F32), cx)
                cy = jnp.where(here, (row_t * TILE + 8).astype(F32), cy)
                length = jnp.where(here, len_ref[b, tile].astype(F32), length)
                sl_ref[b, t : t + 1, :] = slots_ref[b, pl.ds(tile, 1), :]
                for channel in range(3):
                    aim_ref[b, pl.ds(group_no * 24 + channel * 8 + t, 1), :] = target_ref[
                        b, pl.ds(tile, 1), channel, :
                    ]
            tile_ref[b, pl.ds(pl.multiple_of(group_no * 8, 8), 8), :] = jnp.concatenate(
                [cx, cy, length, jnp.zeros((5, 128), F32)], axis=0
            )
            picks = []
            for j in range(16):
                half = (j // 8) * 128
                picked = take_lanes(sl_ref[b, :, half : half + 128], (lane >> 3) + (j % 8) * 16)
                picks.append(
                    jnp.sum(jnp.where(diag, picked.astype(F32), 0.0), axis=0, keepdims=True)
                )
            ix_ref[b, pl.ds(pl.multiple_of(group_no * 16, 16), 16), :] = jnp.concatenate(
                picks, axis=0
            ).astype(jnp.int32)
        return carry

    lax.fori_loop(0, GROUPS, group, 0)
    row_high = lax.broadcasted_iota(jnp.int32, (32, PAIRS), 0)
    row_low = lax.broadcasted_iota(jnp.int32, (128, PAIRS), 0)

    def step(tile_no, sums):
        out = []
        for b in range(BATCHES):
            view = lax.div(ids_ref[b, tile_no], TILES_VIEW).astype(F32) * 0.5
            slots = slots_ref[b, pl.ds(tile_no, 1), :]
            lhs = jnp.where(row_high == (slots >> 7), view, 0.0).astype(BF16)
            rhs = jnp.where(row_low == (slots & 127), 1.0, 0.0).astype(BF16)
            out.append(sums[b] + dot(lhs, rhs, NT))
        return tuple(out)

    zero = jnp.zeros((32, 128), F32)
    sums = lax.fori_loop(0, TILES_DEV, step, (zero, zero))
    for b in range(BATCHES):
        out_ref[b] = sums[b]


def blend_kernel(
    order_ref, len_ref, cam_ref, feat_ref, view_ref, ix_ref, tile_ref, aim_ref, out_ref,
    sf_ref, tab_ref, two_ref, fr_ref, co_ref, cc_ref,
    al_ref, w_ref, ww_ref, pl_ref, dd_ref, rt_ref, mo_ref, gr_ref, sg_ref, err_ref,
):
    lane = lax.broadcasted_iota(jnp.int32, (8, 128), 1)
    sub = lax.broadcasted_iota(jnp.int32, (8, 128), 0)
    quarter = lane >> 5
    diag = sub == (lane & 7)
    lane_k = lane >> 3
    row_a = lax.broadcasted_iota(jnp.int32, (16, 256), 0)
    row_low = lax.broadcasted_iota(jnp.int32, (128, 256), 0)
    pix = lax.broadcasted_iota(jnp.int32, (8, 256), 1)
    term = lax.broadcasted_iota(jnp.int32, (8, 256), 0)
    px = (pix & 15).astype(F32) - 7.5
    py = (pix >> 4).astype(F32) - 7.5
    basis = jnp.where(
        term == 0, px * px,
        jnp.where(
            term == 1, px * py,
            jnp.where(
                term == 2, py * py,
                jnp.where(term == 3, px, jnp.where(term == 4, py, jnp.where(term == 5, 1.0, 0.0))),
            ),
        ),
    )
    basis_b = jnp.concatenate([basis] * 4, axis=0).astype(BF16)
    basis_t = jnp.transpose(
        jnp.concatenate([basis, jnp.zeros((120, 256), F32)], axis=0)
    ).astype(BF16)
    row_t = lax.broadcasted_iota(jnp.int32, (256, 128), 0) & 7
    lane_t = lax.broadcasted_iota(jnp.int32, (256, 128), 1)
    own = (lane_t < 8) | ((lane_t & 7) == row_t)
    zero8 = jnp.zeros((8, 128), F32)
    both = range(BATCHES)

    sg_ref[...] = jnp.zeros(sg_ref.shape, F32)
    co_ref[...] = jnp.zeros(co_ref.shape, F32)
    err_ref[...] = jnp.zeros(err_ref.shape, F32)
    for b in both:
        rt_ref[b, 0:256, :] = basis_t
        rt_ref[b, 256:512, :] = basis_t

    def table(step, carry):
        for n in range(4):
            high = step * 4 + n
            for b in both:
                tiles = [feat_ref[high * 4 + i, b * 8 : b * 8 + 8, :] for i in range(4)]
                for q in range(3):
                    sf_ref[b, pl.ds(q * 256 + high, 8, stride=32), :] = by_quarter(
                        quarter, [turn(tiles[i], i - q) for i in range(4)]
                    )
        return carry

    lax.fori_loop(0, 8, table, 0)

    def screen(block, carry):
        row0 = pl.multiple_of(block * 8, 8)
        for b in both:

            def raw(f, b=b):
                return sf_ref[b, pl.ds(f * 32 + row0, 8), :]

            view = view_ref[b, pl.ds(row0, 8), :]
            cam = pick_camera(cam_ref, b, view)
            feats = list(
                screen_terms([raw(f) for f in range(3)], [raw(f) for f in range(3, 10)], cam)
            ) + [raw(10)]
            for channel in range(3):
                shade = raw(11 + channel)
                for view_no in range(1, VIEWS):
                    shade = jnp.where(view == view_no, raw(11 + 3 * view_no + channel), shade)
                feats.append(shade)
            for f in range(4):
                tab_ref[b, pl.ds(row0 * 4 + f, 8, stride=4), :] = feats[f]
                tab_ref[b, pl.ds(128 + row0 * 4 + f, 8, stride=4), :] = feats[4 + f]
            tab_ref[b, pl.ds(256 + row0, 8), :] = feats[8]
        return carry

    lax.fori_loop(0, 4, screen, 0)
    for b in both:
        hi, mid = split2(tab_ref[b, 128:288, :])
        two_ref[b, :, 0:128] = hi.astype(BF16)
        two_ref[b, :, 128:256] = mid.astype(BF16)

    def group(group_no, carry):
        longest = jnp.int32(0)
        centre = []
        lengths = []
        unit0 = group_no * 16
        for b in both:
            longest = jnp.maximum(longest, len_ref[b, order_ref[b, group_no * 8]])
            row = tile_ref[b, pl.ds(pl.multiple_of(group_no * 8, 8), 8), :]
            cx, cy, length = [jnp.broadcast_to(row[n : n + 1], (8, 128)) for n in range(3)]
            centre.append((cx, cy))
            lengths.append(length)
        chunks = lax.div(longest + 31, 32)

        def gather(step, carry):
            for b, i in [(b, step * 2 + n) for n in range(2) for b in both]:
                units = [ix_ref[b, pl.ds(unit0 + i * 2 + n, 1), :] for n in range(2)]
                index = jnp.concatenate(units, axis=1)
                one = jnp.where(row_low == (index & 127), 1.0, 0.0).astype(BF16)
                got = dot(two_ref[b], jnp.concatenate([one, one], axis=0), NN)
                for n in range(2):
                    lanes = slice(n * 128, n * 128 + 128)
                    unit = jnp.broadcast_to(units[n], (8, 128))
                    low = unit & 127
                    high = unit >> 7
                    odd = (high & 1) == 1
                    exact = zero8
                    near = zero8
                    last = zero8
                    for h in range(16):
                        rows = slice(h * 8, h * 8 + 8)
                        hit = (high >> 1) == h
                        exact = jnp.where(hit, take_lanes(tab_ref[b, rows, :], low), exact)
                        near = jnp.where(hit, got[rows, lanes], near)
                    for h in range(4):
                        rows = slice(128 + h * 8, 136 + h * 8)
                        last = jnp.where((high >> 3) == h, got[rows, lanes], last)
                    last = jnp.sum(
                        jnp.where(sub == (high & 7), last, 0.0), axis=0, keepdims=True
                    )
                    feats = jnp.where(
                        sub < 4,
                        jnp.where(odd, pltpu.roll(exact, 4, 0), exact),
                        jnp.where(odd, near, pltpu.roll(near, 4, 0)),
                    )
                    j = i * 2 + n
                    fr_ref[b, pl.ds(j, 8, stride=16), :] = feats
                    fr_ref[b, pl.ds(128 + j, 1), :] = last
            return carry

        lax.fori_loop(0, lax.div(chunks + 1, 2), gather, 0)

        for b in both:
            cx, cy = centre[b]
            for part in range(2):
                c0 = part * 8

                def got(f, b=b, c0=c0):
                    return fr_ref[b, f * 16 + c0 : f * 16 + c0 + 8, :]

                u = got(0) - cx
                v = got(1) - cy
                con_a, con_b, con_c = [got(f) for f in range(2, 5)]
                fr_ref[b, c0 : c0 + 8, :] = u
                fr_ref[b, 16 + c0 : 16 + c0 + 8, :] = v
                live = (lane_k + (sub + c0) * 16).astype(F32) < lengths[b]
                coefs = [
                    con_a * (-0.5 * LOG2_E),
                    con_b * -LOG2_E,
                    con_c * (-0.5 * LOG2_E),
                    (con_a * u + con_b * v) * LOG2_E,
                    (con_b * u + con_c * v) * LOG2_E,
                    jnp.where(
                        live,
                        (got(5) - 0.5 * (con_a * u * u + con_c * v * v) - con_b * u * v) * LOG2_E,
                        -1e30,
                    ),
                ]
                for f, value in enumerate(coefs):
                    hi, rest = split2(value)
                    mid, lo = split2(rest)
                    for p, piece in enumerate((hi, mid, lo)):
                        co_ref[b, pl.ds(c0 * 32 + p * 8 + f, 8, stride=32), :] = piece
                for channel, shade in enumerate((got(6), got(7), got(8))):
                    hi, lo = split2(shade)
                    cc_ref[b, pl.ds(c0 * 8 + channel, 8, stride=8), :] = hi
                    cc_ref[b, pl.ds(c0 * 8 + 3 + channel, 8, stride=8), :] = lo

        def colours_of(b, i):
            rows = cc_ref[b, pl.ds(pl.multiple_of(i * 16, 16), 16), :]
            return jnp.concatenate(
                [
                    jnp.concatenate(
                        [jnp.where(diag, rows[n * 8 + r : n * 8 + r + 1], 0.0) for r in range(6)],
                        axis=0,
                    )
                    for n in range(2)
                ],
                axis=1,
            ).astype(BF16)

        def fade(b, i):
            row0 = pl.multiple_of(i * 256, 256)
            pair = co_ref[b, pl.ds(pl.multiple_of(i * 64, 64), 64), :].astype(BF16)
            lhs = jnp.concatenate([pair[0:32], pair[32:64]], axis=1)
            al_ref[b, pl.ds(row0, 256), :] = jnp.exp2(dot(lhs, basis_b, TN))

        def weigh(b, i, through):
            row0 = pl.multiple_of(i * 256, 256)
            alphas = al_ref[b, pl.ds(row0, 256), :]
            weights = []
            for k in range(32):
                weight = through * alphas[k * 8 : k * 8 + 8]
                through = through - weight
                weights.append(weight)
            weight = jnp.concatenate(weights, axis=0)
            w_hi, w_lo = split2(weight)
            w_ref[b, pl.ds(row0, 256), :] = weight
            ww_ref[b, pl.ds(row0, 256), 0:256] = w_hi.astype(BF16)
            ww_ref[b, pl.ds(row0, 256), 256:512] = w_lo.astype(BF16)
            return through

        def shade(b, i, colour):
            row0 = pl.multiple_of(i * 256, 256)
            c_two = colours_of(b, i)
            prod = dot(c_two, ww_ref[b, pl.ds(row0, 256), 0:256], NN)
            prod_lo = dot(c_two, ww_ref[b, pl.ds(row0, 256), 256:512], NN)
            return colour + prod[0:24] + prod[24:48] + prod_lo[0:24] + prod_lo[24:48]

        def forward(i, carry):
            carry = list(carry)
            colours = [shade(b, i - 1, carry[b][1]) for b in both]
            through = [weigh(b, i, carry[b][0]) for b in both]
            for b in both:
                fade(b, i + 1)
            return tuple((through[b], colours[b]) for b in both)

        for b in both:
            fade(b, 0)
        start = [weigh(b, 0, jnp.ones((8, 256), F32)) for b in both]
        for b in both:
            fade(b, 1)
        dark = jnp.zeros((24, 256), F32)
        done = lax.fori_loop(1, chunks, forward, tuple((start[b], dark) for b in both))
        done = [(None, shade(b, chunks - 1, done[b][1])) for b in both]
        r_four = []
        for b in both:
            resid = done[b][1] - aim_ref[b, pl.ds(pl.multiple_of(group_no * 24, 8), 24), :]
            err_ref[b] += resid * resid
            r_hi, r_lo = split2(2.0 * resid)
            r_four.append(jnp.concatenate([r_hi, r_hi, r_lo, r_lo], axis=0).astype(BF16))
            r_t = jnp.transpose(
                jnp.concatenate(
                    [jnp.zeros((8, 256), F32), r_hi, r_lo, jnp.zeros((72, 256), F32)], axis=0
                )
            ).astype(BF16)
            rt_ref[b, 512:768, :] = r_t
            rt_ref[b, 768:1024, :] = r_t

        def pull(b, i):
            c_two = colours_of(b, i)
            pl_ref[b] = dot(jnp.concatenate([c_two, c_two], axis=0), r_four[b], TN)

        def slope(b, i, behind):
            row0 = pl.multiple_of(i * 256, 256)
            pulls = pl_ref[b]
            alphas = al_ref[b, pl.ds(row0, 256), :]
            weight = w_ref[b, pl.ds(row0, 256), :]
            parts = []
            for k in range(31, -1, -1):
                diff = pulls[k * 8 : k * 8 + 8] - behind
                parts.append(weight[k * 8 : k * 8 + 8] * diff)
                behind = behind + alphas[k * 8 : k * 8 + 8] * diff
            d_hi, d_lo = split2(jnp.concatenate(parts[::-1], axis=0))
            dd_ref[b, :, 0:256] = d_hi.astype(BF16)
            dd_ref[b, :, 256:512] = d_lo.astype(BF16)
            return behind

        def collect(b, i):
            row0 = pl.multiple_of(i * 256, 256)
            lhs = jnp.concatenate([dd_ref[b], ww_ref[b, pl.ds(row0, 256), :]], axis=1)
            sums = jnp.where(own, dot(lhs, rt_ref[b], NN), 0.0)
            for n in range(2):
                flip = jnp.transpose(sums[n * 128 : n * 128 + 128])
                j = i * 2 + n
                mo_ref[b, pl.ds(j, 8, stride=16), :] = flip[0:8]
                for h in range(3):
                    mo_ref[b, pl.ds((8 + h) * 16 + j, 1), :] = jnp.sum(
                        flip[8 + h * 8 : 16 + h * 8] + flip[32 + h * 8 : 40 + h * 8],
                        axis=0,
                        keepdims=True,
                    )

        def backward(step, carry):
            i = chunks - 1 - step
            for b in both:
                collect(b, i + 1)
            carry = tuple(slope(b, i, carry[b]) for b in both)
            for b in both:
                pull(b, jnp.maximum(i - 1, 0))
            return carry

        for b in both:
            pull(b, chunks - 1)
        start = tuple(slope(b, chunks - 1, jnp.zeros((8, 256), F32)) for b in both)
        for b in both:
            pull(b, jnp.maximum(chunks - 2, 0))
        lax.fori_loop(1, chunks, backward, start)
        for b in both:
            collect(b, 0)

        for b in both:
            for part in range(2):
                c0 = part * 8

                def moment(f, b=b, c0=c0):
                    return mo_ref[b, f * 16 + c0 : f * 16 + c0 + 8, :]

                u, v, con_a, con_b, con_c = [
                    fr_ref[b, f * 16 + c0 : f * 16 + c0 + 8, :] for f in range(5)
                ]
                m_xx, m_xy, m_yy, m_x, m_y, m_1 = [moment(f) for f in range(6)]
                s_x = m_x - u * m_1
                s_y = m_y - v * m_1
                grads = [
                    con_a * s_x + con_b * s_y,
                    con_b * s_x + con_c * s_y,
                    -0.5 * (m_xx - u * (m_x + s_x)),
                    -(m_xy - u * m_y - v * s_x),
                    -0.5 * (m_yy - v * (m_y + s_y)),
                    m_1,
                    moment(8),
                    moment(9),
                    moment(10),
                ]
                used = (sub + c0) < 2 * chunks
                for f, value in enumerate(grads):
                    hi, lo = split2(jnp.where(used, value, 0.0))
                    gr_ref[b, f * 16 + c0 : f * 16 + c0 + 8, :] = hi
                    gr_ref[b, 144 + f * 16 + c0 : 144 + f * 16 + c0 + 8, :] = lo

        def scatter(step, carry):
            for b in both:
                total = None
                for n in range(2):
                    j = step * 4 + n * 2
                    index = jnp.concatenate(
                        [ix_ref[b, pl.ds(unit0 + j + n, 1), :] for n in range(2)], axis=1
                    )
                    hit = row_a == (index >> 8)
                    rows = []
                    for f in range(18):
                        row = f * 16 + j
                        value = jnp.concatenate(
                            [gr_ref[b, pl.ds(row, 1), :], gr_ref[b, pl.ds(row + 1, 1), :]], axis=1
                        )
                        rows.append(jnp.where(hit, value, 0.0))
                    add = dot(jnp.concatenate(rows, axis=0).astype(BF16), scatter_rhs(index), NT)
                    add = add[0:144] + add[144:288]
                    total = add if total is None else total + add
                for half in range(2):
                    sg_ref[b, half, 0:144, :] += total[:, half * 128 : half * 128 + 128]
            return carry

        lax.fori_loop(0, lax.div(chunks + 1, 2), scatter, 0)
        return carry

    lax.fori_loop(0, GROUPS, group, 0)
    for b in both:
        total = jnp.sum(jnp.sum(err_ref[b], axis=0, keepdims=True), axis=1, keepdims=True)
        for half in range(2):
            sg_ref[b, half, 144:160, :] = view_ref[b, pl.ds(half, 16, stride=2), :]
            sg_ref[b, half, 240:256, :] = jnp.broadcast_to(total, (16, 128))

    for a in range(16):
        for half in range(2):
            parts = [
                sg_ref[b, half, pl.ds(q * 128 + a, 8, stride=16), :]
                for b in both
                for q in range(2)
            ]
            for r in range(4):
                out_ref[(a * 2 + half) * 4 + r] = by_quarter(
                    quarter, [turn(parts[q], q - r) for q in range(4)]
                )


def grads_kernel(
    cam_ref, params_ref, send_ref, grad_ref, out_ref, err_ref, flat_ref, res_ref, gg_ref, sems
):
    copies = fetch_params(params_ref, flat_ref, sems)
    row_a = lax.broadcasted_iota(jnp.int32, (16, 256), 0)
    quarter = lax.broadcasted_iota(jnp.int32, (8, 128), 1) >> 5
    gg_ref[...] = jnp.zeros(gg_ref.shape, F32)

    def place(chunk, total):
        tiles = [grad_ref[chunk * 8 + i] for i in range(8)]
        for tile in tiles:
            total = total + tile
        for batch_no in range(BATCHES):
            index = send_ref[batch_no, pl.ds(chunk, 1), :]
            hit = row_a == (index >> 8)
            rhs = scatter_rhs(index)
            high = []
            low = []
            for q in range(2):
                values = jnp.concatenate(
                    [
                        by_quarter(
                            quarter,
                            [turn(tiles[4 * n + i], i - 2 * batch_no - q) for i in range(4)],
                        )
                        for n in range(2)
                    ],
                    axis=1,
                )
                g_hi, g_lo = split2(values)
                for f in range(8 if q == 0 else 2):
                    high.append(jnp.where(hit, g_hi[f : f + 1], 0.0))
                    low.append(jnp.where(hit, g_lo[f : f + 1], 0.0))
            add = dot(jnp.concatenate(high + low, axis=0).astype(BF16), rhs, NT)
            gg_ref[batch_no] += add[0:160] + add[160:320]
        return total

    total = lax.fori_loop(0, 16, place, jnp.zeros((8, 128), F32))
    for copy in copies:
        copy.wait()

    def block(block_no, carry):
        row0 = pl.multiple_of((block_no // 2) * 8, 8)
        half = block_no % 2
        lane0 = pl.multiple_of(half * 128, 128)
        cols = [param_rows(flat_ref, row0, half, p) for p in range(PARAMS)]
        geo = [0.0] * 10
        opac = 0.0
        shade = [0.0] * 48
        for batch_no in range(BATCHES):

            def feat(f, batch_no=batch_no):
                return gg_ref[batch_no, pl.ds(f * 16 + row0, 8), pl.ds(lane0, 128)]

            cam = pick_camera(cam_ref, batch_no, feat(9))
            _, pull_geo = jax.vjp(
                lambda c: screen_terms(c[0:3], shape_terms(c), cam), cols[0:10]
            )
            (d_geo,) = pull_geo(tuple(feat(f) for f in range(5)))
            basis, pull_ray = jax.vjp(lambda c: ray_basis(c, cam), cols[0:3])
            d_col = [feat(6 + h) for h in range(3)]
            (d_ray,) = pull_ray(
                [
                    d_col[0] * cols[11 + k] + d_col[1] * cols[27 + k] + d_col[2] * cols[43 + k]
                    for k in range(16)
                ]
            )
            for i in range(10):
                geo[i] = geo[i] + d_geo[i]
            for i in range(3):
                geo[i] = geo[i] + d_ray[i]
            opac = opac + feat(5)
            for h in range(3):
                for k in range(16):
                    shade[16 * h + k] = shade[16 * h + k] + d_col[h] * basis[k]
        opac = opac / (1.0 + jnp.exp(cols[10]))
        for p, value in enumerate(geo + [opac] + shade):
            res_ref[pl.ds((2 * row0 + half) * PITCH + p, 8, stride=2 * PITCH), :] = value
        return carry

    lax.fori_loop(0, 4, block, 0)
    copies = [
        pltpu.make_async_copy(
            res_ref.at[pl.ds(j * PITCH, PARAMS), :],
            out_ref.at[:, pl.ds(j * 128, 128)],
            sems.at[j],
        )
        for j in range(32)
    ]
    for copy in copies:
        copy.start()
    lane = lax.broadcasted_iota(jnp.int32, (1, 128), 1)
    errors = jnp.sum(
        jnp.where((lane == 32) | (lane == 96), total[7:8], 0.0), axis=1, keepdims=True
    )
    err_ref[...] = errors * (1.0 / (BATCHES * OWNERS * TILES_DEV * 3 * TILE_PX))
    for copy in copies:
        copy.wait()


def exchange(values):
    return lax.all_to_all(values, "dev", split_axis=0, concat_axis=0, tiled=True)


SMEM = pl.BlockSpec(memory_space=pltpu.SMEM)
VMEM = pl.BlockSpec(memory_space=pltpu.VMEM)
HBM = pl.BlockSpec(memory_space=pl.ANY)
CALL = pltpu.CompilerParams(vmem_limit_bytes=VMEM_BYTES)


def local(params, cameras, send_lists, tile_slots, tile_ids, tile_len, targets):
    cams = camera_table(cameras)
    lengths = tile_len[:, 0]
    tile_no = jnp.arange(TILES_DEV, dtype=jnp.int32)
    ahead = (lengths[:, None, :] > lengths[:, :, None]) | (
        (lengths[:, None, :] == lengths[:, :, None]) & (tile_no[None, None, :] < tile_no[None, :, None])
    )
    rank = jnp.sum(ahead.astype(jnp.int32), axis=2)
    order = jnp.sum(
        jnp.where(rank[:, None, :] == tile_no[None, :, None], tile_no[None, None, :], 0), axis=2
    )
    send = send_lists[:, 0].reshape(BATCHES, 16, 256)

    feats = pl.pallas_call(
        offer_kernel,
        out_shape=jax.ShapeDtypeStruct((OWNERS, 16, 128), F32),
        in_specs=[SMEM, HBM, VMEM],
        out_specs=VMEM,
        scratch_shapes=[
            pltpu.VMEM((32 * PITCH, 128), F32),
            pltpu.VMEM((BATCHES, 768, 128), F32),
            pltpu.VMEM((BATCHES, 512, 256), BF16),
            pltpu.SemaphoreType.DMA((32,)),
        ],
        compiler_params=CALL,
        name="offer",
    )(cams, params, send)
    feats = exchange(feats)

    views, slots, tiles, aims = pl.pallas_call(
        plan_kernel,
        out_shape=(
            jax.ShapeDtypeStruct((BATCHES, 32, 128), F32),
            jax.ShapeDtypeStruct((BATCHES, GROUPS * 16, 128), jnp.int32),
            jax.ShapeDtypeStruct((BATCHES, GROUPS * 8, 128), F32),
            jax.ShapeDtypeStruct((BATCHES, GROUPS * 24, 256), F32),
        ),
        in_specs=[SMEM, SMEM, SMEM, VMEM, VMEM],
        out_specs=(VMEM, VMEM, VMEM, VMEM),
        scratch_shapes=[pltpu.VMEM((BATCHES, 8, 256), jnp.int32)],
        compiler_params=CALL,
        name="plan",
    )(order, tile_ids, lengths, tile_slots, targets)

    rows = TILES_DEV // GROUPS * PAIRS
    slot_grads = pl.pallas_call(
        blend_kernel,
        out_shape=jax.ShapeDtypeStruct((OWNERS, 8, 128), F32),
        in_specs=[SMEM, SMEM, SMEM, VMEM, VMEM, VMEM, VMEM, VMEM],
        out_specs=VMEM,
        scratch_shapes=[
            pltpu.VMEM((BATCHES, 768, 128), F32),
            pltpu.VMEM((BATCHES, 288, 128), F32),
            pltpu.VMEM((BATCHES, 160, 256), BF16),
            pltpu.VMEM((BATCHES, 144, 128), F32),
            pltpu.VMEM((BATCHES, 576, 128), F32),
            pltpu.VMEM((BATCHES, 128, 128), F32),
            pltpu.VMEM((BATCHES, rows + 256, 256), F32),
            pltpu.VMEM((BATCHES, rows, 256), F32),
            pltpu.VMEM((BATCHES, rows, 512), BF16),
            pltpu.VMEM((BATCHES, 256, 256), F32),
            pltpu.VMEM((BATCHES, 256, 512), BF16),
            pltpu.VMEM((BATCHES, 1024, 128), BF16),
            pltpu.VMEM((BATCHES, 176, 128), F32),
            pltpu.VMEM((BATCHES, 288, 128), F32),
            pltpu.VMEM((BATCHES, 2, 256, 128), F32),
            pltpu.VMEM((BATCHES, 24, 256), F32),
        ],
        compiler_params=CALL,
        name="blend",
    )(order, lengths, cams, feats, views, slots, tiles, aims)
    slot_grads = exchange(slot_grads)

    grads, err = pl.pallas_call(
        grads_kernel,
        out_shape=(
            jax.ShapeDtypeStruct((PARAMS, 4096), F32),
            jax.ShapeDtypeStruct((1, 1), F32),
        ),
        in_specs=[SMEM, HBM, VMEM, VMEM],
        out_specs=(HBM, VMEM),
        scratch_shapes=[
            pltpu.VMEM((32 * PITCH, 128), F32),
            pltpu.VMEM((32 * PITCH, 128), F32),
            pltpu.VMEM((BATCHES, 160, 256), F32),
            pltpu.SemaphoreType.DMA((32,)),
        ],
        compiler_params=CALL,
        name="param_grads",
    )(cams, params, send, slot_grads)
    return (grads, err[0, 0])


def solution(mesh):
    placed = (
        P(None, "dev"),
        P(),
        P(None, "dev", None, None),
        P(None, "dev", None),
        P(None, "dev"),
        P(None, "dev", None),
        P(None, "dev", None, None),
    )
    return jax.shard_map(
        local, mesh=mesh, in_specs=placed, out_specs=(P(None, "dev"), P()), check_vma=False
    )
```

```python
import jax
import jax.numpy as jnp
from jax import lax
from jax.experimental import pallas as pl
from jax.experimental.pallas import tpu as pltpu
from jax.sharding import PartitionSpec as P

BATCHES = 2
TILE = 16
PAIRS = 256
TILE_PX = 256
TILES_X = 240
TILES_VIEW = 32400
VIEWS = 4
PARAMS = 59
TILES_DEV = 32
OWNERS = 128
CAP = 32
SLOTS = 4096
GROUPS = 4
PITCH = 72
LOG2_E = 1.4426950408889634
VMEM_BYTES = 56 * 1024 * 1024

SH_ZERO = 0.28209479177387814
SH_ONE = 0.4886025119029199
SH_TWO = (
    1.0925484305920792,
    -1.0925484305920792,
    0.31539156525252005,
    -1.0925484305920792,
    0.5462742152960396,
)
SH_THREE = (
    -0.5900435899266435,
    2.890611442640554,
    -0.4570457994644658,
    0.3731763325901154,
    -0.4570457994644658,
    1.445305721320277,
    -0.5900435899266435,
)

F32 = jnp.float32
BF16 = jnp.bfloat16
NN = (((1,), (0,)), ((), ()))
NT = (((1,), (1,)), ((), ()))
TN = (((0,), (0,)), ((), ()))


def dot(lhs, rhs, dims):
    return lax.dot_general(lhs, rhs, dims, preferred_element_type=F32)


def split2(value):
    high = value.astype(BF16).astype(F32)
    return high, value - high


def camera_table(cameras):
    fields = [jnp.broadcast_to(cameras[:, n : n + 1], (8, 128)) for n in range(8)]
    cos_yaw = jnp.cos(fields[0])
    sin_yaw = jnp.sin(fields[0])
    cos_pitch = jnp.cos(fields[1])
    sin_pitch = jnp.sin(fields[1])
    frame = [
        cos_yaw,
        sin_yaw,
        sin_pitch * sin_yaw,
        cos_pitch,
        -sin_pitch * cos_yaw,
        -cos_pitch * sin_yaw,
        sin_pitch,
        cos_pitch * cos_yaw,
    ]
    shift = fields[2:5]
    centre = [
        -(frame[0] * shift[0] + frame[2] * shift[1] + frame[5] * shift[2]),
        -(frame[3] * shift[1] + frame[6] * shift[2]),
        -(frame[1] * shift[0] + frame[4] * shift[1] + frame[7] * shift[2]),
    ]
    return frame + shift + centre + fields[5:8]


CAM_ROWS = 17


def sh_basis(dir_x, dir_y, dir_z):
    square_x = dir_x * dir_x
    square_y = dir_y * dir_y
    square_z = dir_z * dir_z
    return [
        SH_ZERO * jnp.ones_like(dir_x),
        -SH_ONE * dir_y,
        SH_ONE * dir_z,
        -SH_ONE * dir_x,
        SH_TWO[0] * dir_x * dir_y,
        SH_TWO[1] * dir_y * dir_z,
        SH_TWO[2] * (2.0 * square_z - square_x - square_y),
        SH_TWO[3] * dir_x * dir_z,
        SH_TWO[4] * (square_x - square_y),
        SH_THREE[0] * dir_y * (3.0 * square_x - square_y),
        SH_THREE[1] * dir_x * dir_y * dir_z,
        SH_THREE[2] * dir_y * (4.0 * square_z - square_x - square_y),
        SH_THREE[3] * dir_z * (2.0 * square_z - 3.0 * square_x - 3.0 * square_y),
        SH_THREE[4] * dir_x * (4.0 * square_z - square_x - square_y),
        SH_THREE[5] * dir_z * (square_x - square_y),
        SH_THREE[6] * dir_x * (square_x - 3.0 * square_y),
    ]


def shape_terms(cols):
    inv_quat = 1.0 / jnp.sqrt(
        cols[6] * cols[6] + cols[7] * cols[7] + cols[8] * cols[8] + cols[9] * cols[9]
    )
    return [jnp.exp(cols[3 + i]) for i in range(3)] + [cols[6 + i] * inv_quat for i in range(4)]


def screen_terms(position, shape, cam):
    spread = shape[0:3]
    quat_w, quat_x, quat_y, quat_z = shape[3:7]
    frame = ((cam[0], None, cam[1]), (cam[2], cam[3], cam[4]), (cam[5], cam[6], cam[7]))
    shift = cam[8:11]
    focal = cam[14]
    viewed = [
        frame[0][0] * position[0] + frame[0][2] * position[2] + shift[0],
        frame[1][0] * position[0]
        + frame[1][1] * position[1]
        + frame[1][2] * position[2]
        + shift[1],
        frame[2][0] * position[0]
        + frame[2][1] * position[1]
        + frame[2][2] * position[2]
        + shift[2],
    ]
    inv_depth = 1.0 / viewed[2]
    screen_u = focal * viewed[0] * inv_depth + cam[15]
    screen_v = focal * viewed[1] * inv_depth + cam[16]
    rotation = (
        (
            1.0 - 2.0 * (quat_y * quat_y + quat_z * quat_z),
            2.0 * (quat_x * quat_y - quat_w * quat_z),
            2.0 * (quat_x * quat_z + quat_w * quat_y),
        ),
        (
            2.0 * (quat_x * quat_y + quat_w * quat_z),
            1.0 - 2.0 * (quat_x * quat_x + quat_z * quat_z),
            2.0 * (quat_y * quat_z - quat_w * quat_x),
        ),
        (
            2.0 * (quat_x * quat_z - quat_w * quat_y),
            2.0 * (quat_y * quat_z + quat_w * quat_x),
            1.0 - 2.0 * (quat_x * quat_x + quat_y * quat_y),
        ),
    )
    jac_main = focal * inv_depth
    jac_u = -jac_main * viewed[0] * inv_depth
    jac_v = -jac_main * viewed[1] * inv_depth
    row_u = [
        jac_main * frame[0][0] + jac_u * frame[2][0],
        jac_u * frame[2][1],
        jac_main * frame[0][2] + jac_u * frame[2][2],
    ]
    row_v = [jac_main * frame[1][i] + jac_v * frame[2][i] for i in range(3)]
    along_u = [
        (row_u[0] * rotation[0][j] + row_u[1] * rotation[1][j] + row_u[2] * rotation[2][j])
        * spread[j]
        for j in range(3)
    ]
    along_v = [
        (row_v[0] * rotation[0][j] + row_v[1] * rotation[1][j] + row_v[2] * rotation[2][j])
        * spread[j]
        for j in range(3)
    ]
    cov_uu = along_u[0] * along_u[0] + along_u[1] * along_u[1] + along_u[2] * along_u[2] + 0.3
    cov_uv = along_u[0] * along_v[0] + along_u[1] * along_v[1] + along_u[2] * along_v[2]
    cov_vv = along_v[0] * along_v[0] + along_v[1] * along_v[1] + along_v[2] * along_v[2] + 0.3
    inv_det = 1.0 / (cov_uu * cov_vv - cov_uv * cov_uv)
    return screen_u, screen_v, cov_vv * inv_det, -cov_uv * inv_det, cov_uu * inv_det


def ray_basis(position, cam):
    ray = [position[i] - cam[11 + i] for i in range(3)]
    inv_len = 1.0 / jnp.sqrt(ray[0] * ray[0] + ray[1] * ray[1] + ray[2] * ray[2])
    return sh_basis(ray[0] * inv_len, ray[1] * inv_len, ray[2] * inv_len)


def camera_field(cam_ref, field, batch_no, view_no):
    row = field * 8 + batch_no * VIEWS + view_no
    return jnp.broadcast_to(cam_ref[row : row + 1, :], (8, 128))


def pick_camera(cam_ref, batch_no, view):
    picked = []
    for field in range(CAM_ROWS):
        value = camera_field(cam_ref, field, batch_no, VIEWS - 1)
        for view_no in range(VIEWS - 2, -1, -1):
            value = jnp.where(
                view == view_no, camera_field(cam_ref, field, batch_no, view_no), value
            )
        picked.append(value)
    return picked


def take_lanes(table, index):
    return jnp.take_along_axis(table, index, axis=1, mode="promise_in_bounds")


def by_quarter(quarter, values):
    out = values[0]
    for q in range(1, len(values)):
        out = jnp.where(quarter == q, values[q], out)
    return out


def turn(value, quarters):
    quarters = quarters % 4
    return value if quarters == 0 else pltpu.roll(value, 32 * quarters, 1)


def scatter_rhs(index):
    row = lax.broadcasted_iota(jnp.int32, (256, index.shape[1]), 0)
    return jnp.where(row == (index & 255), 1.0, 0.0).astype(BF16)


def fetch_params(params_ref, flat_ref, sems):
    copies = [
        pltpu.make_async_copy(
            params_ref.at[:, pl.ds(j * 128, 128)],
            flat_ref.at[pl.ds(j * PITCH, PARAMS), :],
            sems.at[j],
        )
        for j in range(32)
    ]
    for copy in copies:
        copy.start()
    return copies


def param_rows(flat_ref, row0, half, param):
    return flat_ref[pl.ds((2 * row0 + half) * PITCH + param, 8, stride=2 * PITCH), :]


def offer_kernel(
    camera_ref, params_ref, list_ref, out_ref, cam_ref, send_ref, flat_ref, tab_ref, two_ref, sems
):
    copies = fetch_params(params_ref, flat_ref, sems)
    quarter = lax.broadcasted_iota(jnp.int32, (8, 128), 1) >> 5
    upper = lax.broadcasted_iota(jnp.int32, (8, 128), 0) < 4
    row_low = lax.broadcasted_iota(jnp.int32, (128, 256), 0)
    place = (lax.broadcasted_iota(jnp.int32, (8, 128), 0) & 3) == quarter
    cameras = jnp.concatenate([camera_ref[0], camera_ref[1]], axis=0)
    for field, value in enumerate(camera_table(cameras)):
        cam_ref[field * 8 : field * 8 + 8, :] = value
    for batch_no in range(BATCHES):
        for chunk in range(16):
            lists = list_ref[batch_no, 0, chunk * 8 : chunk * 8 + 8, :].astype(F32)
            lists = jnp.where(place, jnp.concatenate([lists] * 4, axis=1), 0.0)
            for half in range(2):
                line = jnp.sum(lists[half * 4 : half * 4 + 4], axis=0, keepdims=True)
                send_ref[batch_no, chunk : chunk + 1, half * 128 : half * 128 + 128] = line.astype(
                    jnp.int32
                )
    for copy in copies:
        copy.wait()

    def block(block_no, carry):
        row0 = (block_no // 2) * 8
        half = block_no % 2
        cols = [param_rows(flat_ref, row0, half, p) for p in range(PARAMS)]
        opac = -(jnp.maximum(-cols[10], 0.0) + jnp.log1p(jnp.exp(-jnp.abs(cols[10]))))
        shared = cols[0:3] + shape_terms(cols) + [opac]
        for batch_no in range(BATCHES):
            feats = list(shared)
            for view_no in range(VIEWS):
                cam = [
                    camera_field(cam_ref, field, batch_no, view_no) for field in range(CAM_ROWS)
                ]
                basis = ray_basis(cols[0:3], cam)
                for channel in range(3):
                    shade = 0.5
                    for term in range(16):
                        shade = shade + basis[term] * cols[11 + 16 * channel + term]
                    feats.append(shade)
            feats.append(jnp.zeros((8, 128), F32))
            for f, value in enumerate(feats):
                start = (2 * row0 + half) * 24 + f
                tab_ref[batch_no, pl.ds(start, 8, stride=48), :] = value
        return carry

    lax.fori_loop(0, 4, block, 0)

    def pieces(step, carry):
        for batch_no in range(BATCHES):
            for n in range(8):
                h = step * 8 + n
                hi, mid = split2(tab_ref[batch_no, pl.ds(pl.multiple_of(h * 24 + 8, 8), 16), :])
                row = pl.multiple_of(h * 16, 16)
                two_ref[batch_no, pl.ds(row, 16), 0:128] = hi.astype(BF16)
                two_ref[batch_no, pl.ds(row, 16), 128:256] = mid.astype(BF16)
        return carry

    lax.fori_loop(0, 4, pieces, 0)

    def pick(chunk, carry):
        cut = []
        for batch_no in range(BATCHES):
            index = send_ref[batch_no, pl.ds(chunk, 1), :]
            high = jnp.broadcast_to(index >> 7, (8, 256))
            low = jnp.broadcast_to(index & 127, (8, 256))
            one = jnp.where(row_low == (index & 127), 1.0, 0.0).astype(BF16)
            one = jnp.concatenate([one, one], axis=0)
            exact = [jnp.zeros((8, 128), F32)] * 2
            acc = [jnp.zeros((8, 256), F32)] * 2
            for part in range(4):
                got = dot(two_ref[batch_no, part * 128 : part * 128 + 128, :], one, NN)
                for n in range(8):
                    h = part * 8 + n
                    hit = high == h
                    for q in range(2):
                        row = n * 16 + q * 8
                        acc[q] = jnp.where(hit, got[row : row + 8], acc[q])
                    rows = tab_ref[batch_no, h * 24 : h * 24 + 8, :]
                    for half in range(2):
                        lanes = slice(half * 128, half * 128 + 128)
                        exact[half] = jnp.where(
                            hit[:, lanes], take_lanes(rows, low[:, lanes]), exact[half]
                        )
            cut.append((exact, [[a[:, 0:128], a[:, 128:256]] for a in acc]))
        for half in range(2):
            heads = [cut[0][0][half], cut[0][1][0][half], cut[0][1][1][half], cut[1][0][half]]
            tails = [cut[1][1][q][half] for q in range(2)]
            folded = [pltpu.roll(tail, 4, 0) for tail in tails]
            main = []
            tail = []
            for r in range(4):
                main.append(by_quarter(quarter, [turn(heads[q], q - r) for q in range(4)]))
                tail.append(
                    by_quarter(
                        quarter,
                        [
                            turn(tails[0], -r),
                            turn(folded[0], 1 - r),
                            turn(tails[1], 2 - r),
                            turn(folded[1], 3 - r),
                        ],
                    )
                )
            for r in range(0, 4, 2):
                row0 = pl.multiple_of((chunk * 2 + half) * 48 + r * 12, 8)
                middle = pltpu.roll(main[r + 1], 4, 0)
                out_ref[pl.ds(row0, 8), :] = main[r]
                out_ref[pl.ds(row0 + 8, 8), :] = jnp.where(upper, tail[r], middle)
                out_ref[pl.ds(row0 + 16, 8), :] = jnp.where(
                    upper, middle, pltpu.roll(tail[r + 1], 4, 0)
                )
        return carry

    lax.fori_loop(0, 16, pick, 0)


def plan_kernel(
    order_ref, ids_ref, len_ref, slots_ref, target_ref,
    out_ref, ix_ref, tile_ref, aim_ref, sl_ref,
):
    lane = lax.broadcasted_iota(jnp.int32, (8, 128), 1)
    sub = lax.broadcasted_iota(jnp.int32, (8, 128), 0)
    diag = sub == (lane & 7)

    def group(group_no, carry):
        for b in range(BATCHES):
            cx = jnp.zeros((1, 128), F32)
            cy = jnp.zeros((1, 128), F32)
            length = jnp.zeros((1, 128), F32)
            for t in range(8):
                tile = order_ref[b, group_no * 8 + t]
                in_view = lax.rem(ids_ref[b, tile], TILES_VIEW)
                row_t = lax.div(in_view, TILES_X)
                col_t = in_view - row_t * TILES_X
                here = (lane[0:1] & 7) == t
                cx = jnp.where(here, (col_t * TILE + 8).astype(F32), cx)
                cy = jnp.where(here, (row_t * TILE + 8).astype(F32), cy)
                length = jnp.where(here, len_ref[b, tile].astype(F32), length)
                sl_ref[b, t : t + 1, :] = slots_ref[b, pl.ds(tile, 1), :]
                for channel in range(3):
                    aim_ref[b, pl.ds(group_no * 24 + channel * 8 + t, 1), :] = target_ref[
                        b, pl.ds(tile, 1), channel, :
                    ]
            tile_ref[b, pl.ds(pl.multiple_of(group_no * 8, 8), 8), :] = jnp.concatenate(
                [cx, cy, length, jnp.zeros((5, 128), F32)], axis=0
            )
            picks = []
            for j in range(16):
                half = (j // 8) * 128
                picked = take_lanes(sl_ref[b, :, half : half + 128], (lane >> 3) + (j % 8) * 16)
                picks.append(
                    jnp.sum(jnp.where(diag, picked.astype(F32), 0.0), axis=0, keepdims=True)
                )
            ix_ref[b, pl.ds(pl.multiple_of(group_no * 16, 16), 16), :] = jnp.concatenate(
                picks, axis=0
            ).astype(jnp.int32)
        return carry

    lax.fori_loop(0, GROUPS, group, 0)
    row_high = lax.broadcasted_iota(jnp.int32, (32, PAIRS), 0)
    row_low = lax.broadcasted_iota(jnp.int32, (128, PAIRS), 0)

    def step(tile_no, sums):
        out = []
        for b in range(BATCHES):
            view = lax.div(ids_ref[b, tile_no], TILES_VIEW).astype(F32) * 0.5
            slots = slots_ref[b, pl.ds(tile_no, 1), :]
            lhs = jnp.where(row_high == (slots >> 7), view, 0.0).astype(BF16)
            rhs = jnp.where(row_low == (slots & 127), 1.0, 0.0).astype(BF16)
            out.append(sums[b] + dot(lhs, rhs, NT))
        return tuple(out)

    zero = jnp.zeros((32, 128), F32)
    sums = lax.fori_loop(0, TILES_DEV, step, (zero, zero))
    for b in range(BATCHES):
        out_ref[b] = sums[b]


def blend_kernel(
    order_ref, len_ref, cam_ref, feat_ref, view_ref, ix_ref, tile_ref, aim_ref, out_ref,
    sf_ref, tab_ref, two_ref, fr_ref, co_ref, cc_ref,
    al_ref, w_ref, ww_ref, pl_ref, dd_ref, rt_ref, mo_ref, gr_ref, sg_ref, err_ref,
):
    lane = lax.broadcasted_iota(jnp.int32, (8, 128), 1)
    sub = lax.broadcasted_iota(jnp.int32, (8, 128), 0)
    quarter = lane >> 5
    diag = sub == (lane & 7)
    lane_k = lane >> 3
    row_a = lax.broadcasted_iota(jnp.int32, (16, 256), 0)
    row_low = lax.broadcasted_iota(jnp.int32, (128, 256), 0)
    pix = lax.broadcasted_iota(jnp.int32, (8, 256), 1)
    term = lax.broadcasted_iota(jnp.int32, (8, 256), 0)
    px = (pix & 15).astype(F32) - 7.5
    py = (pix >> 4).astype(F32) - 7.5
    basis = jnp.where(
        term == 0, px * px,
        jnp.where(
            term == 1, px * py,
            jnp.where(
                term == 2, py * py,
                jnp.where(term == 3, px, jnp.where(term == 4, py, jnp.where(term == 5, 1.0, 0.0))),
            ),
        ),
    )
    basis_b = jnp.concatenate([basis] * 4, axis=0).astype(BF16)
    basis_t = jnp.transpose(
        jnp.concatenate([basis, jnp.zeros((120, 256), F32)], axis=0)
    ).astype(BF16)
    row_t = lax.broadcasted_iota(jnp.int32, (256, 128), 0) & 7
    lane_t = lax.broadcasted_iota(jnp.int32, (256, 128), 1)
    own = (lane_t < 8) | ((lane_t & 7) == row_t)
    zero8 = jnp.zeros((8, 128), F32)
    both = range(BATCHES)

    sg_ref[...] = jnp.zeros(sg_ref.shape, F32)
    co_ref[...] = jnp.zeros(co_ref.shape, F32)
    err_ref[...] = jnp.zeros(err_ref.shape, F32)
    for b in both:
        rt_ref[b, 0:256, :] = basis_t
        rt_ref[b, 256:512, :] = basis_t

    upper = sub < 4

    def table(step, carry):
        for n in range(4):
            high = step * 4 + n
            main = []
            tail = []
            for r in range(0, 4, 2):
                row0 = pl.multiple_of(high * 48 + r * 12, 8)
                tiles = [feat_ref[pl.ds(row0 + m * 8, 8), :] for m in range(3)]
                main.append(tiles[0])
                main.append(pltpu.roll(jnp.where(upper, tiles[2], tiles[1]), 4, 0))
                tail.append(tiles[1])
                tail.append(pltpu.roll(tiles[2], 4, 0))
            folded = [pltpu.roll(value, 4, 0) for value in tail]
            for q in range(4):
                sf_ref[q // 3, pl.ds((q % 3) * 256 + high, 8, stride=32), :] = by_quarter(
                    quarter, [turn(main[i], i - q) for i in range(4)]
                )
            for q in range(2):
                sf_ref[1, pl.ds((q + 1) * 256 + high, 8, stride=32), :] = by_quarter(
                    quarter,
                    [
                        jnp.where(
                            upper, turn(tail[i], i - 2 * q), turn(folded[i], i - 2 * q - 1)
                        )
                        for i in range(4)
                    ],
                )
        return carry

    lax.fori_loop(0, 8, table, 0)

    def screen(block, carry):
        row0 = pl.multiple_of(block * 8, 8)
        for b in both:

            def raw(f, b=b):
                return sf_ref[b, pl.ds(f * 32 + row0, 8), :]

            view = view_ref[b, pl.ds(row0, 8), :]
            cam = pick_camera(cam_ref, b, view)
            feats = list(
                screen_terms([raw(f) for f in range(3)], [raw(f) for f in range(3, 10)], cam)
            ) + [raw(10)]
            for channel in range(3):
                shade = raw(11 + channel)
                for view_no in range(1, VIEWS):
                    shade = jnp.where(view == view_no, raw(11 + 3 * view_no + channel), shade)
                feats.append(shade)
            for f in range(4):
                tab_ref[b, pl.ds(row0 * 4 + f, 8, stride=4), :] = feats[f]
                tab_ref[b, pl.ds(128 + row0 * 4 + f, 8, stride=4), :] = feats[4 + f]
            tab_ref[b, pl.ds(256 + row0, 8), :] = feats[8]
        return carry

    lax.fori_loop(0, 4, screen, 0)
    for b in both:
        hi, mid = split2(tab_ref[b, 128:288, :])
        two_ref[b, :, 0:128] = hi.astype(BF16)
        two_ref[b, :, 128:256] = mid.astype(BF16)

    def group(group_no, carry):
        longest = jnp.int32(0)
        centre = []
        lengths = []
        unit0 = group_no * 16
        for b in both:
            longest = jnp.maximum(longest, len_ref[b, order_ref[b, group_no * 8]])
            row = tile_ref[b, pl.ds(pl.multiple_of(group_no * 8, 8), 8), :]
            cx, cy, length = [jnp.broadcast_to(row[n : n + 1], (8, 128)) for n in range(3)]
            centre.append((cx, cy))
            lengths.append(length)
        chunks = lax.div(longest + 31, 32)

        def gather(step, carry):
            for b, i in [(b, step * 2 + n) for n in range(2) for b in both]:
                units = [ix_ref[b, pl.ds(unit0 + i * 2 + n, 1), :] for n in range(2)]
                index = jnp.concatenate(units, axis=1)
                one = jnp.where(row_low == (index & 127), 1.0, 0.0).astype(BF16)
                got = dot(two_ref[b], jnp.concatenate([one, one], axis=0), NN)
                for n in range(2):
                    lanes = slice(n * 128, n * 128 + 128)
                    unit = jnp.broadcast_to(units[n], (8, 128))
                    low = unit & 127
                    high = unit >> 7
                    odd = (high & 1) == 1
                    exact = zero8
                    near = zero8
                    last = zero8
                    for h in range(16):
                        rows = slice(h * 8, h * 8 + 8)
                        hit = (high >> 1) == h
                        exact = jnp.where(hit, take_lanes(tab_ref[b, rows, :], low), exact)
                        near = jnp.where(hit, got[rows, lanes], near)
                    for h in range(4):
                        rows = slice(128 + h * 8, 136 + h * 8)
                        last = jnp.where((high >> 3) == h, got[rows, lanes], last)
                    last = jnp.sum(
                        jnp.where(sub == (high & 7), last, 0.0), axis=0, keepdims=True
                    )
                    feats = jnp.where(
                        sub < 4,
                        jnp.where(odd, pltpu.roll(exact, 4, 0), exact),
                        jnp.where(odd, near, pltpu.roll(near, 4, 0)),
                    )
                    j = i * 2 + n
                    fr_ref[b, pl.ds(j, 8, stride=16), :] = feats
                    fr_ref[b, pl.ds(128 + j, 1), :] = last
            return carry

        lax.fori_loop(0, lax.div(chunks + 1, 2), gather, 0)

        for b in both:
            cx, cy = centre[b]
            for part in range(2):
                c0 = part * 8

                def got(f, b=b, c0=c0):
                    return fr_ref[b, f * 16 + c0 : f * 16 + c0 + 8, :]

                u = got(0) - cx
                v = got(1) - cy
                con_a, con_b, con_c = [got(f) for f in range(2, 5)]
                fr_ref[b, c0 : c0 + 8, :] = u
                fr_ref[b, 16 + c0 : 16 + c0 + 8, :] = v
                live = (lane_k + (sub + c0) * 16).astype(F32) < lengths[b]
                coefs = [
                    con_a * (-0.5 * LOG2_E),
                    con_b * -LOG2_E,
                    con_c * (-0.5 * LOG2_E),
                    (con_a * u + con_b * v) * LOG2_E,
                    (con_b * u + con_c * v) * LOG2_E,
                    jnp.where(
                        live,
                        (got(5) - 0.5 * (con_a * u * u + con_c * v * v) - con_b * u * v) * LOG2_E,
                        -1e30,
                    ),
                ]
                for f, value in enumerate(coefs):
                    hi, rest = split2(value)
                    mid, lo = split2(rest)
                    for p, piece in enumerate((hi, mid, lo)):
                        co_ref[b, pl.ds(c0 * 32 + p * 8 + f, 8, stride=32), :] = piece
                for channel, shade in enumerate((got(6), got(7), got(8))):
                    hi, lo = split2(shade)
                    cc_ref[b, pl.ds(c0 * 8 + channel, 8, stride=8), :] = hi
                    cc_ref[b, pl.ds(c0 * 8 + 3 + channel, 8, stride=8), :] = lo

        def colours_of(b, i):
            rows = cc_ref[b, pl.ds(pl.multiple_of(i * 16, 16), 16), :]
            return jnp.concatenate(
                [
                    jnp.concatenate(
                        [jnp.where(diag, rows[n * 8 + r : n * 8 + r + 1], 0.0) for r in range(6)],
                        axis=0,
                    )
                    for n in range(2)
                ],
                axis=1,
            ).astype(BF16)

        def fade(b, i):
            row0 = pl.multiple_of(i * 256, 256)
            pair = co_ref[b, pl.ds(pl.multiple_of(i * 64, 64), 64), :].astype(BF16)
            lhs = jnp.concatenate([pair[0:32], pair[32:64]], axis=1)
            al_ref[b, pl.ds(row0, 256), :] = jnp.exp2(dot(lhs, basis_b, TN))

        def weigh(b, i, through):
            row0 = pl.multiple_of(i * 256, 256)
            alphas = al_ref[b, pl.ds(row0, 256), :]
            weights = []
            for k in range(32):
                weight = through * alphas[k * 8 : k * 8 + 8]
                through = through - weight
                weights.append(weight)
            weight = jnp.concatenate(weights, axis=0)
            w_hi, w_lo = split2(weight)
            w_ref[b, pl.ds(row0, 256), :] = weight
            ww_ref[b, pl.ds(row0, 256), 0:256] = w_hi.astype(BF16)
            ww_ref[b, pl.ds(row0, 256), 256:512] = w_lo.astype(BF16)
            return through

        def shade(b, i, colour):
            row0 = pl.multiple_of(i * 256, 256)
            c_two = colours_of(b, i)
            prod = dot(c_two, ww_ref[b, pl.ds(row0, 256), 0:256], NN)
            prod_lo = dot(c_two, ww_ref[b, pl.ds(row0, 256), 256:512], NN)
            return colour + prod[0:24] + prod[24:48] + prod_lo[0:24] + prod_lo[24:48]

        def forward(i, carry):
            carry = list(carry)
            colours = [shade(b, i - 1, carry[b][1]) for b in both]
            through = [weigh(b, i, carry[b][0]) for b in both]
            for b in both:
                fade(b, i + 1)
            return tuple((through[b], colours[b]) for b in both)

        for b in both:
            fade(b, 0)
        start = [weigh(b, 0, jnp.ones((8, 256), F32)) for b in both]
        for b in both:
            fade(b, 1)
        dark = jnp.zeros((24, 256), F32)
        done = lax.fori_loop(1, chunks, forward, tuple((start[b], dark) for b in both))
        done = [(None, shade(b, chunks - 1, done[b][1])) for b in both]
        r_four = []
        for b in both:
            resid = done[b][1] - aim_ref[b, pl.ds(pl.multiple_of(group_no * 24, 8), 24), :]
            err_ref[b] += resid * resid
            r_hi, r_lo = split2(2.0 * resid)
            r_four.append(jnp.concatenate([r_hi, r_hi, r_lo, r_lo], axis=0).astype(BF16))
            r_t = jnp.transpose(
                jnp.concatenate(
                    [jnp.zeros((8, 256), F32), r_hi, r_lo, jnp.zeros((72, 256), F32)], axis=0
                )
            ).astype(BF16)
            rt_ref[b, 512:768, :] = r_t
            rt_ref[b, 768:1024, :] = r_t

        def pull(b, i):
            c_two = colours_of(b, i)
            pl_ref[b] = dot(jnp.concatenate([c_two, c_two], axis=0), r_four[b], TN)

        def slope(b, i, behind):
            row0 = pl.multiple_of(i * 256, 256)
            pulls = pl_ref[b]
            alphas = al_ref[b, pl.ds(row0, 256), :]
            weight = w_ref[b, pl.ds(row0, 256), :]
            parts = []
            for k in range(31, -1, -1):
                diff = pulls[k * 8 : k * 8 + 8] - behind
                parts.append(weight[k * 8 : k * 8 + 8] * diff)
                behind = behind + alphas[k * 8 : k * 8 + 8] * diff
            d_hi, d_lo = split2(jnp.concatenate(parts[::-1], axis=0))
            dd_ref[b, :, 0:256] = d_hi.astype(BF16)
            dd_ref[b, :, 256:512] = d_lo.astype(BF16)
            return behind

        def collect(b, i):
            row0 = pl.multiple_of(i * 256, 256)
            lhs = jnp.concatenate([dd_ref[b], ww_ref[b, pl.ds(row0, 256), :]], axis=1)
            sums = jnp.where(own, dot(lhs, rt_ref[b], NN), 0.0)
            for n in range(2):
                flip = jnp.transpose(sums[n * 128 : n * 128 + 128])
                j = i * 2 + n
                mo_ref[b, pl.ds(j, 8, stride=16), :] = flip[0:8]
                for h in range(3):
                    mo_ref[b, pl.ds((8 + h) * 16 + j, 1), :] = jnp.sum(
                        flip[8 + h * 8 : 16 + h * 8] + flip[32 + h * 8 : 40 + h * 8],
                        axis=0,
                        keepdims=True,
                    )

        def backward(step, carry):
            i = chunks - 1 - step
            for b in both:
                collect(b, i + 1)
            carry = tuple(slope(b, i, carry[b]) for b in both)
            for b in both:
                pull(b, jnp.maximum(i - 1, 0))
            return carry

        for b in both:
            pull(b, chunks - 1)
        start = tuple(slope(b, chunks - 1, jnp.zeros((8, 256), F32)) for b in both)
        for b in both:
            pull(b, jnp.maximum(chunks - 2, 0))
        lax.fori_loop(1, chunks, backward, start)
        for b in both:
            collect(b, 0)

        for b in both:
            for part in range(2):
                c0 = part * 8

                def moment(f, b=b, c0=c0):
                    return mo_ref[b, f * 16 + c0 : f * 16 + c0 + 8, :]

                u, v, con_a, con_b, con_c = [
                    fr_ref[b, f * 16 + c0 : f * 16 + c0 + 8, :] for f in range(5)
                ]
                m_xx, m_xy, m_yy, m_x, m_y, m_1 = [moment(f) for f in range(6)]
                s_x = m_x - u * m_1
                s_y = m_y - v * m_1
                grads = [
                    con_a * s_x + con_b * s_y,
                    con_b * s_x + con_c * s_y,
                    -0.5 * (m_xx - u * (m_x + s_x)),
                    -(m_xy - u * m_y - v * s_x),
                    -0.5 * (m_yy - v * (m_y + s_y)),
                    m_1,
                    moment(8),
                    moment(9),
                    moment(10),
                ]
                used = (sub + c0) < 2 * chunks
                for f, value in enumerate(grads):
                    hi, lo = split2(jnp.where(used, value, 0.0))
                    gr_ref[b, f * 16 + c0 : f * 16 + c0 + 8, :] = hi
                    gr_ref[b, 144 + f * 16 + c0 : 144 + f * 16 + c0 + 8, :] = lo

        def scatter(step, carry):
            for b in both:
                total = None
                for n in range(2):
                    j = step * 4 + n * 2
                    index = jnp.concatenate(
                        [ix_ref[b, pl.ds(unit0 + j + n, 1), :] for n in range(2)], axis=1
                    )
                    hit = row_a == (index >> 8)
                    rows = []
                    for f in range(18):
                        row = f * 16 + j
                        value = jnp.concatenate(
                            [gr_ref[b, pl.ds(row, 1), :], gr_ref[b, pl.ds(row + 1, 1), :]], axis=1
                        )
                        rows.append(jnp.where(hit, value, 0.0))
                    add = dot(jnp.concatenate(rows, axis=0).astype(BF16), scatter_rhs(index), NT)
                    add = add[0:144] + add[144:288]
                    total = add if total is None else total + add
                for half in range(2):
                    sg_ref[b, half, 0:144, :] += total[:, half * 128 : half * 128 + 128]
            return carry

        lax.fori_loop(0, lax.div(chunks + 1, 2), scatter, 0)
        return carry

    lax.fori_loop(0, GROUPS, group, 0)
    for b in both:
        total = jnp.sum(jnp.sum(err_ref[b], axis=0, keepdims=True), axis=1, keepdims=True)
        for half in range(2):
            sg_ref[b, half, 144:160, :] = view_ref[b, pl.ds(half, 16, stride=2), :]
            sg_ref[b, half, 240:256, :] = jnp.broadcast_to(total, (16, 128))

    for a in range(16):
        for half in range(2):
            parts = [
                sg_ref[b, half, pl.ds(q * 128 + a, 8, stride=16), :]
                for b in both
                for q in range(2)
            ]
            for r in range(4):
                out_ref[(a * 2 + half) * 4 + r] = by_quarter(
                    quarter, [turn(parts[q], q - r) for q in range(4)]
                )


def grads_kernel(
    cam_ref, params_ref, send_ref, grad_ref, out_ref, err_ref, flat_ref, res_ref, gg_ref, sems
):
    copies = fetch_params(params_ref, flat_ref, sems)
    row_a = lax.broadcasted_iota(jnp.int32, (16, 256), 0)
    quarter = lax.broadcasted_iota(jnp.int32, (8, 128), 1) >> 5
    gg_ref[...] = jnp.zeros(gg_ref.shape, F32)

    def place(step, total):
        tiles_of = [[grad_ref[step * 16 + n * 8 + i] for i in range(8)] for n in range(2)]
        for tile in tiles_of[0] + tiles_of[1]:
            total = total + tile
        sums = [None] * BATCHES
        for part, batch_no in [(n, b) for n in range(2) for b in range(BATCHES)]:
            tiles = tiles_of[part]
            index = send_ref[batch_no, pl.ds(step * 2 + part, 1), :]
            hit = row_a == (index >> 8)
            rhs = scatter_rhs(index)
            high = []
            low = []
            for q in range(2):
                values = jnp.concatenate(
                    [
                        by_quarter(
                            quarter,
                            [turn(tiles[4 * n + i], i - 2 * batch_no - q) for i in range(4)],
                        )
                        for n in range(2)
                    ],
                    axis=1,
                )
                g_hi, g_lo = split2(values)
                for f in range(8 if q == 0 else 2):
                    high.append(jnp.where(hit, g_hi[f : f + 1], 0.0))
                    low.append(jnp.where(hit, g_lo[f : f + 1], 0.0))
            add = dot(jnp.concatenate(high + low, axis=0).astype(BF16), rhs, NT)
            add = add[0:160] + add[160:320]
            sums[batch_no] = add if part == 0 else sums[batch_no] + add
        for batch_no in range(BATCHES):
            gg_ref[batch_no] += sums[batch_no]
        return total

    total = lax.fori_loop(0, 8, place, jnp.zeros((8, 128), F32))
    for copy in copies:
        copy.wait()

    def block(block_no, carry):
        row0 = pl.multiple_of((block_no // 2) * 8, 8)
        half = block_no % 2
        lane0 = pl.multiple_of(half * 128, 128)
        cols = [param_rows(flat_ref, row0, half, p) for p in range(PARAMS)]
        geo = [0.0] * 10
        opac = 0.0
        shade = [0.0] * 48
        for batch_no in range(BATCHES):

            def feat(f, batch_no=batch_no):
                return gg_ref[batch_no, pl.ds(f * 16 + row0, 8), pl.ds(lane0, 128)]

            cam = pick_camera(cam_ref, batch_no, feat(9))
            _, pull_geo = jax.vjp(
                lambda c: screen_terms(c[0:3], shape_terms(c), cam), cols[0:10]
            )
            (d_geo,) = pull_geo(tuple(feat(f) for f in range(5)))
            basis, pull_ray = jax.vjp(lambda c: ray_basis(c, cam), cols[0:3])
            d_col = [feat(6 + h) for h in range(3)]
            (d_ray,) = pull_ray(
                [
                    d_col[0] * cols[11 + k] + d_col[1] * cols[27 + k] + d_col[2] * cols[43 + k]
                    for k in range(16)
                ]
            )
            for i in range(10):
                geo[i] = geo[i] + d_geo[i]
            for i in range(3):
                geo[i] = geo[i] + d_ray[i]
            opac = opac + feat(5)
            for h in range(3):
                for k in range(16):
                    shade[16 * h + k] = shade[16 * h + k] + d_col[h] * basis[k]
        opac = opac / (1.0 + jnp.exp(cols[10]))
        for p, value in enumerate(geo + [opac] + shade):
            res_ref[pl.ds((2 * row0 + half) * PITCH + p, 8, stride=2 * PITCH), :] = value
        return carry

    lax.fori_loop(0, 4, block, 0)
    copies = [
        pltpu.make_async_copy(
            res_ref.at[pl.ds(j * PITCH, PARAMS), :],
            out_ref.at[:, pl.ds(j * 128, 128)],
            sems.at[j],
        )
        for j in range(32)
    ]
    for copy in copies:
        copy.start()
    lane = lax.broadcasted_iota(jnp.int32, (1, 128), 1)
    errors = jnp.sum(
        jnp.where((lane == 32) | (lane == 96), total[7:8], 0.0), axis=1, keepdims=True
    )
    err_ref[...] = errors * (1.0 / (BATCHES * OWNERS * TILES_DEV * 3 * TILE_PX))
    for copy in copies:
        copy.wait()


def exchange(values):
    return lax.all_to_all(values, "dev", split_axis=0, concat_axis=0, tiled=True)


SMEM = pl.BlockSpec(memory_space=pltpu.SMEM)
VMEM = pl.BlockSpec(memory_space=pltpu.VMEM)
HBM = pl.BlockSpec(memory_space=pl.ANY)
CALL = pltpu.CompilerParams(vmem_limit_bytes=VMEM_BYTES)


def local(params, cameras, send_lists, tile_slots, tile_ids, tile_len, targets):
    lengths = tile_len[:, 0]
    tile_no = jnp.arange(TILES_DEV, dtype=jnp.int32)
    ahead = (lengths[:, None, :] > lengths[:, :, None]) | (
        (lengths[:, None, :] == lengths[:, :, None]) & (tile_no[None, None, :] < tile_no[None, :, None])
    )
    rank = jnp.sum(ahead.astype(jnp.int32), axis=2)
    order = jnp.sum(
        jnp.where(rank[:, None, :] == tile_no[None, :, None], tile_no[None, None, :], 0), axis=2
    )

    feats, cams, send = pl.pallas_call(
        offer_kernel,
        out_shape=(
            jax.ShapeDtypeStruct((OWNERS * 12, 128), F32),
            jax.ShapeDtypeStruct((CAM_ROWS * 8, 128), F32),
            jax.ShapeDtypeStruct((BATCHES, 16, 256), jnp.int32),
        ),
        in_specs=[VMEM, HBM, VMEM],
        out_specs=(VMEM, VMEM, VMEM),
        scratch_shapes=[
            pltpu.VMEM((32 * PITCH, 128), F32),
            pltpu.VMEM((BATCHES, 768, 128), F32),
            pltpu.VMEM((BATCHES, 512, 256), BF16),
            pltpu.SemaphoreType.DMA((32,)),
        ],
        compiler_params=CALL,
        name="offer",
    )(cameras, params, send_lists)
    feats = exchange(feats.reshape(OWNERS, 1, 1536)).reshape(OWNERS * 12, 128)

    views, slots, tiles, aims = pl.pallas_call(
        plan_kernel,
        out_shape=(
            jax.ShapeDtypeStruct((BATCHES, 32, 128), F32),
            jax.ShapeDtypeStruct((BATCHES, GROUPS * 16, 128), jnp.int32),
            jax.ShapeDtypeStruct((BATCHES, GROUPS * 8, 128), F32),
            jax.ShapeDtypeStruct((BATCHES, GROUPS * 24, 256), F32),
        ),
        in_specs=[SMEM, SMEM, SMEM, VMEM, VMEM],
        out_specs=(VMEM, VMEM, VMEM, VMEM),
        scratch_shapes=[pltpu.VMEM((BATCHES, 8, 256), jnp.int32)],
        compiler_params=CALL,
        name="plan",
    )(order, tile_ids, lengths, tile_slots, targets)

    rows = TILES_DEV // GROUPS * PAIRS
    slot_grads = pl.pallas_call(
        blend_kernel,
        out_shape=jax.ShapeDtypeStruct((OWNERS, 8, 128), F32),
        in_specs=[SMEM, SMEM, VMEM, VMEM, VMEM, VMEM, VMEM, VMEM],
        out_specs=VMEM,
        scratch_shapes=[
            pltpu.VMEM((BATCHES, 768, 128), F32),
            pltpu.VMEM((BATCHES, 288, 128), F32),
            pltpu.VMEM((BATCHES, 160, 256), BF16),
            pltpu.VMEM((BATCHES, 144, 128), F32),
            pltpu.VMEM((BATCHES, 576, 128), F32),
            pltpu.VMEM((BATCHES, 128, 128), F32),
            pltpu.VMEM((BATCHES, rows + 256, 256), F32),
            pltpu.VMEM((BATCHES, rows, 256), F32),
            pltpu.VMEM((BATCHES, rows, 512), BF16),
            pltpu.VMEM((BATCHES, 256, 256), F32),
            pltpu.VMEM((BATCHES, 256, 512), BF16),
            pltpu.VMEM((BATCHES, 1024, 128), BF16),
            pltpu.VMEM((BATCHES, 176, 128), F32),
            pltpu.VMEM((BATCHES, 288, 128), F32),
            pltpu.VMEM((BATCHES, 2, 256, 128), F32),
            pltpu.VMEM((BATCHES, 24, 256), F32),
        ],
        compiler_params=CALL,
        name="blend",
    )(order, lengths, cams, feats, views, slots, tiles, aims)
    slot_grads = exchange(slot_grads)

    grads, err = pl.pallas_call(
        grads_kernel,
        out_shape=(
            jax.ShapeDtypeStruct((PARAMS, 4096), F32),
            jax.ShapeDtypeStruct((1, 1), F32),
        ),
        in_specs=[VMEM, HBM, VMEM, VMEM],
        out_specs=(HBM, VMEM),
        scratch_shapes=[
            pltpu.VMEM((32 * PITCH, 128), F32),
            pltpu.VMEM((32 * PITCH, 128), F32),
            pltpu.VMEM((BATCHES, 160, 256), F32),
            pltpu.SemaphoreType.DMA((32,)),
        ],
        compiler_params=CALL,
        name="param_grads",
    )(cams, params, send, slot_grads)
    return (grads, err[0, 0])


def solution(mesh):
    placed = (
        P(None, "dev"),
        P(),
        P(None, "dev", None, None),
        P(None, "dev", None),
        P(None, "dev"),
        P(None, "dev", None),
        P(None, "dev", None, None),
    )
    return jax.shard_map(
        local, mesh=mesh, in_specs=placed, out_specs=(P(None, "dev"), P()), check_vma=False
    )
```

```python
import jax
import jax.numpy as jnp
from jax import lax
from jax.experimental import pallas as pl
from jax.experimental.pallas import tpu as pltpu
from jax.sharding import PartitionSpec as P

BATCHES = 2
TILE = 16
PAIRS = 256
TILE_PX = 256
TILES_X = 240
TILES_VIEW = 32400
VIEWS = 4
PARAMS = 59
TILES_DEV = 32
OWNERS = 128
CAP = 32
SLOTS = 4096
GROUPS = 4
PITCH = 72
LOG2_E = 1.4426950408889634

SH_ZERO = 0.28209479177387814
SH_ONE = 0.4886025119029199
SH_TWO = (
    1.0925484305920792,
    -1.0925484305920792,
    0.31539156525252005,
    -1.0925484305920792,
    0.5462742152960396,
)
SH_THREE = (
    -0.5900435899266435,
    2.890611442640554,
    -0.4570457994644658,
    0.3731763325901154,
    -0.4570457994644658,
    1.445305721320277,
    -0.5900435899266435,
)

F32 = jnp.float32
BF16 = jnp.bfloat16
NN = (((1,), (0,)), ((), ()))
NT = (((1,), (1,)), ((), ()))
TN = (((0,), (0,)), ((), ()))


def dot(lhs, rhs, dims):
    return lax.dot_general(lhs, rhs, dims, preferred_element_type=F32)


def split2(value):
    high = value.astype(BF16).astype(F32)
    return high, value - high


def camera_table(cameras):
    fields = [jnp.broadcast_to(cameras[:, n : n + 1], (8, 128)) for n in range(8)]
    cos_yaw = jnp.cos(fields[0])
    sin_yaw = jnp.sin(fields[0])
    cos_pitch = jnp.cos(fields[1])
    sin_pitch = jnp.sin(fields[1])
    frame = [
        cos_yaw,
        sin_yaw,
        sin_pitch * sin_yaw,
        cos_pitch,
        -sin_pitch * cos_yaw,
        -cos_pitch * sin_yaw,
        sin_pitch,
        cos_pitch * cos_yaw,
    ]
    shift = fields[2:5]
    centre = [
        -(frame[0] * shift[0] + frame[2] * shift[1] + frame[5] * shift[2]),
        -(frame[3] * shift[1] + frame[6] * shift[2]),
        -(frame[1] * shift[0] + frame[4] * shift[1] + frame[7] * shift[2]),
    ]
    return frame + shift + centre + fields[5:8]


CAM_ROWS = 17


def sh_basis(dir_x, dir_y, dir_z):
    square_x = dir_x * dir_x
    square_y = dir_y * dir_y
    square_z = dir_z * dir_z
    return [
        SH_ZERO * jnp.ones_like(dir_x),
        -SH_ONE * dir_y,
        SH_ONE * dir_z,
        -SH_ONE * dir_x,
        SH_TWO[0] * dir_x * dir_y,
        SH_TWO[1] * dir_y * dir_z,
        SH_TWO[2] * (2.0 * square_z - square_x - square_y),
        SH_TWO[3] * dir_x * dir_z,
        SH_TWO[4] * (square_x - square_y),
        SH_THREE[0] * dir_y * (3.0 * square_x - square_y),
        SH_THREE[1] * dir_x * dir_y * dir_z,
        SH_THREE[2] * dir_y * (4.0 * square_z - square_x - square_y),
        SH_THREE[3] * dir_z * (2.0 * square_z - 3.0 * square_x - 3.0 * square_y),
        SH_THREE[4] * dir_x * (4.0 * square_z - square_x - square_y),
        SH_THREE[5] * dir_z * (square_x - square_y),
        SH_THREE[6] * dir_x * (square_x - 3.0 * square_y),
    ]


def shape_terms(cols):
    inv_quat = 1.0 / jnp.sqrt(
        cols[6] * cols[6] + cols[7] * cols[7] + cols[8] * cols[8] + cols[9] * cols[9]
    )
    return [jnp.exp(cols[3 + i]) for i in range(3)] + [cols[6 + i] * inv_quat for i in range(4)]


def screen_terms(position, shape, cam):
    spread = shape[0:3]
    quat_w, quat_x, quat_y, quat_z = shape[3:7]
    frame = ((cam[0], None, cam[1]), (cam[2], cam[3], cam[4]), (cam[5], cam[6], cam[7]))
    shift = cam[8:11]
    focal = cam[14]
    viewed = [
        frame[0][0] * position[0] + frame[0][2] * position[2] + shift[0],
        frame[1][0] * position[0]
        + frame[1][1] * position[1]
        + frame[1][2] * position[2]
        + shift[1],
        frame[2][0] * position[0]
        + frame[2][1] * position[1]
        + frame[2][2] * position[2]
        + shift[2],
    ]
    inv_depth = 1.0 / viewed[2]
    screen_u = focal * viewed[0] * inv_depth + cam[15]
    screen_v = focal * viewed[1] * inv_depth + cam[16]
    rotation = (
        (
            1.0 - 2.0 * (quat_y * quat_y + quat_z * quat_z),
            2.0 * (quat_x * quat_y - quat_w * quat_z),
            2.0 * (quat_x * quat_z + quat_w * quat_y),
        ),
        (
            2.0 * (quat_x * quat_y + quat_w * quat_z),
            1.0 - 2.0 * (quat_x * quat_x + quat_z * quat_z),
            2.0 * (quat_y * quat_z - quat_w * quat_x),
        ),
        (
            2.0 * (quat_x * quat_z - quat_w * quat_y),
            2.0 * (quat_y * quat_z + quat_w * quat_x),
            1.0 - 2.0 * (quat_x * quat_x + quat_y * quat_y),
        ),
    )
    jac_main = focal * inv_depth
    jac_u = -jac_main * viewed[0] * inv_depth
    jac_v = -jac_main * viewed[1] * inv_depth
    row_u = [
        jac_main * frame[0][0] + jac_u * frame[2][0],
        jac_u * frame[2][1],
        jac_main * frame[0][2] + jac_u * frame[2][2],
    ]
    row_v = [jac_main * frame[1][i] + jac_v * frame[2][i] for i in range(3)]
    along_u = [
        (row_u[0] * rotation[0][j] + row_u[1] * rotation[1][j] + row_u[2] * rotation[2][j])
        * spread[j]
        for j in range(3)
    ]
    along_v = [
        (row_v[0] * rotation[0][j] + row_v[1] * rotation[1][j] + row_v[2] * rotation[2][j])
        * spread[j]
        for j in range(3)
    ]
    cov_uu = along_u[0] * along_u[0] + along_u[1] * along_u[1] + along_u[2] * along_u[2] + 0.3
    cov_uv = along_u[0] * along_v[0] + along_u[1] * along_v[1] + along_u[2] * along_v[2]
    cov_vv = along_v[0] * along_v[0] + along_v[1] * along_v[1] + along_v[2] * along_v[2] + 0.3
    inv_det = 1.0 / (cov_uu * cov_vv - cov_uv * cov_uv)
    return screen_u, screen_v, cov_vv * inv_det, -cov_uv * inv_det, cov_uu * inv_det


def ray_basis(position, cam):
    ray = [position[i] - cam[11 + i] for i in range(3)]
    inv_len = 1.0 / jnp.sqrt(ray[0] * ray[0] + ray[1] * ray[1] + ray[2] * ray[2])
    return sh_basis(ray[0] * inv_len, ray[1] * inv_len, ray[2] * inv_len)


def camera_field(cam_ref, field, batch_no, view_no):
    row = field * 8 + batch_no * VIEWS + view_no
    return jnp.broadcast_to(cam_ref[row : row + 1, :], (8, 128))


def pick_camera(cam_ref, batch_no, view):
    picked = []
    for field in range(CAM_ROWS):
        value = camera_field(cam_ref, field, batch_no, VIEWS - 1)
        for view_no in range(VIEWS - 2, -1, -1):
            value = jnp.where(
                view == view_no, camera_field(cam_ref, field, batch_no, view_no), value
            )
        picked.append(value)
    return picked


def take_lanes(table, index):
    return jnp.take_along_axis(table, index, axis=1, mode="promise_in_bounds")


def by_quarter(quarter, values):
    out = values[0]
    for q in range(1, len(values)):
        out = jnp.where(quarter == q, values[q], out)
    return out


def turn(value, quarters):
    quarters = quarters % 4
    return value if quarters == 0 else pltpu.roll(value, 32 * quarters, 1)


def scatter_rhs(index):
    row = lax.broadcasted_iota(jnp.int32, (256, index.shape[1]), 0)
    return jnp.where(row == (index & 255), 1.0, 0.0).astype(BF16)


def fetch_params(params_ref, flat_ref, sems):
    copies = [
        pltpu.make_async_copy(
            params_ref.at[:, pl.ds(j * 128, 128)],
            flat_ref.at[pl.ds(j * PITCH, PARAMS), :],
            sems.at[j],
        )
        for j in range(32)
    ]
    for copy in copies:
        copy.start()
    return copies


def param_rows(flat_ref, row0, half, param):
    return flat_ref[pl.ds((2 * row0 + half) * PITCH + param, 8, stride=2 * PITCH), :]


def offer_kernel(
    camera_ref, params_ref, list_ref, out_ref, cam_ref, send_ref, flat_ref, tab_ref, two_ref, sems
):
    copies = fetch_params(params_ref, flat_ref, sems)
    quarter = lax.broadcasted_iota(jnp.int32, (8, 128), 1) >> 5
    upper = lax.broadcasted_iota(jnp.int32, (8, 128), 0) < 4
    row_low = lax.broadcasted_iota(jnp.int32, (128, 256), 0)
    place = (lax.broadcasted_iota(jnp.int32, (8, 128), 0) & 3) == quarter
    cameras = jnp.concatenate([camera_ref[0], camera_ref[1]], axis=0)
    for field, value in enumerate(camera_table(cameras)):
        cam_ref[field * 8 : field * 8 + 8, :] = value
    for batch_no in range(BATCHES):
        by_owner = jnp.transpose(
            jnp.concatenate([list_ref[batch_no, 0].astype(F32)] * 4, axis=0)
        )
        for chunk in range(16):
            lists = jnp.where(place, by_owner[chunk * 8 : chunk * 8 + 8], 0.0)
            for half in range(2):
                line = jnp.sum(lists[half * 4 : half * 4 + 4], axis=0, keepdims=True)
                send_ref[batch_no, chunk : chunk + 1, half * 128 : half * 128 + 128] = line.astype(
                    jnp.int32
                )

    def block(block_no, carry):
        row0 = (block_no // 2) * 8
        half = block_no % 2
        cols = [param_rows(flat_ref, row0, half, p) for p in range(PARAMS)]
        opac = -(jnp.maximum(-cols[10], 0.0) + jnp.log1p(jnp.exp(-jnp.abs(cols[10]))))
        shared = cols[0:3] + shape_terms(cols) + [opac]
        for batch_no in range(BATCHES):
            feats = list(shared)
            for view_no in range(VIEWS):
                cam = [
                    camera_field(cam_ref, field, batch_no, view_no) for field in range(CAM_ROWS)
                ]
                basis = ray_basis(cols[0:3], cam)
                for channel in range(3):
                    shade = 0.5
                    for term in range(16):
                        shade = shade + basis[term] * cols[11 + 16 * channel + term]
                    feats.append(shade)
            feats.append(jnp.zeros((8, 128), F32))
            for f, value in enumerate(feats):
                start = (2 * row0 + half) * 24 + f
                tab_ref[batch_no, pl.ds(start, 8, stride=48), :] = value
        return carry

    for part in range(2):
        for copy in copies[part * 16 : part * 16 + 16]:
            copy.wait()
        lax.fori_loop(part * 2, part * 2 + 2, block, 0)

    def pieces(step, carry):
        for batch_no in range(BATCHES):
            for n in range(8):
                h = step * 8 + n
                hi, mid = split2(tab_ref[batch_no, pl.ds(pl.multiple_of(h * 24 + 8, 8), 16), :])
                row = pl.multiple_of(h * 16, 16)
                two_ref[batch_no, pl.ds(row, 16), 0:128] = hi.astype(BF16)
                two_ref[batch_no, pl.ds(row, 16), 128:256] = mid.astype(BF16)
        return carry

    lax.fori_loop(0, 4, pieces, 0)

    def pick(chunk, carry):
        cut = []
        for batch_no in range(BATCHES):
            index = send_ref[batch_no, pl.ds(chunk, 1), :]
            high = jnp.broadcast_to(index >> 7, (8, 256))
            low = jnp.broadcast_to(index & 127, (8, 256))
            one = jnp.where(row_low == (index & 127), 1.0, 0.0).astype(BF16)
            one = jnp.concatenate([one, one], axis=0)
            exact = [jnp.zeros((8, 128), F32)] * 2
            acc = [jnp.zeros((8, 256), F32)] * 2
            for part in range(4):
                got = dot(two_ref[batch_no, part * 128 : part * 128 + 128, :], one, NN)
                for n in range(8):
                    h = part * 8 + n
                    hit = high == h
                    for q in range(2):
                        row = n * 16 + q * 8
                        acc[q] = jnp.where(hit, got[row : row + 8], acc[q])
                    rows = tab_ref[batch_no, h * 24 : h * 24 + 8, :]
                    for half in range(2):
                        lanes = slice(half * 128, half * 128 + 128)
                        exact[half] = jnp.where(
                            hit[:, lanes], take_lanes(rows, low[:, lanes]), exact[half]
                        )
            cut.append((exact, [[a[:, 0:128], a[:, 128:256]] for a in acc]))
        for half in range(2):
            heads = [cut[0][0][half], cut[0][1][0][half], cut[0][1][1][half], cut[1][0][half]]
            tails = [cut[1][1][q][half] for q in range(2)]
            folded = [pltpu.roll(tail, 4, 0) for tail in tails]
            main = []
            tail = []
            for r in range(4):
                main.append(by_quarter(quarter, [turn(heads[q], q - r) for q in range(4)]))
                tail.append(
                    by_quarter(
                        quarter,
                        [
                            turn(tails[0], -r),
                            turn(folded[0], 1 - r),
                            turn(tails[1], 2 - r),
                            turn(folded[1], 3 - r),
                        ],
                    )
                )
            for r in range(0, 4, 2):
                row0 = pl.multiple_of((chunk * 2 + half) * 48 + r * 12, 8)
                middle = pltpu.roll(main[r + 1], 4, 0)
                out_ref[pl.ds(row0, 8), :] = main[r]
                out_ref[pl.ds(row0 + 8, 8), :] = jnp.where(upper, tail[r], middle)
                out_ref[pl.ds(row0 + 16, 8), :] = jnp.where(
                    upper, middle, pltpu.roll(tail[r + 1], 4, 0)
                )
        return carry

    lax.fori_loop(0, 16, pick, 0)


def plan_kernel(
    order_ref, ids_ref, len_ref, slots_ref, target_ref,
    out_ref, ix_ref, tile_ref, aim_ref, sl_ref,
):
    lane = lax.broadcasted_iota(jnp.int32, (8, 128), 1)
    sub = lax.broadcasted_iota(jnp.int32, (8, 128), 0)
    diag = sub == (lane & 7)

    def group(group_no, carry):
        for b in range(BATCHES):
            cx = jnp.zeros((1, 128), F32)
            cy = jnp.zeros((1, 128), F32)
            length = jnp.zeros((1, 128), F32)
            for t in range(8):
                tile = order_ref[b, group_no * 8 + t]
                in_view = lax.rem(ids_ref[b, tile], TILES_VIEW)
                row_t = lax.div(in_view, TILES_X)
                col_t = in_view - row_t * TILES_X
                here = (lane[0:1] & 7) == t
                cx = jnp.where(here, (col_t * TILE + 8).astype(F32), cx)
                cy = jnp.where(here, (row_t * TILE + 8).astype(F32), cy)
                length = jnp.where(here, len_ref[b, tile].astype(F32), length)
                sl_ref[b, t : t + 1, :] = slots_ref[b, pl.ds(tile, 1), :]
                for channel in range(3):
                    aim_ref[b, pl.ds(group_no * 24 + channel * 8 + t, 1), :] = target_ref[
                        b, pl.ds(tile, 1), channel, :
                    ]
            tile_ref[b, pl.ds(pl.multiple_of(group_no * 8, 8), 8), :] = jnp.concatenate(
                [cx, cy, length, jnp.zeros((5, 128), F32)], axis=0
            )
            picks = []
            for j in range(16):
                half = (j // 8) * 128
                picked = take_lanes(sl_ref[b, :, half : half + 128], (lane >> 3) + (j % 8) * 16)
                picks.append(
                    jnp.sum(jnp.where(diag, picked.astype(F32), 0.0), axis=0, keepdims=True)
                )
            ix_ref[b, pl.ds(pl.multiple_of(group_no * 16, 16), 16), :] = jnp.concatenate(
                picks, axis=0
            ).astype(jnp.int32)
        return carry

    lax.fori_loop(0, GROUPS, group, 0)
    row_high = lax.broadcasted_iota(jnp.int32, (32, PAIRS), 0)
    row_low = lax.broadcasted_iota(jnp.int32, (128, PAIRS), 0)

    def step(tile_no, sums):
        out = []
        for b in range(BATCHES):
            view = lax.div(ids_ref[b, tile_no], TILES_VIEW).astype(F32) * 0.5
            slots = slots_ref[b, pl.ds(tile_no, 1), :]
            lhs = jnp.where(row_high == (slots >> 7), view, 0.0).astype(BF16)
            rhs = jnp.where(row_low == (slots & 127), 1.0, 0.0).astype(BF16)
            out.append(sums[b] + dot(lhs, rhs, NT))
        return tuple(out)

    zero = jnp.zeros((32, 128), F32)
    sums = lax.fori_loop(0, TILES_DEV, step, (zero, zero))
    for b in range(BATCHES):
        out_ref[b] = sums[b]


def blend_kernel(
    order_ref, len_ref, cam_ref, feat_ref, view_ref, ix_ref, tile_ref, aim_ref, out_ref,
    sf_ref, tab_ref, two_ref, fr_ref, co_ref, cc_ref,
    al_ref, w_ref, ww_ref, pl_ref, dd_ref, rt_ref, mo_ref, gr_ref, sg_ref, err_ref,
):
    lane = lax.broadcasted_iota(jnp.int32, (8, 128), 1)
    sub = lax.broadcasted_iota(jnp.int32, (8, 128), 0)
    quarter = lane >> 5
    diag = sub == (lane & 7)
    lane_k = lane >> 3
    row_a = lax.broadcasted_iota(jnp.int32, (16, 256), 0)
    row_low = lax.broadcasted_iota(jnp.int32, (128, 256), 0)
    pix = lax.broadcasted_iota(jnp.int32, (8, 256), 1)
    term = lax.broadcasted_iota(jnp.int32, (8, 256), 0)
    px = (pix & 15).astype(F32) - 7.5
    py = (pix >> 4).astype(F32) - 7.5
    basis = jnp.where(
        term == 0, px * px,
        jnp.where(
            term == 1, px * py,
            jnp.where(
                term == 2, py * py,
                jnp.where(term == 3, px, jnp.where(term == 4, py, jnp.where(term == 5, 1.0, 0.0))),
            ),
        ),
    )
    basis_b = jnp.concatenate([basis] * 4, axis=0).astype(BF16)
    basis_t = jnp.transpose(
        jnp.concatenate([basis, jnp.zeros((120, 256), F32)], axis=0)
    ).astype(BF16)
    row_t = lax.broadcasted_iota(jnp.int32, (256, 128), 0) & 7
    lane_t = lax.broadcasted_iota(jnp.int32, (256, 128), 1)
    own = (lane_t < 8) | ((lane_t & 7) == row_t)
    zero8 = jnp.zeros((8, 128), F32)
    both = range(BATCHES)

    sg_ref[...] = jnp.zeros(sg_ref.shape, F32)
    co_ref[...] = jnp.zeros(co_ref.shape, F32)
    err_ref[...] = jnp.zeros(err_ref.shape, F32)
    for b in both:
        rt_ref[b, 0:256, :] = basis_t
        rt_ref[b, 256:512, :] = basis_t

    upper = sub < 4

    def table(step, carry):
        for n in range(4):
            high = step * 4 + n
            main = []
            tail = []
            for r in range(0, 4, 2):
                row0 = pl.multiple_of(high * 48 + r * 12, 8)
                tiles = [feat_ref[pl.ds(row0 + m * 8, 8), :] for m in range(3)]
                main.append(tiles[0])
                main.append(pltpu.roll(jnp.where(upper, tiles[2], tiles[1]), 4, 0))
                tail.append(tiles[1])
                tail.append(pltpu.roll(tiles[2], 4, 0))
            folded = [pltpu.roll(value, 4, 0) for value in tail]
            for q in range(4):
                sf_ref[q // 3, pl.ds((q % 3) * 256 + high, 8, stride=32), :] = by_quarter(
                    quarter, [turn(main[i], i - q) for i in range(4)]
                )
            for q in range(2):
                sf_ref[1, pl.ds((q + 1) * 256 + high, 8, stride=32), :] = by_quarter(
                    quarter,
                    [
                        jnp.where(
                            upper, turn(tail[i], i - 2 * q), turn(folded[i], i - 2 * q - 1)
                        )
                        for i in range(4)
                    ],
                )
        return carry

    lax.fori_loop(0, 8, table, 0)

    def screen(block, carry):
        row0 = pl.multiple_of(block * 8, 8)
        for b in both:

            def raw(f, b=b):
                return sf_ref[b, pl.ds(f * 32 + row0, 8), :]

            view = view_ref[b, pl.ds(row0, 8), :]
            cam = pick_camera(cam_ref, b, view)
            feats = list(
                screen_terms([raw(f) for f in range(3)], [raw(f) for f in range(3, 10)], cam)
            ) + [raw(10)]
            for channel in range(3):
                shade = raw(11 + channel)
                for view_no in range(1, VIEWS):
                    shade = jnp.where(view == view_no, raw(11 + 3 * view_no + channel), shade)
                feats.append(shade)
            for f in range(4):
                tab_ref[b, pl.ds(row0 * 4 + f, 8, stride=4), :] = feats[f]
                tab_ref[b, pl.ds(128 + row0 * 4 + f, 8, stride=4), :] = feats[4 + f]
            tab_ref[b, pl.ds(256 + row0, 8), :] = feats[8]
        return carry

    lax.fori_loop(0, 4, screen, 0)
    for b in both:
        hi, mid = split2(tab_ref[b, 128:288, :])
        two_ref[b, :, 0:128] = hi.astype(BF16)
        two_ref[b, :, 128:256] = mid.astype(BF16)

    def group(group_no, carry):
        longest = jnp.int32(0)
        centre = []
        lengths = []
        unit0 = group_no * 16
        for b in both:
            longest = jnp.maximum(longest, len_ref[b, order_ref[b, group_no * 8]])
            row = tile_ref[b, pl.ds(pl.multiple_of(group_no * 8, 8), 8), :]
            cx, cy, length = [jnp.broadcast_to(row[n : n + 1], (8, 128)) for n in range(3)]
            centre.append((cx, cy))
            lengths.append(length)
        chunks = lax.div(longest + 31, 32)

        def gather(step, carry):
            for b, i in [(b, step * 2 + n) for n in range(2) for b in both]:
                units = [ix_ref[b, pl.ds(unit0 + i * 2 + n, 1), :] for n in range(2)]
                index = jnp.concatenate(units, axis=1)
                one = jnp.where(row_low == (index & 127), 1.0, 0.0).astype(BF16)
                got = dot(two_ref[b], jnp.concatenate([one, one], axis=0), NN)
                for n in range(2):
                    lanes = slice(n * 128, n * 128 + 128)
                    unit = jnp.broadcast_to(units[n], (8, 128))
                    low = unit & 127
                    high = unit >> 7
                    odd = (high & 1) == 1
                    exact = zero8
                    near = zero8
                    last = zero8
                    for h in range(16):
                        rows = slice(h * 8, h * 8 + 8)
                        hit = (high >> 1) == h
                        exact = jnp.where(hit, take_lanes(tab_ref[b, rows, :], low), exact)
                        near = jnp.where(hit, got[rows, lanes], near)
                    for h in range(4):
                        rows = slice(128 + h * 8, 136 + h * 8)
                        last = jnp.where((high >> 3) == h, got[rows, lanes], last)
                    last = jnp.sum(
                        jnp.where(sub == (high & 7), last, 0.0), axis=0, keepdims=True
                    )
                    feats = jnp.where(
                        sub < 4,
                        jnp.where(odd, pltpu.roll(exact, 4, 0), exact),
                        jnp.where(odd, near, pltpu.roll(near, 4, 0)),
                    )
                    j = i * 2 + n
                    fr_ref[b, pl.ds(j, 8, stride=16), :] = feats
                    fr_ref[b, pl.ds(128 + j, 1), :] = last
            return carry

        lax.fori_loop(0, lax.div(chunks + 1, 2), gather, 0)

        for b in both:
            cx, cy = centre[b]
            for part in range(2):
                c0 = part * 8

                def got(f, b=b, c0=c0):
                    return fr_ref[b, f * 16 + c0 : f * 16 + c0 + 8, :]

                u = got(0) - cx
                v = got(1) - cy
                con_a, con_b, con_c = [got(f) for f in range(2, 5)]
                fr_ref[b, c0 : c0 + 8, :] = u
                fr_ref[b, 16 + c0 : 16 + c0 + 8, :] = v
                live = (lane_k + (sub + c0) * 16).astype(F32) < lengths[b]
                coefs = [
                    con_a * (-0.5 * LOG2_E),
                    con_b * -LOG2_E,
                    con_c * (-0.5 * LOG2_E),
                    (con_a * u + con_b * v) * LOG2_E,
                    (con_b * u + con_c * v) * LOG2_E,
                    jnp.where(
                        live,
                        (got(5) - 0.5 * (con_a * u * u + con_c * v * v) - con_b * u * v) * LOG2_E,
                        -1e30,
                    ),
                ]
                for f, value in enumerate(coefs):
                    hi, rest = split2(value)
                    mid, lo = split2(rest)
                    for p, piece in enumerate((hi, mid, lo)):
                        co_ref[b, pl.ds(c0 * 32 + p * 8 + f, 8, stride=32), :] = piece
                for channel, shade in enumerate((got(6), got(7), got(8))):
                    hi, lo = split2(shade)
                    cc_ref[b, pl.ds(c0 * 8 + channel, 8, stride=8), :] = hi
                    cc_ref[b, pl.ds(c0 * 8 + 3 + channel, 8, stride=8), :] = lo

        def colours_of(b, i):
            rows = cc_ref[b, pl.ds(pl.multiple_of(i * 16, 16), 16), :]
            return jnp.concatenate(
                [
                    jnp.concatenate(
                        [jnp.where(diag, rows[n * 8 + r : n * 8 + r + 1], 0.0) for r in range(6)],
                        axis=0,
                    )
                    for n in range(2)
                ],
                axis=1,
            ).astype(BF16)

        def fade(b, i):
            row0 = pl.multiple_of(i * 256, 256)
            pair = co_ref[b, pl.ds(pl.multiple_of(i * 64, 64), 64), :].astype(BF16)
            lhs = jnp.concatenate([pair[0:32], pair[32:64]], axis=1)
            al_ref[b, pl.ds(row0, 256), :] = jnp.exp2(dot(lhs, basis_b, TN))

        def weigh(b, i, through):
            row0 = pl.multiple_of(i * 256, 256)
            alphas = al_ref[b, pl.ds(row0, 256), :]
            weights = []
            for k in range(32):
                weight = through * alphas[k * 8 : k * 8 + 8]
                through = through - weight
                weights.append(weight)
            weight = jnp.concatenate(weights, axis=0)
            w_hi, w_lo = split2(weight)
            w_ref[b, pl.ds(row0, 256), :] = weight
            ww_ref[b, pl.ds(row0, 256), 0:256] = w_hi.astype(BF16)
            ww_ref[b, pl.ds(row0, 256), 256:512] = w_lo.astype(BF16)
            return through

        def shade(b, i, colour):
            row0 = pl.multiple_of(i * 256, 256)
            c_two = colours_of(b, i)
            prod = dot(c_two, ww_ref[b, pl.ds(row0, 256), 0:256], NN)
            prod_lo = dot(c_two, ww_ref[b, pl.ds(row0, 256), 256:512], NN)
            return colour + prod[0:24] + prod[24:48] + prod_lo[0:24] + prod_lo[24:48]

        def forward(i, carry):
            carry = list(carry)
            colours = [shade(b, i - 1, carry[b][1]) for b in both]
            through = [weigh(b, i, carry[b][0]) for b in both]
            for b in both:
                fade(b, i + 1)
            return tuple((through[b], colours[b]) for b in both)

        for b in both:
            fade(b, 0)
        start = [weigh(b, 0, jnp.ones((8, 256), F32)) for b in both]
        for b in both:
            fade(b, 1)
        dark = jnp.zeros((24, 256), F32)
        done = lax.fori_loop(1, chunks, forward, tuple((start[b], dark) for b in both))
        done = [(None, shade(b, chunks - 1, done[b][1])) for b in both]
        r_four = []
        for b in both:
            resid = done[b][1] - aim_ref[b, pl.ds(pl.multiple_of(group_no * 24, 8), 24), :]
            err_ref[b] += resid * resid
            r_hi, r_lo = split2(2.0 * resid)
            r_four.append(jnp.concatenate([r_hi, r_hi, r_lo, r_lo], axis=0).astype(BF16))
            r_t = jnp.transpose(
                jnp.concatenate(
                    [jnp.zeros((8, 256), F32), r_hi, r_lo, jnp.zeros((72, 256), F32)], axis=0
                )
            ).astype(BF16)
            rt_ref[b, 512:768, :] = r_t
            rt_ref[b, 768:1024, :] = r_t

        def pull(b, i):
            c_two = colours_of(b, i)
            pl_ref[b] = dot(jnp.concatenate([c_two, c_two], axis=0), r_four[b], TN)

        def slope(b, i, behind):
            row0 = pl.multiple_of(i * 256, 256)
            pulls = pl_ref[b]
            alphas = al_ref[b, pl.ds(row0, 256), :]
            weight = w_ref[b, pl.ds(row0, 256), :]
            parts = []
            for k in range(31, -1, -1):
                diff = pulls[k * 8 : k * 8 + 8] - behind
                parts.append(weight[k * 8 : k * 8 + 8] * diff)
                behind = behind + alphas[k * 8 : k * 8 + 8] * diff
            d_hi, d_lo = split2(jnp.concatenate(parts[::-1], axis=0))
            dd_ref[b, :, 0:256] = d_hi.astype(BF16)
            dd_ref[b, :, 256:512] = d_lo.astype(BF16)
            return behind

        def collect(b, i):
            row0 = pl.multiple_of(i * 256, 256)
            lhs = jnp.concatenate([dd_ref[b], ww_ref[b, pl.ds(row0, 256), :]], axis=1)
            sums = jnp.where(own, dot(lhs, rt_ref[b], NN), 0.0)
            for n in range(2):
                flip = jnp.transpose(sums[n * 128 : n * 128 + 128])
                j = i * 2 + n
                mo_ref[b, pl.ds(j, 8, stride=16), :] = flip[0:8]
                for h in range(3):
                    mo_ref[b, pl.ds((8 + h) * 16 + j, 1), :] = jnp.sum(
                        flip[8 + h * 8 : 16 + h * 8] + flip[32 + h * 8 : 40 + h * 8],
                        axis=0,
                        keepdims=True,
                    )

        def backward(step, carry):
            i = chunks - 1 - step
            for b in both:
                collect(b, i + 1)
            carry = tuple(slope(b, i, carry[b]) for b in both)
            for b in both:
                pull(b, jnp.maximum(i - 1, 0))
            return carry

        for b in both:
            pull(b, chunks - 1)
        start = tuple(slope(b, chunks - 1, jnp.zeros((8, 256), F32)) for b in both)
        for b in both:
            pull(b, jnp.maximum(chunks - 2, 0))
        lax.fori_loop(1, chunks, backward, start)
        for b in both:
            collect(b, 0)

        for b in both:
            for part in range(2):
                c0 = part * 8

                def moment(f, b=b, c0=c0):
                    return mo_ref[b, f * 16 + c0 : f * 16 + c0 + 8, :]

                u, v, con_a, con_b, con_c = [
                    fr_ref[b, f * 16 + c0 : f * 16 + c0 + 8, :] for f in range(5)
                ]
                m_xx, m_xy, m_yy, m_x, m_y, m_1 = [moment(f) for f in range(6)]
                s_x = m_x - u * m_1
                s_y = m_y - v * m_1
                grads = [
                    con_a * s_x + con_b * s_y,
                    con_b * s_x + con_c * s_y,
                    -0.5 * (m_xx - u * (m_x + s_x)),
                    -(m_xy - u * m_y - v * s_x),
                    -0.5 * (m_yy - v * (m_y + s_y)),
                    m_1,
                    moment(8),
                    moment(9),
                    moment(10),
                ]
                used = (sub + c0) < 2 * chunks
                for f, value in enumerate(grads):
                    hi, lo = split2(jnp.where(used, value, 0.0))
                    gr_ref[b, f * 16 + c0 : f * 16 + c0 + 8, :] = hi
                    gr_ref[b, 144 + f * 16 + c0 : 144 + f * 16 + c0 + 8, :] = lo

        def scatter(step, carry):
            for b in both:
                total = None
                for n in range(2):
                    j = step * 4 + n * 2
                    index = jnp.concatenate(
                        [ix_ref[b, pl.ds(unit0 + j + n, 1), :] for n in range(2)], axis=1
                    )
                    hit = row_a == (index >> 8)
                    rows = []
                    for f in range(18):
                        row = f * 16 + j
                        value = jnp.concatenate(
                            [gr_ref[b, pl.ds(row, 1), :], gr_ref[b, pl.ds(row + 1, 1), :]], axis=1
                        )
                        rows.append(jnp.where(hit, value, 0.0))
                    add = dot(jnp.concatenate(rows, axis=0).astype(BF16), scatter_rhs(index), NT)
                    add = add[0:144] + add[144:288]
                    total = add if total is None else total + add
                for half in range(2):
                    sg_ref[b, half, 0:144, :] += total[:, half * 128 : half * 128 + 128]
            return carry

        lax.fori_loop(0, lax.div(chunks + 1, 2), scatter, 0)
        return carry

    lax.fori_loop(0, GROUPS, group, 0)
    for b in both:
        total = jnp.sum(jnp.sum(err_ref[b], axis=0, keepdims=True), axis=1, keepdims=True)
        for half in range(2):
            sg_ref[b, half, 144:160, :] = view_ref[b, pl.ds(half, 16, stride=2), :]
            sg_ref[b, half, 240:256, :] = jnp.broadcast_to(total, (16, 128))

    for a in range(16):
        for half in range(2):
            parts = [
                sg_ref[b, half, pl.ds(q * 128 + a, 8, stride=16), :]
                for b in both
                for q in range(2)
            ]
            for r in range(4):
                out_ref[(a * 2 + half) * 4 + r] = by_quarter(
                    quarter, [turn(parts[q], q - r) for q in range(4)]
                )


def grads_kernel(
    cam_ref, params_ref, send_ref, grad_ref, out_ref, err_ref, flat_ref, res_ref, gg_ref, sems
):
    copies = fetch_params(params_ref, flat_ref, sems)
    row_a = lax.broadcasted_iota(jnp.int32, (16, 256), 0)
    quarter = lax.broadcasted_iota(jnp.int32, (8, 128), 1) >> 5
    gg_ref[...] = jnp.zeros(gg_ref.shape, F32)

    def place(step, total):
        tiles_of = [[grad_ref[step * 16 + n * 8 + i] for i in range(8)] for n in range(2)]
        for tile in tiles_of[0] + tiles_of[1]:
            total = total + tile
        sums = [None] * BATCHES
        for part, batch_no in [(n, b) for n in range(2) for b in range(BATCHES)]:
            tiles = tiles_of[part]
            index = send_ref[batch_no, pl.ds(step * 2 + part, 1), :]
            hit = row_a == (index >> 8)
            rhs = scatter_rhs(index)
            high = []
            low = []
            for q in range(2):
                values = jnp.concatenate(
                    [
                        by_quarter(
                            quarter,
                            [turn(tiles[4 * n + i], i - 2 * batch_no - q) for i in range(4)],
                        )
                        for n in range(2)
                    ],
                    axis=1,
                )
                g_hi, g_lo = split2(values)
                for f in range(8 if q == 0 else 2):
                    high.append(jnp.where(hit, g_hi[f : f + 1], 0.0))
                    low.append(jnp.where(hit, g_lo[f : f + 1], 0.0))
            add = dot(jnp.concatenate(high + low, axis=0).astype(BF16), rhs, NT)
            add = add[0:160] + add[160:320]
            sums[batch_no] = add if part == 0 else sums[batch_no] + add
        for batch_no in range(BATCHES):
            gg_ref[batch_no] += sums[batch_no]
        return total

    total = lax.fori_loop(0, 8, place, jnp.zeros((8, 128), F32))
    for copy in copies:
        copy.wait()

    def block(block_no, carry):
        row0 = pl.multiple_of((block_no // 2) * 8, 8)
        half = block_no % 2
        lane0 = pl.multiple_of(half * 128, 128)
        cols = [param_rows(flat_ref, row0, half, p) for p in range(PARAMS)]
        geo = [0.0] * 10
        opac = 0.0
        shade = [0.0] * 48
        for batch_no in range(BATCHES):

            def feat(f, batch_no=batch_no):
                return gg_ref[batch_no, pl.ds(f * 16 + row0, 8), pl.ds(lane0, 128)]

            cam = pick_camera(cam_ref, batch_no, feat(9))
            _, pull_geo = jax.vjp(
                lambda c: screen_terms(c[0:3], shape_terms(c), cam), cols[0:10]
            )
            (d_geo,) = pull_geo(tuple(feat(f) for f in range(5)))
            basis, pull_ray = jax.vjp(lambda c: ray_basis(c, cam), cols[0:3])
            d_col = [feat(6 + h) for h in range(3)]
            (d_ray,) = pull_ray(
                [
                    d_col[0] * cols[11 + k] + d_col[1] * cols[27 + k] + d_col[2] * cols[43 + k]
                    for k in range(16)
                ]
            )
            for i in range(10):
                geo[i] = geo[i] + d_geo[i]
            for i in range(3):
                geo[i] = geo[i] + d_ray[i]
            opac = opac + feat(5)
            for h in range(3):
                for k in range(16):
                    shade[16 * h + k] = shade[16 * h + k] + d_col[h] * basis[k]
        opac = opac / (1.0 + jnp.exp(cols[10]))
        for p, value in enumerate(geo + [opac] + shade):
            res_ref[pl.ds((2 * row0 + half) * PITCH + p, 8, stride=2 * PITCH), :] = value
        return carry

    copies = [
        pltpu.make_async_copy(
            res_ref.at[pl.ds(j * PITCH, PARAMS), :],
            out_ref.at[:, pl.ds(j * 128, 128)],
            sems.at[j],
        )
        for j in range(32)
    ]
    for part in range(2):
        lax.fori_loop(part * 2, part * 2 + 2, block, 0)
        for copy in copies[part * 16 : part * 16 + 16]:
            copy.start()
    lane = lax.broadcasted_iota(jnp.int32, (1, 128), 1)
    errors = jnp.sum(
        jnp.where((lane == 32) | (lane == 96), total[7:8], 0.0), axis=1, keepdims=True
    )
    err_ref[...] = errors * (1.0 / (BATCHES * OWNERS * TILES_DEV * 3 * TILE_PX))
    for copy in copies:
        copy.wait()


def exchange(values):
    return lax.all_to_all(values, "dev", split_axis=0, concat_axis=0, tiled=True)


SMEM = pl.BlockSpec(memory_space=pltpu.SMEM)
VMEM = pl.BlockSpec(memory_space=pltpu.VMEM)
HBM = pl.BlockSpec(memory_space=pltpu.HBM)
CALL = pltpu.CompilerParams(vmem_limit_bytes=16 * 1024 * 1024)
OFFER_CALL = pltpu.CompilerParams(vmem_limit_bytes=60 * 1024 * 1024)
BLEND_CALL = pltpu.CompilerParams(vmem_limit_bytes=28 * 1024 * 1024)


def local(params, cameras, send_lists, tile_slots, tile_ids, tile_len, targets):
    lengths = tile_len[:, 0]
    tile_no = jnp.arange(TILES_DEV, dtype=jnp.int32)
    ahead = (lengths[:, None, :] > lengths[:, :, None]) | (
        (lengths[:, None, :] == lengths[:, :, None]) & (tile_no[None, None, :] < tile_no[None, :, None])
    )
    rank = jnp.sum(ahead.astype(jnp.int32), axis=2)
    order = jnp.sum(
        jnp.where(rank[:, None, :] == tile_no[None, :, None], tile_no[None, None, :], 0), axis=2
    )

    feats, cams, send = pl.pallas_call(
        offer_kernel,
        out_shape=(
            jax.ShapeDtypeStruct((OWNERS * 12, 128), F32),
            jax.ShapeDtypeStruct((CAM_ROWS * 8, 128), F32),
            jax.ShapeDtypeStruct((BATCHES, 16, 256), jnp.int32),
        ),
        in_specs=[VMEM, HBM, VMEM],
        out_specs=(VMEM, VMEM, VMEM),
        scratch_shapes=[
            pltpu.VMEM((32 * PITCH, 128), F32),
            pltpu.VMEM((BATCHES, 768, 128), F32),
            pltpu.VMEM((BATCHES, 512, 256), BF16),
            pltpu.SemaphoreType.DMA((32,)),
        ],
        compiler_params=OFFER_CALL,
        name="offer",
    )(cameras, params, jnp.transpose(send_lists, (0, 1, 3, 2)))
    feats = exchange(feats.reshape(OWNERS, 1, 1536)).reshape(OWNERS * 12, 128)

    views, slots, tiles, aims = pl.pallas_call(
        plan_kernel,
        out_shape=(
            jax.ShapeDtypeStruct((BATCHES, 32, 128), F32),
            jax.ShapeDtypeStruct((BATCHES, GROUPS * 16, 128), jnp.int32),
            jax.ShapeDtypeStruct((BATCHES, GROUPS * 8, 128), F32),
            jax.ShapeDtypeStruct((BATCHES, GROUPS * 24, 256), F32),
        ),
        in_specs=[SMEM, SMEM, SMEM, VMEM, VMEM],
        out_specs=(VMEM, VMEM, VMEM, VMEM),
        scratch_shapes=[pltpu.VMEM((BATCHES, 8, 256), jnp.int32)],
        compiler_params=CALL,
        name="plan",
    )(order, tile_ids, lengths, tile_slots, targets)

    rows = TILES_DEV // GROUPS * PAIRS
    slot_grads = pl.pallas_call(
        blend_kernel,
        out_shape=jax.ShapeDtypeStruct((OWNERS, 8, 128), F32),
        in_specs=[SMEM, SMEM, VMEM, VMEM, VMEM, VMEM, VMEM, VMEM],
        out_specs=VMEM,
        scratch_shapes=[
            pltpu.VMEM((BATCHES, 768, 128), F32),
            pltpu.VMEM((BATCHES, 288, 128), F32),
            pltpu.VMEM((BATCHES, 160, 256), BF16),
            pltpu.VMEM((BATCHES, 144, 128), F32),
            pltpu.VMEM((BATCHES, 576, 128), F32),
            pltpu.VMEM((BATCHES, 128, 128), F32),
            pltpu.VMEM((BATCHES, rows + 256, 256), F32),
            pltpu.VMEM((BATCHES, rows, 256), F32),
            pltpu.VMEM((BATCHES, rows, 512), BF16),
            pltpu.VMEM((BATCHES, 256, 256), F32),
            pltpu.VMEM((BATCHES, 256, 512), BF16),
            pltpu.VMEM((BATCHES, 1024, 128), BF16),
            pltpu.VMEM((BATCHES, 176, 128), F32),
            pltpu.VMEM((BATCHES, 288, 128), F32),
            pltpu.VMEM((BATCHES, 2, 256, 128), F32),
            pltpu.VMEM((BATCHES, 24, 256), F32),
        ],
        compiler_params=BLEND_CALL,
        name="blend",
    )(order, lengths, cams, feats, views, slots, tiles, aims)
    slot_grads = exchange(slot_grads)

    grads, err = pl.pallas_call(
        grads_kernel,
        out_shape=(
            jax.ShapeDtypeStruct((PARAMS, 4096), F32),
            jax.ShapeDtypeStruct((1, 1), F32),
        ),
        in_specs=[VMEM, HBM, VMEM, VMEM],
        out_specs=(HBM, VMEM),
        scratch_shapes=[
            pltpu.VMEM((32 * PITCH, 128), F32),
            pltpu.VMEM((32 * PITCH, 128), F32),
            pltpu.VMEM((BATCHES, 160, 256), F32),
            pltpu.SemaphoreType.DMA((32,)),
        ],
        compiler_params=CALL,
        name="param_grads",
    )(cams, params, send, slot_grads)
    return (grads, err[0, 0])


def solution(mesh):
    placed = (
        P(None, "dev"),
        P(),
        P(None, "dev", None, None),
        P(None, "dev", None),
        P(None, "dev"),
        P(None, "dev", None),
        P(None, "dev", None, None),
    )
    return jax.shard_map(
        local, mesh=mesh, in_specs=placed, out_specs=(P(None, "dev"), P()), check_vma=False
    )
```

```python
import jax
import jax.numpy as jnp
from jax import lax
from jax.experimental import pallas as pl
from jax.experimental.pallas import tpu as pltpu
from jax.sharding import PartitionSpec as P

BATCHES = 2
TILE = 16
PAIRS = 256
TILE_PX = 256
TILES_X = 240
TILES_VIEW = 32400
VIEWS = 4
PARAMS = 59
TILES_DEV = 32
OWNERS = 128
CAP = 32
SLOTS = 4096
GROUPS = 4
PITCH = 72
LOG2_E = 1.4426950408889634

SH_ZERO = 0.28209479177387814
SH_ONE = 0.4886025119029199
SH_TWO = (
    1.0925484305920792,
    -1.0925484305920792,
    0.31539156525252005,
    -1.0925484305920792,
    0.5462742152960396,
)
SH_THREE = (
    -0.5900435899266435,
    2.890611442640554,
    -0.4570457994644658,
    0.3731763325901154,
    -0.4570457994644658,
    1.445305721320277,
    -0.5900435899266435,
)

F32 = jnp.float32
BF16 = jnp.bfloat16
NN = (((1,), (0,)), ((), ()))
NT = (((1,), (1,)), ((), ()))
TN = (((0,), (0,)), ((), ()))


def dot(lhs, rhs, dims):
    return lax.dot_general(lhs, rhs, dims, preferred_element_type=F32)


def split2(value):
    high = value.astype(BF16).astype(F32)
    return high, value - high


def camera_table(cameras):
    fields = [jnp.broadcast_to(cameras[:, n : n + 1], (8, 128)) for n in range(8)]
    cos_yaw = jnp.cos(fields[0])
    sin_yaw = jnp.sin(fields[0])
    cos_pitch = jnp.cos(fields[1])
    sin_pitch = jnp.sin(fields[1])
    frame = [
        cos_yaw,
        sin_yaw,
        sin_pitch * sin_yaw,
        cos_pitch,
        -sin_pitch * cos_yaw,
        -cos_pitch * sin_yaw,
        sin_pitch,
        cos_pitch * cos_yaw,
    ]
    shift = fields[2:5]
    centre = [
        -(frame[0] * shift[0] + frame[2] * shift[1] + frame[5] * shift[2]),
        -(frame[3] * shift[1] + frame[6] * shift[2]),
        -(frame[1] * shift[0] + frame[4] * shift[1] + frame[7] * shift[2]),
    ]
    return frame + shift + centre + fields[5:8]


CAM_ROWS = 17


def sh_basis(dir_x, dir_y, dir_z):
    square_x = dir_x * dir_x
    square_y = dir_y * dir_y
    square_z = dir_z * dir_z
    return [
        SH_ZERO * jnp.ones_like(dir_x),
        -SH_ONE * dir_y,
        SH_ONE * dir_z,
        -SH_ONE * dir_x,
        SH_TWO[0] * dir_x * dir_y,
        SH_TWO[1] * dir_y * dir_z,
        SH_TWO[2] * (2.0 * square_z - square_x - square_y),
        SH_TWO[3] * dir_x * dir_z,
        SH_TWO[4] * (square_x - square_y),
        SH_THREE[0] * dir_y * (3.0 * square_x - square_y),
        SH_THREE[1] * dir_x * dir_y * dir_z,
        SH_THREE[2] * dir_y * (4.0 * square_z - square_x - square_y),
        SH_THREE[3] * dir_z * (2.0 * square_z - 3.0 * square_x - 3.0 * square_y),
        SH_THREE[4] * dir_x * (4.0 * square_z - square_x - square_y),
        SH_THREE[5] * dir_z * (square_x - square_y),
        SH_THREE[6] * dir_x * (square_x - 3.0 * square_y),
    ]


def shape_terms(cols):
    inv_quat = 1.0 / jnp.sqrt(
        cols[6] * cols[6] + cols[7] * cols[7] + cols[8] * cols[8] + cols[9] * cols[9]
    )
    return [jnp.exp(cols[3 + i]) for i in range(3)] + [cols[6 + i] * inv_quat for i in range(4)]


def screen_terms(position, shape, cam):
    spread = shape[0:3]
    quat_w, quat_x, quat_y, quat_z = shape[3:7]
    frame = ((cam[0], None, cam[1]), (cam[2], cam[3], cam[4]), (cam[5], cam[6], cam[7]))
    shift = cam[8:11]
    focal = cam[14]
    viewed = [
        frame[0][0] * position[0] + frame[0][2] * position[2] + shift[0],
        frame[1][0] * position[0]
        + frame[1][1] * position[1]
        + frame[1][2] * position[2]
        + shift[1],
        frame[2][0] * position[0]
        + frame[2][1] * position[1]
        + frame[2][2] * position[2]
        + shift[2],
    ]
    inv_depth = 1.0 / viewed[2]
    screen_u = focal * viewed[0] * inv_depth + cam[15]
    screen_v = focal * viewed[1] * inv_depth + cam[16]
    rotation = (
        (
            1.0 - 2.0 * (quat_y * quat_y + quat_z * quat_z),
            2.0 * (quat_x * quat_y - quat_w * quat_z),
            2.0 * (quat_x * quat_z + quat_w * quat_y),
        ),
        (
            2.0 * (quat_x * quat_y + quat_w * quat_z),
            1.0 - 2.0 * (quat_x * quat_x + quat_z * quat_z),
            2.0 * (quat_y * quat_z - quat_w * quat_x),
        ),
        (
            2.0 * (quat_x * quat_z - quat_w * quat_y),
            2.0 * (quat_y * quat_z + quat_w * quat_x),
            1.0 - 2.0 * (quat_x * quat_x + quat_y * quat_y),
        ),
    )
    jac_main = focal * inv_depth
    jac_u = -jac_main * viewed[0] * inv_depth
    jac_v = -jac_main * viewed[1] * inv_depth
    row_u = [
        jac_main * frame[0][0] + jac_u * frame[2][0],
        jac_u * frame[2][1],
        jac_main * frame[0][2] + jac_u * frame[2][2],
    ]
    row_v = [jac_main * frame[1][i] + jac_v * frame[2][i] for i in range(3)]
    along_u = [
        (row_u[0] * rotation[0][j] + row_u[1] * rotation[1][j] + row_u[2] * rotation[2][j])
        * spread[j]
        for j in range(3)
    ]
    along_v = [
        (row_v[0] * rotation[0][j] + row_v[1] * rotation[1][j] + row_v[2] * rotation[2][j])
        * spread[j]
        for j in range(3)
    ]
    cov_uu = along_u[0] * along_u[0] + along_u[1] * along_u[1] + along_u[2] * along_u[2] + 0.3
    cov_uv = along_u[0] * along_v[0] + along_u[1] * along_v[1] + along_u[2] * along_v[2]
    cov_vv = along_v[0] * along_v[0] + along_v[1] * along_v[1] + along_v[2] * along_v[2] + 0.3
    inv_det = 1.0 / (cov_uu * cov_vv - cov_uv * cov_uv)
    return screen_u, screen_v, cov_vv * inv_det, -cov_uv * inv_det, cov_uu * inv_det


def ray_basis(position, cam):
    ray = [position[i] - cam[11 + i] for i in range(3)]
    inv_len = 1.0 / jnp.sqrt(ray[0] * ray[0] + ray[1] * ray[1] + ray[2] * ray[2])
    return sh_basis(ray[0] * inv_len, ray[1] * inv_len, ray[2] * inv_len)


def camera_field(cam_ref, field, batch_no, view_no):
    row = field * 8 + batch_no * VIEWS + view_no
    return jnp.broadcast_to(cam_ref[row : row + 1, :], (8, 128))


def pick_camera(cam_ref, batch_no, view):
    picked = []
    for field in range(CAM_ROWS):
        value = camera_field(cam_ref, field, batch_no, VIEWS - 1)
        for view_no in range(VIEWS - 2, -1, -1):
            value = jnp.where(
                view == view_no, camera_field(cam_ref, field, batch_no, view_no), value
            )
        picked.append(value)
    return picked


def take_lanes(table, index):
    return jnp.take_along_axis(table, index, axis=1, mode="promise_in_bounds")


def by_quarter(quarter, values):
    out = values[0]
    for q in range(1, len(values)):
        out = jnp.where(quarter == q, values[q], out)
    return out


def turn(value, quarters):
    quarters = quarters % 4
    return value if quarters == 0 else pltpu.roll(value, 32 * quarters, 1)


def scatter_rhs(index):
    row = lax.broadcasted_iota(jnp.int32, (256, index.shape[1]), 0)
    return jnp.where(row == (index & 255), 1.0, 0.0).astype(BF16)


def fetch_params(params_ref, flat_ref, sems):
    copies = [
        pltpu.make_async_copy(
            params_ref.at[:, pl.ds(j * 128, 128)],
            flat_ref.at[pl.ds(j * PITCH, PARAMS), :],
            sems.at[j],
        )
        for j in range(32)
    ]
    for copy in copies:
        copy.start()
    return copies


def param_rows(flat_ref, row0, half, param):
    return flat_ref[pl.ds((2 * row0 + half) * PITCH + param, 8, stride=2 * PITCH), :]


def offer_kernel(
    camera_ref, params_ref, list_ref, out_ref, cam_ref, send_ref, flat_ref, tab_ref, two_ref, sems
):
    copies = fetch_params(params_ref, flat_ref, sems)
    quarter = lax.broadcasted_iota(jnp.int32, (8, 128), 1) >> 5
    upper = lax.broadcasted_iota(jnp.int32, (8, 128), 0) < 4
    row_low = lax.broadcasted_iota(jnp.int32, (128, 256), 0)
    place = (lax.broadcasted_iota(jnp.int32, (8, 128), 0) & 3) == quarter
    cameras = jnp.concatenate([camera_ref[0], camera_ref[1]], axis=0)
    for field, value in enumerate(camera_table(cameras)):
        cam_ref[field * 8 : field * 8 + 8, :] = value
    for batch_no in range(BATCHES):
        by_owner = jnp.transpose(
            jnp.concatenate([list_ref[batch_no, 0].astype(F32)] * 4, axis=0)
        )
        for chunk in range(16):
            lists = jnp.where(place, by_owner[chunk * 8 : chunk * 8 + 8], 0.0)
            for half in range(2):
                line = jnp.sum(lists[half * 4 : half * 4 + 4], axis=0, keepdims=True)
                send_ref[batch_no, chunk : chunk + 1, half * 128 : half * 128 + 128] = line.astype(
                    jnp.int32
                )

    def block(block_no, carry):
        row0 = (block_no // 2) * 8
        half = block_no % 2
        cols = [param_rows(flat_ref, row0, half, p) for p in range(PARAMS)]
        opac = -(jnp.maximum(-cols[10], 0.0) + jnp.log1p(jnp.exp(-jnp.abs(cols[10]))))
        shared = cols[0:3] + shape_terms(cols) + [opac]
        for batch_no in range(BATCHES):
            feats = list(shared)
            for view_no in range(VIEWS):
                cam = [
                    camera_field(cam_ref, field, batch_no, view_no) for field in range(CAM_ROWS)
                ]
                basis = ray_basis(cols[0:3], cam)
                for channel in range(3):
                    shade = 0.5
                    for term in range(16):
                        shade = shade + basis[term] * cols[11 + 16 * channel + term]
                    feats.append(shade)
            feats.append(jnp.zeros((8, 128), F32))
            for f, value in enumerate(feats):
                start = (2 * row0 + half) * 24 + f
                tab_ref[batch_no, pl.ds(start, 8, stride=48), :] = value
        return carry

    for part in range(2):
        for copy in copies[part * 16 : part * 16 + 16]:
            copy.wait()
        lax.fori_loop(part * 2, part * 2 + 2, block, 0)

    def pieces(step, carry):
        for batch_no in range(BATCHES):
            for n in range(8):
                h = step * 8 + n
                hi, mid = split2(tab_ref[batch_no, pl.ds(pl.multiple_of(h * 24 + 8, 8), 16), :])
                row = pl.multiple_of(h * 16, 16)
                two_ref[batch_no, pl.ds(row, 16), 0:128] = hi.astype(BF16)
                two_ref[batch_no, pl.ds(row, 16), 128:256] = mid.astype(BF16)
        return carry

    lax.fori_loop(0, 4, pieces, 0)

    def pick(chunk, carry):
        cut = []
        for batch_no in range(BATCHES):
            index = send_ref[batch_no, pl.ds(chunk, 1), :]
            high = jnp.broadcast_to(index >> 7, (8, 256))
            low = jnp.broadcast_to(index & 127, (8, 256))
            one = jnp.where(row_low == (index & 127), 1.0, 0.0).astype(BF16)
            one = jnp.concatenate([one, one], axis=0)
            exact = [jnp.zeros((8, 128), F32)] * 2
            acc = [jnp.zeros((8, 256), F32)] * 2
            for part in range(4):
                got = dot(two_ref[batch_no, part * 128 : part * 128 + 128, :], one, NN)
                for n in range(8):
                    h = part * 8 + n
                    hit = high == h
                    for q in range(2):
                        row = n * 16 + q * 8
                        acc[q] = jnp.where(hit, got[row : row + 8], acc[q])
                    rows = tab_ref[batch_no, h * 24 : h * 24 + 8, :]
                    for half in range(2):
                        lanes = slice(half * 128, half * 128 + 128)
                        exact[half] = jnp.where(
                            hit[:, lanes], take_lanes(rows, low[:, lanes]), exact[half]
                        )
            cut.append((exact, [[a[:, 0:128], a[:, 128:256]] for a in acc]))
        for half in range(2):
            heads = [cut[0][0][half], cut[0][1][0][half], cut[0][1][1][half], cut[1][0][half]]
            tails = [cut[1][1][q][half] for q in range(2)]
            folded = [pltpu.roll(tail, 4, 0) for tail in tails]
            main = []
            tail = []
            for r in range(4):
                main.append(by_quarter(quarter, [turn(heads[q], q - r) for q in range(4)]))
                tail.append(
                    by_quarter(
                        quarter,
                        [
                            turn(tails[0], -r),
                            turn(folded[0], 1 - r),
                            turn(tails[1], 2 - r),
                            turn(folded[1], 3 - r),
                        ],
                    )
                )
            for r in range(0, 4, 2):
                row0 = pl.multiple_of((chunk * 2 + half) * 48 + r * 12, 8)
                middle = pltpu.roll(main[r + 1], 4, 0)
                out_ref[pl.ds(row0, 8), :] = main[r]
                out_ref[pl.ds(row0 + 8, 8), :] = jnp.where(upper, tail[r], middle)
                out_ref[pl.ds(row0 + 16, 8), :] = jnp.where(
                    upper, middle, pltpu.roll(tail[r + 1], 4, 0)
                )
        return carry

    lax.fori_loop(0, 16, pick, 0)


def plan_kernel(
    order_ref, ids_ref, len_ref, slots_ref, target_ref,
    out_ref, ix_ref, tile_ref, aim_ref, sl_ref,
):
    lane = lax.broadcasted_iota(jnp.int32, (8, 128), 1)
    sub = lax.broadcasted_iota(jnp.int32, (8, 128), 0)
    diag = sub == (lane & 7)

    def group(group_no, carry):
        for b in range(BATCHES):
            cx = jnp.zeros((1, 128), F32)
            cy = jnp.zeros((1, 128), F32)
            length = jnp.zeros((1, 128), F32)
            for t in range(8):
                tile = order_ref[b, group_no * 8 + t]
                in_view = lax.rem(ids_ref[b, tile], TILES_VIEW)
                row_t = lax.div(in_view, TILES_X)
                col_t = in_view - row_t * TILES_X
                here = (lane[0:1] & 7) == t
                cx = jnp.where(here, (col_t * TILE + 8).astype(F32), cx)
                cy = jnp.where(here, (row_t * TILE + 8).astype(F32), cy)
                length = jnp.where(here, len_ref[b, tile].astype(F32), length)
                sl_ref[b, t : t + 1, :] = slots_ref[b, pl.ds(tile, 1), :]
                for channel in range(3):
                    aim_ref[b, pl.ds(group_no * 24 + channel * 8 + t, 1), :] = target_ref[
                        b, pl.ds(tile, 1), channel, :
                    ]
            tile_ref[b, pl.ds(pl.multiple_of(group_no * 8, 8), 8), :] = jnp.concatenate(
                [cx, cy, length, jnp.zeros((5, 128), F32)], axis=0
            )
            picks = []
            for j in range(16):
                half = (j // 8) * 128
                picked = take_lanes(sl_ref[b, :, half : half + 128], (lane >> 3) + (j % 8) * 16)
                picks.append(
                    jnp.sum(jnp.where(diag, picked.astype(F32), 0.0), axis=0, keepdims=True)
                )
            ix_ref[b, pl.ds(pl.multiple_of(group_no * 16, 16), 16), :] = jnp.concatenate(
                picks, axis=0
            ).astype(jnp.int32)
        return carry

    lax.fori_loop(0, GROUPS, group, 0)
    row_high = lax.broadcasted_iota(jnp.int32, (32, PAIRS), 0)
    row_low = lax.broadcasted_iota(jnp.int32, (128, PAIRS), 0)

    def step(tile_no, sums):
        out = []
        for b in range(BATCHES):
            view = lax.div(ids_ref[b, tile_no], TILES_VIEW).astype(F32) * 0.5
            slots = slots_ref[b, pl.ds(tile_no, 1), :]
            lhs = jnp.where(row_high == (slots >> 7), view, 0.0).astype(BF16)
            rhs = jnp.where(row_low == (slots & 127), 1.0, 0.0).astype(BF16)
            out.append(sums[b] + dot(lhs, rhs, NT))
        return tuple(out)

    zero = jnp.zeros((32, 128), F32)
    sums = lax.fori_loop(0, TILES_DEV, step, (zero, zero))
    for b in range(BATCHES):
        out_ref[b] = sums[b]


def blend_kernel(
    order_ref, len_ref, cam_ref, feat_ref, view_ref, ix_ref, tile_ref, aim_ref, out_ref,
    sf_ref, tab_ref, two_ref, fr_ref, co_ref, cc_ref,
    al_ref, w_ref, ww_ref, pl_ref, dd_ref, rt_ref, mo_ref, gr_ref, sg_ref, err_ref,
):
    lane = lax.broadcasted_iota(jnp.int32, (8, 128), 1)
    sub = lax.broadcasted_iota(jnp.int32, (8, 128), 0)
    quarter = lane >> 5
    diag = sub == (lane & 7)
    lane_k = lane >> 3
    row_a = lax.broadcasted_iota(jnp.int32, (16, 256), 0)
    row_low = lax.broadcasted_iota(jnp.int32, (128, 256), 0)
    pix = lax.broadcasted_iota(jnp.int32, (8, 256), 1)
    term = lax.broadcasted_iota(jnp.int32, (8, 256), 0)
    px = (pix & 15).astype(F32) - 7.5
    py = (pix >> 4).astype(F32) - 7.5
    basis = jnp.where(
        term == 0, px * px,
        jnp.where(
            term == 1, px * py,
            jnp.where(
                term == 2, py * py,
                jnp.where(term == 3, px, jnp.where(term == 4, py, jnp.where(term == 5, 1.0, 0.0))),
            ),
        ),
    )
    basis_b = jnp.concatenate([basis] * 4, axis=0).astype(BF16)
    basis_2 = jnp.concatenate([jnp.concatenate([basis, basis], axis=1)] * 2, axis=0).astype(BF16)
    row_t = lax.broadcasted_iota(jnp.int32, (256, 128), 0) & 7
    lane_t = lax.broadcasted_iota(jnp.int32, (256, 128), 1)
    own = (lane_t & 7) == row_t
    zero8 = jnp.zeros((8, 128), F32)
    both = range(BATCHES)

    sg_ref[...] = jnp.zeros(sg_ref.shape, F32)
    co_ref[...] = jnp.zeros(co_ref.shape, F32)
    err_ref[...] = jnp.zeros(err_ref.shape, F32)

    upper = sub < 4

    def table(step, carry):
        for n in range(4):
            high = step * 4 + n
            main = []
            tail = []
            for r in range(0, 4, 2):
                row0 = pl.multiple_of(high * 48 + r * 12, 8)
                tiles = [feat_ref[pl.ds(row0 + m * 8, 8), :] for m in range(3)]
                main.append(tiles[0])
                main.append(pltpu.roll(jnp.where(upper, tiles[2], tiles[1]), 4, 0))
                tail.append(tiles[1])
                tail.append(pltpu.roll(tiles[2], 4, 0))
            folded = [pltpu.roll(value, 4, 0) for value in tail]
            for q in range(4):
                sf_ref[q // 3, pl.ds((q % 3) * 256 + high, 8, stride=32), :] = by_quarter(
                    quarter, [turn(main[i], i - q) for i in range(4)]
                )
            for q in range(2):
                sf_ref[1, pl.ds((q + 1) * 256 + high, 8, stride=32), :] = by_quarter(
                    quarter,
                    [
                        jnp.where(
                            upper, turn(tail[i], i - 2 * q), turn(folded[i], i - 2 * q - 1)
                        )
                        for i in range(4)
                    ],
                )
        return carry

    lax.fori_loop(0, 8, table, 0)

    def screen(block, carry):
        row0 = pl.multiple_of(block * 8, 8)
        for b in both:

            def raw(f, b=b):
                return sf_ref[b, pl.ds(f * 32 + row0, 8), :]

            view = view_ref[b, pl.ds(row0, 8), :]
            cam = pick_camera(cam_ref, b, view)
            feats = list(
                screen_terms([raw(f) for f in range(3)], [raw(f) for f in range(3, 10)], cam)
            ) + [raw(10)]
            for channel in range(3):
                shade = raw(11 + channel)
                for view_no in range(1, VIEWS):
                    shade = jnp.where(view == view_no, raw(11 + 3 * view_no + channel), shade)
                feats.append(shade)
            for f in range(4):
                tab_ref[b, pl.ds(row0 * 4 + f, 8, stride=4), :] = feats[f]
                tab_ref[b, pl.ds(128 + row0 * 4 + f, 8, stride=4), :] = feats[4 + f]
            tab_ref[b, pl.ds(256 + row0, 8), :] = feats[8]
        return carry

    lax.fori_loop(0, 4, screen, 0)
    for b in both:
        hi, mid = split2(tab_ref[b, 128:288, :])
        two_ref[b, :, 0:128] = hi.astype(BF16)
        two_ref[b, :, 128:256] = mid.astype(BF16)

    def group(group_no, carry):
        longest = jnp.int32(0)
        centre = []
        lengths = []
        unit0 = group_no * 16
        for b in both:
            longest = jnp.maximum(longest, len_ref[b, order_ref[b, group_no * 8]])
            row = tile_ref[b, pl.ds(pl.multiple_of(group_no * 8, 8), 8), :]
            cx, cy, length = [jnp.broadcast_to(row[n : n + 1], (8, 128)) for n in range(3)]
            centre.append((cx, cy))
            lengths.append(length)
        chunks = lax.div(longest + 31, 32)

        def gather(step, carry):
            for b, i in [(b, step * 2 + n) for n in range(2) for b in both]:
                units = [ix_ref[b, pl.ds(unit0 + i * 2 + n, 1), :] for n in range(2)]
                index = jnp.concatenate(units, axis=1)
                one = jnp.where(row_low == (index & 127), 1.0, 0.0).astype(BF16)
                got = dot(two_ref[b], jnp.concatenate([one, one], axis=0), NN)
                for n in range(2):
                    lanes = slice(n * 128, n * 128 + 128)
                    unit = jnp.broadcast_to(units[n], (8, 128))
                    low = unit & 127
                    high = unit >> 7
                    odd = (high & 1) == 1
                    exact = zero8
                    near = zero8
                    last = zero8
                    for h in range(16):
                        rows = slice(h * 8, h * 8 + 8)
                        hit = (high >> 1) == h
                        exact = jnp.where(hit, take_lanes(tab_ref[b, rows, :], low), exact)
                        near = jnp.where(hit, got[rows, lanes], near)
                    for h in range(4):
                        rows = slice(128 + h * 8, 136 + h * 8)
                        last = jnp.where((high >> 3) == h, got[rows, lanes], last)
                    last = jnp.sum(
                        jnp.where(sub == (high & 7), last, 0.0), axis=0, keepdims=True
                    )
                    feats = jnp.where(
                        sub < 4,
                        jnp.where(odd, pltpu.roll(exact, 4, 0), exact),
                        jnp.where(odd, near, pltpu.roll(near, 4, 0)),
                    )
                    j = i * 2 + n
                    fr_ref[b, pl.ds(j, 8, stride=16), :] = feats
                    fr_ref[b, pl.ds(128 + j, 1), :] = last
            return carry

        lax.fori_loop(0, lax.div(chunks + 1, 2), gather, 0)

        for b in both:
            cx, cy = centre[b]
            for part in range(2):
                c0 = part * 8

                def got(f, b=b, c0=c0):
                    return fr_ref[b, f * 16 + c0 : f * 16 + c0 + 8, :]

                u = got(0) - cx
                v = got(1) - cy
                con_a, con_b, con_c = [got(f) for f in range(2, 5)]
                fr_ref[b, c0 : c0 + 8, :] = u
                fr_ref[b, 16 + c0 : 16 + c0 + 8, :] = v
                live = (lane_k + (sub + c0) * 16).astype(F32) < lengths[b]
                coefs = [
                    con_a * (-0.5 * LOG2_E),
                    con_b * -LOG2_E,
                    con_c * (-0.5 * LOG2_E),
                    (con_a * u + con_b * v) * LOG2_E,
                    (con_b * u + con_c * v) * LOG2_E,
                    jnp.where(
                        live,
                        (got(5) - 0.5 * (con_a * u * u + con_c * v * v) - con_b * u * v) * LOG2_E,
                        -1e30,
                    ),
                ]
                for f, value in enumerate(coefs):
                    hi, rest = split2(value)
                    mid, lo = split2(rest)
                    for p, piece in enumerate((hi, mid, lo)):
                        co_ref[b, pl.ds(c0 * 32 + p * 8 + f, 8, stride=32), :] = piece
                for channel, shade in enumerate((got(6), got(7), got(8))):
                    hi, lo = split2(shade)
                    cc_ref[b, pl.ds(c0 * 8 + channel, 8, stride=8), :] = hi
                    cc_ref[b, pl.ds(c0 * 8 + 3 + channel, 8, stride=8), :] = lo

        def colours_of(b, i):
            rows = cc_ref[b, pl.ds(pl.multiple_of(i * 16, 16), 16), :]
            return jnp.concatenate(
                [
                    jnp.concatenate(
                        [jnp.where(diag, rows[n * 8 + r : n * 8 + r + 1], 0.0) for r in range(6)],
                        axis=0,
                    )
                    for n in range(2)
                ],
                axis=1,
            ).astype(BF16)

        def fade(b, i):
            row0 = pl.multiple_of(i * 256, 256)
            pair = co_ref[b, pl.ds(pl.multiple_of(i * 64, 64), 64), :].astype(BF16)
            lhs = jnp.concatenate([pair[0:32], pair[32:64]], axis=1)
            al_ref[b, pl.ds(row0, 256), :] = jnp.exp2(dot(lhs, basis_b, TN))

        def weigh(b, i, through):
            row0 = pl.multiple_of(i * 256, 256)
            alphas = al_ref[b, pl.ds(row0, 256), :]
            weights = []
            for k in range(32):
                weight = through * alphas[k * 8 : k * 8 + 8]
                through = through - weight
                weights.append(weight)
            weight = jnp.concatenate(weights, axis=0)
            w_hi, w_lo = split2(weight)
            w_ref[b, pl.ds(row0, 256), :] = weight
            ww_ref[b, pl.ds(row0, 256), 0:256] = w_hi.astype(BF16)
            ww_ref[b, pl.ds(row0, 256), 256:512] = w_lo.astype(BF16)
            return through

        def shade(b, i, colour):
            row0 = pl.multiple_of(i * 256, 256)
            c_two = colours_of(b, i)
            prod = dot(c_two, ww_ref[b, pl.ds(row0, 256), 0:256], NN)
            prod_lo = dot(c_two, ww_ref[b, pl.ds(row0, 256), 256:512], NN)
            return colour + prod[0:24] + prod[24:48] + prod_lo[0:24] + prod_lo[24:48]

        def forward(i, carry):
            carry = list(carry)
            colours = [shade(b, i - 1, carry[b][1]) for b in both]
            through = [weigh(b, i, carry[b][0]) for b in both]
            for b in both:
                fade(b, i + 1)
            return tuple((through[b], colours[b]) for b in both)

        for b in both:
            fade(b, 0)
        start = [weigh(b, 0, jnp.ones((8, 256), F32)) for b in both]
        for b in both:
            fade(b, 1)
        dark = jnp.zeros((24, 256), F32)
        done = lax.fori_loop(1, chunks, forward, tuple((start[b], dark) for b in both))
        done = [(None, shade(b, chunks - 1, done[b][1])) for b in both]
        r_four = []
        for b in both:
            resid = done[b][1] - aim_ref[b, pl.ds(pl.multiple_of(group_no * 24, 8), 24), :]
            err_ref[b] += resid * resid
            r_hi, r_lo = split2(2.0 * resid)
            r_four.append(jnp.concatenate([r_hi, r_hi, r_lo, r_lo], axis=0).astype(BF16))
            r_t = jnp.transpose(
                jnp.concatenate([r_hi, r_lo, jnp.zeros((80, 256), F32)], axis=0)
            ).astype(BF16)
            rt_ref[b, 0:256, :] = r_t
            rt_ref[b, 256:512, :] = r_t

        def pull(b, i):
            c_two = colours_of(b, i)
            pl_ref[b] = dot(jnp.concatenate([c_two, c_two], axis=0), r_four[b], TN)

        def slope(b, i, behind):
            row0 = pl.multiple_of(i * 256, 256)
            pulls = pl_ref[b]
            alphas = al_ref[b, pl.ds(row0, 256), :]
            weight = w_ref[b, pl.ds(row0, 256), :]
            parts = []
            for k in range(31, -1, -1):
                diff = pulls[k * 8 : k * 8 + 8] - behind
                parts.append(weight[k * 8 : k * 8 + 8] * diff)
                behind = behind + alphas[k * 8 : k * 8 + 8] * diff
            d_hi, d_lo = split2(jnp.concatenate(parts[::-1], axis=0))
            dd_ref[b, :, 0:256] = d_hi.astype(BF16)
            dd_ref[b, :, 256:512] = d_lo.astype(BF16)
            return behind

        def collect(b, i):
            row0 = pl.multiple_of(i * 256, 256)
            mom = dot(basis_2, dd_ref[b], NT)
            sums = jnp.where(own, dot(ww_ref[b, pl.ds(row0, 256), :], rt_ref[b], NN), 0.0)
            for n in range(2):
                flip = jnp.transpose(sums[n * 128 : n * 128 + 128])
                j = i * 2 + n
                mo_ref[b, pl.ds(j, 8, stride=16), :] = mom[0:8, n * 128 : n * 128 + 128]
                for h in range(3):
                    mo_ref[b, pl.ds((8 + h) * 16 + j, 1), :] = jnp.sum(
                        flip[h * 8 : h * 8 + 8] + flip[24 + h * 8 : 32 + h * 8],
                        axis=0,
                        keepdims=True,
                    )

        def backward(step, carry):
            i = chunks - 1 - step
            for b in both:
                collect(b, i + 1)
            carry = tuple(slope(b, i, carry[b]) for b in both)
            for b in both:
                pull(b, jnp.maximum(i - 1, 0))
            return carry

        for b in both:
            pull(b, chunks - 1)
        start = tuple(slope(b, chunks - 1, jnp.zeros((8, 256), F32)) for b in both)
        for b in both:
            pull(b, jnp.maximum(chunks - 2, 0))
        lax.fori_loop(1, chunks, backward, start)
        for b in both:
            collect(b, 0)

        for b in both:
            for part in range(2):
                c0 = part * 8

                def moment(f, b=b, c0=c0):
                    return mo_ref[b, f * 16 + c0 : f * 16 + c0 + 8, :]

                u, v, con_a, con_b, con_c = [
                    fr_ref[b, f * 16 + c0 : f * 16 + c0 + 8, :] for f in range(5)
                ]
                m_xx, m_xy, m_yy, m_x, m_y, m_1 = [moment(f) for f in range(6)]
                s_x = m_x - u * m_1
                s_y = m_y - v * m_1
                grads = [
                    con_a * s_x + con_b * s_y,
                    con_b * s_x + con_c * s_y,
                    -0.5 * (m_xx - u * (m_x + s_x)),
                    -(m_xy - u * m_y - v * s_x),
                    -0.5 * (m_yy - v * (m_y + s_y)),
                    m_1,
                    moment(8),
                    moment(9),
                    moment(10),
                ]
                used = (sub + c0) < 2 * chunks
                for f, value in enumerate(grads):
                    hi, lo = split2(jnp.where(used, value, 0.0))
                    gr_ref[b, f * 16 + c0 : f * 16 + c0 + 8, :] = hi
                    gr_ref[b, 144 + f * 16 + c0 : 144 + f * 16 + c0 + 8, :] = lo

        def scatter(step, carry):
            for b in both:
                total = None
                for n in range(2):
                    j = step * 4 + n * 2
                    index = jnp.concatenate(
                        [ix_ref[b, pl.ds(unit0 + j + n, 1), :] for n in range(2)], axis=1
                    )
                    hit = row_a == (index >> 8)
                    rows = []
                    for f in range(18):
                        row = f * 16 + j
                        value = jnp.concatenate(
                            [gr_ref[b, pl.ds(row, 1), :], gr_ref[b, pl.ds(row + 1, 1), :]], axis=1
                        )
                        rows.append(jnp.where(hit, value, 0.0))
                    add = dot(jnp.concatenate(rows, axis=0).astype(BF16), scatter_rhs(index), NT)
                    add = add[0:144] + add[144:288]
                    total = add if total is None else total + add
                for half in range(2):
                    sg_ref[b, half, 0:144, :] += total[:, half * 128 : half * 128 + 128]
            return carry

        lax.fori_loop(0, lax.div(chunks + 1, 2), scatter, 0)
        return carry

    lax.fori_loop(0, GROUPS, group, 0)
    for b in both:
        total = jnp.sum(jnp.sum(err_ref[b], axis=0, keepdims=True), axis=1, keepdims=True)
        for half in range(2):
            sg_ref[b, half, 144:160, :] = view_ref[b, pl.ds(half, 16, stride=2), :]
            sg_ref[b, half, 240:256, :] = jnp.broadcast_to(total, (16, 128))

    for a in range(16):
        for half in range(2):
            parts = [
                sg_ref[b, half, pl.ds(q * 128 + a, 8, stride=16), :]
                for b in both
                for q in range(2)
            ]
            for r in range(4):
                out_ref[(a * 2 + half) * 4 + r] = by_quarter(
                    quarter, [turn(parts[q], q - r) for q in range(4)]
                )


def grads_kernel(
    cam_ref, params_ref, send_ref, grad_ref, out_ref, err_ref, flat_ref, res_ref, gg_ref, sems
):
    copies = fetch_params(params_ref, flat_ref, sems)
    row_a = lax.broadcasted_iota(jnp.int32, (16, 256), 0)
    quarter = lax.broadcasted_iota(jnp.int32, (8, 128), 1) >> 5
    gg_ref[...] = jnp.zeros(gg_ref.shape, F32)

    def place(step, total):
        tiles_of = [[grad_ref[step * 16 + n * 8 + i] for i in range(8)] for n in range(2)]
        for tile in tiles_of[0] + tiles_of[1]:
            total = total + tile
        sums = [None] * BATCHES
        for part, batch_no in [(n, b) for n in range(2) for b in range(BATCHES)]:
            tiles = tiles_of[part]
            index = send_ref[batch_no, pl.ds(step * 2 + part, 1), :]
            hit = row_a == (index >> 8)
            rhs = scatter_rhs(index)
            high = []
            low = []
            for q in range(2):
                values = jnp.concatenate(
                    [
                        by_quarter(
                            quarter,
                            [turn(tiles[4 * n + i], i - 2 * batch_no - q) for i in range(4)],
                        )
                        for n in range(2)
                    ],
                    axis=1,
                )
                g_hi, g_lo = split2(values)
                for f in range(8 if q == 0 else 2):
                    high.append(jnp.where(hit, g_hi[f : f + 1], 0.0))
                    low.append(jnp.where(hit, g_lo[f : f + 1], 0.0))
            add = dot(jnp.concatenate(high + low, axis=0).astype(BF16), rhs, NT)
            add = add[0:160] + add[160:320]
            sums[batch_no] = add if part == 0 else sums[batch_no] + add
        for batch_no in range(BATCHES):
            gg_ref[batch_no] += sums[batch_no]
        return total

    total = lax.fori_loop(0, 8, place, jnp.zeros((8, 128), F32))
    for copy in copies:
        copy.wait()

    def block(block_no, carry):
        row0 = pl.multiple_of((block_no // 2) * 8, 8)
        half = block_no % 2
        lane0 = pl.multiple_of(half * 128, 128)
        cols = [param_rows(flat_ref, row0, half, p) for p in range(PARAMS)]
        geo = [0.0] * 10
        opac = 0.0
        shade = [0.0] * 48
        for batch_no in range(BATCHES):

            def feat(f, batch_no=batch_no):
                return gg_ref[batch_no, pl.ds(f * 16 + row0, 8), pl.ds(lane0, 128)]

            cam = pick_camera(cam_ref, batch_no, feat(9))
            _, pull_geo = jax.vjp(
                lambda c: screen_terms(c[0:3], shape_terms(c), cam), cols[0:10]
            )
            (d_geo,) = pull_geo(tuple(feat(f) for f in range(5)))
            basis, pull_ray = jax.vjp(lambda c: ray_basis(c, cam), cols[0:3])
            d_col = [feat(6 + h) for h in range(3)]
            (d_ray,) = pull_ray(
                [
                    d_col[0] * cols[11 + k] + d_col[1] * cols[27 + k] + d_col[2] * cols[43 + k]
                    for k in range(16)
                ]
            )
            for i in range(10):
                geo[i] = geo[i] + d_geo[i]
            for i in range(3):
                geo[i] = geo[i] + d_ray[i]
            opac = opac + feat(5)
            for h in range(3):
                for k in range(16):
                    shade[16 * h + k] = shade[16 * h + k] + d_col[h] * basis[k]
        opac = opac / (1.0 + jnp.exp(cols[10]))
        for p, value in enumerate(geo + [opac] + shade):
            res_ref[pl.ds((2 * row0 + half) * PITCH + p, 8, stride=2 * PITCH), :] = value
        return carry

    copies = [
        pltpu.make_async_copy(
            res_ref.at[pl.ds(j * PITCH, PARAMS), :],
            out_ref.at[:, pl.ds(j * 128, 128)],
            sems.at[j],
        )
        for j in range(32)
    ]
    for part in range(2):
        lax.fori_loop(part * 2, part * 2 + 2, block, 0)
        for copy in copies[part * 16 : part * 16 + 16]:
            copy.start()
    lane = lax.broadcasted_iota(jnp.int32, (1, 128), 1)
    errors = jnp.sum(
        jnp.where((lane == 32) | (lane == 96), total[7:8], 0.0), axis=1, keepdims=True
    )
    err_ref[...] = errors * (1.0 / (BATCHES * OWNERS * TILES_DEV * 3 * TILE_PX))
    for copy in copies:
        copy.wait()


def exchange(values):
    return lax.all_to_all(values, "dev", split_axis=0, concat_axis=0, tiled=True)


SMEM = pl.BlockSpec(memory_space=pltpu.SMEM)
VMEM = pl.BlockSpec(memory_space=pltpu.VMEM)
HBM = pl.BlockSpec(memory_space=pltpu.HBM)
CALL = pltpu.CompilerParams(vmem_limit_bytes=16 * 1024 * 1024)
OFFER_CALL = pltpu.CompilerParams(vmem_limit_bytes=60 * 1024 * 1024)
BLEND_CALL = pltpu.CompilerParams(vmem_limit_bytes=28 * 1024 * 1024)


def local(params, cameras, send_lists, tile_slots, tile_ids, tile_len, targets):
    lengths = tile_len[:, 0]
    tile_no = jnp.arange(TILES_DEV, dtype=jnp.int32)
    ahead = (lengths[:, None, :] > lengths[:, :, None]) | (
        (lengths[:, None, :] == lengths[:, :, None]) & (tile_no[None, None, :] < tile_no[None, :, None])
    )
    rank = jnp.sum(ahead.astype(jnp.int32), axis=2)
    order = jnp.sum(
        jnp.where(rank[:, None, :] == tile_no[None, :, None], tile_no[None, None, :], 0), axis=2
    )

    feats, cams, send = pl.pallas_call(
        offer_kernel,
        out_shape=(
            jax.ShapeDtypeStruct((OWNERS * 12, 128), F32),
            jax.ShapeDtypeStruct((CAM_ROWS * 8, 128), F32),
            jax.ShapeDtypeStruct((BATCHES, 16, 256), jnp.int32),
        ),
        in_specs=[VMEM, HBM, VMEM],
        out_specs=(VMEM, VMEM, VMEM),
        scratch_shapes=[
            pltpu.VMEM((32 * PITCH, 128), F32),
            pltpu.VMEM((BATCHES, 768, 128), F32),
            pltpu.VMEM((BATCHES, 512, 256), BF16),
            pltpu.SemaphoreType.DMA((32,)),
        ],
        compiler_params=OFFER_CALL,
        name="offer",
    )(cameras, params, jnp.transpose(send_lists, (0, 1, 3, 2)))
    feats = exchange(feats.reshape(OWNERS, 1, 1536)).reshape(OWNERS * 12, 128)

    views, slots, tiles, aims = pl.pallas_call(
        plan_kernel,
        out_shape=(
            jax.ShapeDtypeStruct((BATCHES, 32, 128), F32),
            jax.ShapeDtypeStruct((BATCHES, GROUPS * 16, 128), jnp.int32),
            jax.ShapeDtypeStruct((BATCHES, GROUPS * 8, 128), F32),
            jax.ShapeDtypeStruct((BATCHES, GROUPS * 24, 256), F32),
        ),
        in_specs=[SMEM, SMEM, SMEM, VMEM, VMEM],
        out_specs=(VMEM, VMEM, VMEM, VMEM),
        scratch_shapes=[pltpu.VMEM((BATCHES, 8, 256), jnp.int32)],
        compiler_params=CALL,
        name="plan",
    )(order, tile_ids, lengths, tile_slots, targets)

    rows = TILES_DEV // GROUPS * PAIRS
    slot_grads = pl.pallas_call(
        blend_kernel,
        out_shape=jax.ShapeDtypeStruct((OWNERS, 8, 128), F32),
        in_specs=[SMEM, SMEM, VMEM, VMEM, VMEM, VMEM, VMEM, VMEM],
        out_specs=VMEM,
        scratch_shapes=[
            pltpu.VMEM((BATCHES, 768, 128), F32),
            pltpu.VMEM((BATCHES, 288, 128), F32),
            pltpu.VMEM((BATCHES, 160, 256), BF16),
            pltpu.VMEM((BATCHES, 144, 128), F32),
            pltpu.VMEM((BATCHES, 576, 128), F32),
            pltpu.VMEM((BATCHES, 128, 128), F32),
            pltpu.VMEM((BATCHES, rows + 256, 256), F32),
            pltpu.VMEM((BATCHES, rows, 256), F32),
            pltpu.VMEM((BATCHES, rows, 512), BF16),
            pltpu.VMEM((BATCHES, 256, 256), F32),
            pltpu.VMEM((BATCHES, 256, 512), BF16),
            pltpu.VMEM((BATCHES, 512, 128), BF16),
            pltpu.VMEM((BATCHES, 176, 128), F32),
            pltpu.VMEM((BATCHES, 288, 128), F32),
            pltpu.VMEM((BATCHES, 2, 256, 128), F32),
            pltpu.VMEM((BATCHES, 24, 256), F32),
        ],
        compiler_params=BLEND_CALL,
        name="blend",
    )(order, lengths, cams, feats, views, slots, tiles, aims)
    slot_grads = exchange(slot_grads)

    grads, err = pl.pallas_call(
        grads_kernel,
        out_shape=(
            jax.ShapeDtypeStruct((PARAMS, 4096), F32),
            jax.ShapeDtypeStruct((1, 1), F32),
        ),
        in_specs=[VMEM, HBM, VMEM, VMEM],
        out_specs=(HBM, VMEM),
        scratch_shapes=[
            pltpu.VMEM((32 * PITCH, 128), F32),
            pltpu.VMEM((32 * PITCH, 128), F32),
            pltpu.VMEM((BATCHES, 160, 256), F32),
            pltpu.SemaphoreType.DMA((32,)),
        ],
        compiler_params=CALL,
        name="param_grads",
    )(cams, params, send, slot_grads)
    return (grads, err[0, 0])


def solution(mesh):
    placed = (
        P(None, "dev"),
        P(),
        P(None, "dev", None, None),
        P(None, "dev", None),
        P(None, "dev"),
        P(None, "dev", None),
        P(None, "dev", None, None),
    )
    return jax.shard_map(
        local, mesh=mesh, in_specs=placed, out_specs=(P(None, "dev"), P()), check_vma=False
    )
```

```python
import jax
import jax.numpy as jnp
from jax import lax
from jax.experimental import pallas as pl
from jax.experimental.pallas import tpu as pltpu
from jax.sharding import PartitionSpec as P

BATCHES = 2
TILE = 16
PAIRS = 256
TILE_PX = 256
TILES_X = 240
TILES_VIEW = 32400
VIEWS = 4
PARAMS = 59
TILES_DEV = 32
OWNERS = 128
CAP = 32
SLOTS = 4096
GROUPS = 4
PITCH = 72
LOG2_E = 1.4426950408889634

SH_ZERO = 0.28209479177387814
SH_ONE = 0.4886025119029199
SH_TWO = (
    1.0925484305920792,
    -1.0925484305920792,
    0.31539156525252005,
    -1.0925484305920792,
    0.5462742152960396,
)
SH_THREE = (
    -0.5900435899266435,
    2.890611442640554,
    -0.4570457994644658,
    0.3731763325901154,
    -0.4570457994644658,
    1.445305721320277,
    -0.5900435899266435,
)

F32 = jnp.float32
BF16 = jnp.bfloat16
NN = (((1,), (0,)), ((), ()))
NT = (((1,), (1,)), ((), ()))
TN = (((0,), (0,)), ((), ()))


def dot(lhs, rhs, dims):
    return lax.dot_general(lhs, rhs, dims, preferred_element_type=F32)


def split2(value):
    high = value.astype(BF16).astype(F32)
    return high, value - high


def camera_table(cameras):
    fields = [jnp.broadcast_to(cameras[:, n : n + 1], (8, 128)) for n in range(8)]
    cos_yaw = jnp.cos(fields[0])
    sin_yaw = jnp.sin(fields[0])
    cos_pitch = jnp.cos(fields[1])
    sin_pitch = jnp.sin(fields[1])
    frame = [
        cos_yaw,
        sin_yaw,
        sin_pitch * sin_yaw,
        cos_pitch,
        -sin_pitch * cos_yaw,
        -cos_pitch * sin_yaw,
        sin_pitch,
        cos_pitch * cos_yaw,
    ]
    shift = fields[2:5]
    centre = [
        -(frame[0] * shift[0] + frame[2] * shift[1] + frame[5] * shift[2]),
        -(frame[3] * shift[1] + frame[6] * shift[2]),
        -(frame[1] * shift[0] + frame[4] * shift[1] + frame[7] * shift[2]),
    ]
    return frame + shift + centre + fields[5:8]


CAM_ROWS = 17


def sh_basis(dir_x, dir_y, dir_z):
    square_x = dir_x * dir_x
    square_y = dir_y * dir_y
    square_z = dir_z * dir_z
    return [
        SH_ZERO * jnp.ones_like(dir_x),
        -SH_ONE * dir_y,
        SH_ONE * dir_z,
        -SH_ONE * dir_x,
        SH_TWO[0] * dir_x * dir_y,
        SH_TWO[1] * dir_y * dir_z,
        SH_TWO[2] * (2.0 * square_z - square_x - square_y),
        SH_TWO[3] * dir_x * dir_z,
        SH_TWO[4] * (square_x - square_y),
        SH_THREE[0] * dir_y * (3.0 * square_x - square_y),
        SH_THREE[1] * dir_x * dir_y * dir_z,
        SH_THREE[2] * dir_y * (4.0 * square_z - square_x - square_y),
        SH_THREE[3] * dir_z * (2.0 * square_z - 3.0 * square_x - 3.0 * square_y),
        SH_THREE[4] * dir_x * (4.0 * square_z - square_x - square_y),
        SH_THREE[5] * dir_z * (square_x - square_y),
        SH_THREE[6] * dir_x * (square_x - 3.0 * square_y),
    ]


def shape_terms(cols):
    inv_quat = 1.0 / jnp.sqrt(
        cols[6] * cols[6] + cols[7] * cols[7] + cols[8] * cols[8] + cols[9] * cols[9]
    )
    return [jnp.exp(cols[3 + i]) for i in range(3)] + [cols[6 + i] * inv_quat for i in range(4)]


def screen_terms(position, shape, cam):
    spread = shape[0:3]
    quat_w, quat_x, quat_y, quat_z = shape[3:7]
    frame = ((cam[0], None, cam[1]), (cam[2], cam[3], cam[4]), (cam[5], cam[6], cam[7]))
    shift = cam[8:11]
    focal = cam[14]
    viewed = [
        frame[0][0] * position[0] + frame[0][2] * position[2] + shift[0],
        frame[1][0] * position[0]
        + frame[1][1] * position[1]
        + frame[1][2] * position[2]
        + shift[1],
        frame[2][0] * position[0]
        + frame[2][1] * position[1]
        + frame[2][2] * position[2]
        + shift[2],
    ]
    inv_depth = 1.0 / viewed[2]
    screen_u = focal * viewed[0] * inv_depth + cam[15]
    screen_v = focal * viewed[1] * inv_depth + cam[16]
    rotation = (
        (
            1.0 - 2.0 * (quat_y * quat_y + quat_z * quat_z),
            2.0 * (quat_x * quat_y - quat_w * quat_z),
            2.0 * (quat_x * quat_z + quat_w * quat_y),
        ),
        (
            2.0 * (quat_x * quat_y + quat_w * quat_z),
            1.0 - 2.0 * (quat_x * quat_x + quat_z * quat_z),
            2.0 * (quat_y * quat_z - quat_w * quat_x),
        ),
        (
            2.0 * (quat_x * quat_z - quat_w * quat_y),
            2.0 * (quat_y * quat_z + quat_w * quat_x),
            1.0 - 2.0 * (quat_x * quat_x + quat_y * quat_y),
        ),
    )
    jac_main = focal * inv_depth
    jac_u = -jac_main * viewed[0] * inv_depth
    jac_v = -jac_main * viewed[1] * inv_depth
    row_u = [
        jac_main * frame[0][0] + jac_u * frame[2][0],
        jac_u * frame[2][1],
        jac_main * frame[0][2] + jac_u * frame[2][2],
    ]
    row_v = [jac_main * frame[1][i] + jac_v * frame[2][i] for i in range(3)]
    along_u = [
        (row_u[0] * rotation[0][j] + row_u[1] * rotation[1][j] + row_u[2] * rotation[2][j])
        * spread[j]
        for j in range(3)
    ]
    along_v = [
        (row_v[0] * rotation[0][j] + row_v[1] * rotation[1][j] + row_v[2] * rotation[2][j])
        * spread[j]
        for j in range(3)
    ]
    cov_uu = along_u[0] * along_u[0] + along_u[1] * along_u[1] + along_u[2] * along_u[2] + 0.3
    cov_uv = along_u[0] * along_v[0] + along_u[1] * along_v[1] + along_u[2] * along_v[2]
    cov_vv = along_v[0] * along_v[0] + along_v[1] * along_v[1] + along_v[2] * along_v[2] + 0.3
    inv_det = 1.0 / (cov_uu * cov_vv - cov_uv * cov_uv)
    return screen_u, screen_v, cov_vv * inv_det, -cov_uv * inv_det, cov_uu * inv_det


def ray_basis(position, cam):
    ray = [position[i] - cam[11 + i] for i in range(3)]
    inv_len = 1.0 / jnp.sqrt(ray[0] * ray[0] + ray[1] * ray[1] + ray[2] * ray[2])
    return sh_basis(ray[0] * inv_len, ray[1] * inv_len, ray[2] * inv_len)


def camera_field(cam_ref, field, batch_no, view_no):
    row = field * 8 + batch_no * VIEWS + view_no
    return jnp.broadcast_to(cam_ref[row : row + 1, :], (8, 128))


def pick_camera(cam_ref, batch_no, view):
    picked = []
    for field in range(CAM_ROWS):
        value = camera_field(cam_ref, field, batch_no, VIEWS - 1)
        for view_no in range(VIEWS - 2, -1, -1):
            value = jnp.where(
                view == view_no, camera_field(cam_ref, field, batch_no, view_no), value
            )
        picked.append(value)
    return picked


def take_lanes(table, index):
    return jnp.take_along_axis(table, index, axis=1, mode="promise_in_bounds")


def by_quarter(quarter, values):
    out = values[0]
    for q in range(1, len(values)):
        out = jnp.where(quarter == q, values[q], out)
    return out


def turn(value, quarters):
    quarters = quarters % 4
    return value if quarters == 0 else pltpu.roll(value, 32 * quarters, 1)


def scatter_rhs(index):
    row = lax.broadcasted_iota(jnp.int32, (256, index.shape[1]), 0)
    return jnp.where(row == (index & 255), 1.0, 0.0).astype(BF16)


def fetch_params(params_ref, flat_ref, sems):
    copies = [
        pltpu.make_async_copy(
            params_ref.at[:, pl.ds(j * 128, 128)],
            flat_ref.at[pl.ds(j * PITCH, PARAMS), :],
            sems.at[j],
        )
        for j in range(32)
    ]
    for copy in copies:
        copy.start()
    return copies


def param_rows(flat_ref, row0, half, param):
    return flat_ref[pl.ds((2 * row0 + half) * PITCH + param, 8, stride=2 * PITCH), :]


def offer_kernel(
    camera_ref, params_ref, list_ref, out_ref, cam_ref, send_ref, flat_ref, tab_ref, two_ref, sems
):
    copies = fetch_params(params_ref, flat_ref, sems)
    quarter = lax.broadcasted_iota(jnp.int32, (8, 128), 1) >> 5
    upper = lax.broadcasted_iota(jnp.int32, (8, 128), 0) < 4
    row_low = lax.broadcasted_iota(jnp.int32, (128, 256), 0)
    place = (lax.broadcasted_iota(jnp.int32, (8, 128), 0) & 3) == quarter
    cameras = jnp.concatenate([camera_ref[0], camera_ref[1]], axis=0)
    for field, value in enumerate(camera_table(cameras)):
        cam_ref[field * 8 : field * 8 + 8, :] = value
    for batch_no in range(BATCHES):
        by_owner = jnp.transpose(
            jnp.concatenate([list_ref[batch_no, 0].astype(F32)] * 4, axis=0)
        )
        for chunk in range(16):
            lists = jnp.where(place, by_owner[chunk * 8 : chunk * 8 + 8], 0.0)
            for half in range(2):
                line = jnp.sum(lists[half * 4 : half * 4 + 4], axis=0, keepdims=True)
                send_ref[batch_no, chunk : chunk + 1, half * 128 : half * 128 + 128] = line.astype(
                    jnp.int32
                )

    def block(block_no, carry):
        row0 = (block_no // 2) * 8
        half = block_no % 2
        cols = [param_rows(flat_ref, row0, half, p) for p in range(PARAMS)]
        opac = -(jnp.maximum(-cols[10], 0.0) + jnp.log1p(jnp.exp(-jnp.abs(cols[10]))))
        shared = cols[0:3] + shape_terms(cols) + [opac]
        for batch_no in range(BATCHES):
            feats = list(shared)
            for view_no in range(VIEWS):
                cam = [
                    camera_field(cam_ref, field, batch_no, view_no) for field in range(CAM_ROWS)
                ]
                basis = ray_basis(cols[0:3], cam)
                for channel in range(3):
                    shade = 0.5
                    for term in range(16):
                        shade = shade + basis[term] * cols[11 + 16 * channel + term]
                    feats.append(shade)
            feats.append(jnp.zeros((8, 128), F32))
            for f, value in enumerate(feats):
                start = (2 * row0 + half) * 24 + f
                tab_ref[batch_no, pl.ds(start, 8, stride=48), :] = value
        return carry

    for part in range(2):
        for copy in copies[part * 16 : part * 16 + 16]:
            copy.wait()
        lax.fori_loop(part * 2, part * 2 + 2, block, 0)

    def pieces(step, carry):
        for batch_no in range(BATCHES):
            for n in range(8):
                h = step * 8 + n
                hi, mid = split2(tab_ref[batch_no, pl.ds(pl.multiple_of(h * 24 + 8, 8), 16), :])
                row = pl.multiple_of(h * 16, 16)
                two_ref[batch_no, pl.ds(row, 16), 0:128] = hi.astype(BF16)
                two_ref[batch_no, pl.ds(row, 16), 128:256] = mid.astype(BF16)
        return carry

    lax.fori_loop(0, 4, pieces, 0)

    def pick(chunk, carry):
        cut = []
        for batch_no in range(BATCHES):
            index = send_ref[batch_no, pl.ds(chunk, 1), :]
            high = jnp.broadcast_to(index >> 7, (8, 256))
            low = jnp.broadcast_to(index & 127, (8, 256))
            one = jnp.where(row_low == (index & 127), 1.0, 0.0).astype(BF16)
            one = jnp.concatenate([one, one], axis=0)
            exact = [jnp.zeros((8, 128), F32)] * 2
            acc = [jnp.zeros((8, 256), F32)] * 2
            for part in range(4):
                got = dot(two_ref[batch_no, part * 128 : part * 128 + 128, :], one, NN)
                for n in range(8):
                    h = part * 8 + n
                    hit = high == h
                    for q in range(2):
                        row = n * 16 + q * 8
                        acc[q] = jnp.where(hit, got[row : row + 8], acc[q])
                    rows = tab_ref[batch_no, h * 24 : h * 24 + 8, :]
                    for half in range(2):
                        lanes = slice(half * 128, half * 128 + 128)
                        exact[half] = jnp.where(
                            hit[:, lanes], take_lanes(rows, low[:, lanes]), exact[half]
                        )
            cut.append((exact, [[a[:, 0:128], a[:, 128:256]] for a in acc]))
        for half in range(2):
            heads = [cut[0][0][half], cut[0][1][0][half], cut[0][1][1][half], cut[1][0][half]]
            tails = [cut[1][1][q][half] for q in range(2)]
            folded = [pltpu.roll(tail, 4, 0) for tail in tails]
            main = []
            tail = []
            for r in range(4):
                main.append(by_quarter(quarter, [turn(heads[q], q - r) for q in range(4)]))
                tail.append(
                    by_quarter(
                        quarter,
                        [
                            turn(tails[0], -r),
                            turn(folded[0], 1 - r),
                            turn(tails[1], 2 - r),
                            turn(folded[1], 3 - r),
                        ],
                    )
                )
            for r in range(0, 4, 2):
                row0 = pl.multiple_of((chunk * 2 + half) * 48 + r * 12, 8)
                middle = pltpu.roll(main[r + 1], 4, 0)
                out_ref[pl.ds(row0, 8), :] = main[r]
                out_ref[pl.ds(row0 + 8, 8), :] = jnp.where(upper, tail[r], middle)
                out_ref[pl.ds(row0 + 16, 8), :] = jnp.where(
                    upper, middle, pltpu.roll(tail[r + 1], 4, 0)
                )
        return carry

    lax.fori_loop(0, 16, pick, 0)


def plan_kernel(
    order_ref, ids_ref, len_ref, slots_ref, target_ref,
    out_ref, ix_ref, tile_ref, aim_ref, sl_ref,
):
    lane = lax.broadcasted_iota(jnp.int32, (8, 128), 1)
    sub = lax.broadcasted_iota(jnp.int32, (8, 128), 0)
    diag = sub == (lane & 7)

    def group(group_no, carry):
        for b in range(BATCHES):
            cx = jnp.zeros((1, 128), F32)
            cy = jnp.zeros((1, 128), F32)
            length = jnp.zeros((1, 128), F32)
            for t in range(8):
                tile = order_ref[b, group_no * 8 + t]
                in_view = lax.rem(ids_ref[b, tile], TILES_VIEW)
                row_t = lax.div(in_view, TILES_X)
                col_t = in_view - row_t * TILES_X
                here = (lane[0:1] & 7) == t
                cx = jnp.where(here, (col_t * TILE + 8).astype(F32), cx)
                cy = jnp.where(here, (row_t * TILE + 8).astype(F32), cy)
                length = jnp.where(here, len_ref[b, tile].astype(F32), length)
                sl_ref[b, t : t + 1, :] = slots_ref[b, pl.ds(tile, 1), :]
                for channel in range(3):
                    aim_ref[b, pl.ds(group_no * 24 + channel * 8 + t, 1), :] = target_ref[
                        b, pl.ds(tile, 1), channel, :
                    ]
            tile_ref[b, pl.ds(pl.multiple_of(group_no * 8, 8), 8), :] = jnp.concatenate(
                [cx, cy, length, jnp.zeros((5, 128), F32)], axis=0
            )
            picks = []
            for j in range(16):
                half = (j // 8) * 128
                picked = take_lanes(sl_ref[b, :, half : half + 128], (lane >> 3) + (j % 8) * 16)
                picks.append(
                    jnp.sum(jnp.where(diag, picked.astype(F32), 0.0), axis=0, keepdims=True)
                )
            ix_ref[b, pl.ds(pl.multiple_of(group_no * 16, 16), 16), :] = jnp.concatenate(
                picks, axis=0
            ).astype(jnp.int32)
        return carry

    lax.fori_loop(0, GROUPS, group, 0)
    row_high = lax.broadcasted_iota(jnp.int32, (32, PAIRS), 0)
    row_low = lax.broadcasted_iota(jnp.int32, (128, PAIRS), 0)

    def step(tile_no, sums):
        out = []
        for b in range(BATCHES):
            view = lax.div(ids_ref[b, tile_no], TILES_VIEW).astype(F32) * 0.5
            slots = slots_ref[b, pl.ds(tile_no, 1), :]
            lhs = jnp.where(row_high == (slots >> 7), view, 0.0).astype(BF16)
            rhs = jnp.where(row_low == (slots & 127), 1.0, 0.0).astype(BF16)
            out.append(sums[b] + dot(lhs, rhs, NT))
        return tuple(out)

    zero = jnp.zeros((32, 128), F32)
    sums = lax.fori_loop(0, TILES_DEV, step, (zero, zero))
    for b in range(BATCHES):
        out_ref[b] = sums[b]


def blend_kernel(
    order_ref, len_ref, cam_ref, feat_ref, view_ref, ix_ref, tile_ref, aim_ref, out_ref,
    sf_ref, tab_ref, two_ref, fr_ref, co_ref, cc_ref,
    al_ref, w_ref, ww_ref, pl_ref, dd_ref, rt_ref, mo_ref, gr_ref, sg_ref, err_ref,
):
    lane = lax.broadcasted_iota(jnp.int32, (8, 128), 1)
    sub = lax.broadcasted_iota(jnp.int32, (8, 128), 0)
    quarter = lane >> 5
    diag = sub == (lane & 7)
    lane_k = lane >> 3
    row_a = lax.broadcasted_iota(jnp.int32, (16, 256), 0)
    row_low = lax.broadcasted_iota(jnp.int32, (128, 256), 0)
    pix = lax.broadcasted_iota(jnp.int32, (8, 256), 1)
    term = lax.broadcasted_iota(jnp.int32, (8, 256), 0)
    px = (pix & 15).astype(F32) - 7.5
    py = (pix >> 4).astype(F32) - 7.5
    basis = jnp.where(
        term == 0, px * px,
        jnp.where(
            term == 1, px * py,
            jnp.where(
                term == 2, py * py,
                jnp.where(term == 3, px, jnp.where(term == 4, py, jnp.where(term == 5, 1.0, 0.0))),
            ),
        ),
    )
    basis_b = jnp.concatenate([basis] * 4, axis=0).astype(BF16)
    basis_2 = jnp.concatenate([jnp.concatenate([basis, basis], axis=1)] * 2, axis=0).astype(BF16)
    row_t = lax.broadcasted_iota(jnp.int32, (256, 128), 0) & 7
    lane_t = lax.broadcasted_iota(jnp.int32, (256, 128), 1)
    own = (lane_t & 7) == row_t
    zero8 = jnp.zeros((8, 128), F32)
    both = range(BATCHES)

    sg_ref[...] = jnp.zeros(sg_ref.shape, F32)
    co_ref[...] = jnp.zeros(co_ref.shape, F32)
    err_ref[...] = jnp.zeros(err_ref.shape, F32)

    upper = sub < 4

    def table(step, carry):
        for n in range(4):
            high = step * 4 + n
            main = []
            tail = []
            for r in range(0, 4, 2):
                row0 = pl.multiple_of(high * 48 + r * 12, 8)
                tiles = [feat_ref[pl.ds(row0 + m * 8, 8), :] for m in range(3)]
                main.append(tiles[0])
                main.append(pltpu.roll(jnp.where(upper, tiles[2], tiles[1]), 4, 0))
                tail.append(tiles[1])
                tail.append(pltpu.roll(tiles[2], 4, 0))
            folded = [pltpu.roll(value, 4, 0) for value in tail]
            for q in range(4):
                sf_ref[q // 3, pl.ds((q % 3) * 256 + high, 8, stride=32), :] = by_quarter(
                    quarter, [turn(main[i], i - q) for i in range(4)]
                )
            for q in range(2):
                sf_ref[1, pl.ds((q + 1) * 256 + high, 8, stride=32), :] = by_quarter(
                    quarter,
                    [
                        jnp.where(
                            upper, turn(tail[i], i - 2 * q), turn(folded[i], i - 2 * q - 1)
                        )
                        for i in range(4)
                    ],
                )
        return carry

    lax.fori_loop(0, 8, table, 0)

    def screen(block, carry):
        row0 = pl.multiple_of(block * 8, 8)
        for b in both:

            def raw(f, b=b):
                return sf_ref[b, pl.ds(f * 32 + row0, 8), :]

            view = view_ref[b, pl.ds(row0, 8), :]
            cam = pick_camera(cam_ref, b, view)
            feats = list(
                screen_terms([raw(f) for f in range(3)], [raw(f) for f in range(3, 10)], cam)
            ) + [raw(10)]
            for channel in range(3):
                shade = raw(11 + channel)
                for view_no in range(1, VIEWS):
                    shade = jnp.where(view == view_no, raw(11 + 3 * view_no + channel), shade)
                feats.append(shade)
            for f in range(4):
                tab_ref[b, pl.ds(row0 * 4 + f, 8, stride=4), :] = feats[f]
                tab_ref[b, pl.ds(128 + row0 * 4 + f, 8, stride=4), :] = feats[4 + f]
            tab_ref[b, pl.ds(256 + row0, 8), :] = feats[8]
        return carry

    lax.fori_loop(0, 4, screen, 0)
    for b in both:
        hi, mid = split2(tab_ref[b, 128:288, :])
        two_ref[b, :, 0:128] = hi.astype(BF16)
        two_ref[b, :, 128:256] = mid.astype(BF16)

    def group(group_no, carry):
        longest = jnp.int32(0)
        centre = []
        lengths = []
        unit0 = group_no * 16
        for b in both:
            longest = jnp.maximum(longest, len_ref[b, order_ref[b, group_no * 8]])
            row = tile_ref[b, pl.ds(pl.multiple_of(group_no * 8, 8), 8), :]
            cx, cy, length = [jnp.broadcast_to(row[n : n + 1], (8, 128)) for n in range(3)]
            centre.append((cx, cy))
            lengths.append(length)
        chunks = lax.div(longest + 31, 32)

        def gather(step, carry):
            for b, i in [(b, step * 2 + n) for n in range(2) for b in both]:
                units = [ix_ref[b, pl.ds(unit0 + i * 2 + n, 1), :] for n in range(2)]
                index = jnp.concatenate(units, axis=1)
                one = jnp.where(row_low == (index & 127), 1.0, 0.0).astype(BF16)
                got = dot(two_ref[b], jnp.concatenate([one, one], axis=0), NN)
                for n in range(2):
                    lanes = slice(n * 128, n * 128 + 128)
                    unit = jnp.broadcast_to(units[n], (8, 128))
                    low = unit & 127
                    high = unit >> 7
                    odd = (high & 1) == 1
                    exact = zero8
                    near = zero8
                    last = zero8
                    for h in range(16):
                        rows = slice(h * 8, h * 8 + 8)
                        hit = (high >> 1) == h
                        exact = jnp.where(hit, take_lanes(tab_ref[b, rows, :], low), exact)
                        near = jnp.where(hit, got[rows, lanes], near)
                    for h in range(4):
                        rows = slice(128 + h * 8, 136 + h * 8)
                        last = jnp.where((high >> 3) == h, got[rows, lanes], last)
                    last = jnp.sum(
                        jnp.where(sub == (high & 7), last, 0.0), axis=0, keepdims=True
                    )
                    feats = jnp.where(
                        sub < 4,
                        jnp.where(odd, pltpu.roll(exact, 4, 0), exact),
                        jnp.where(odd, near, pltpu.roll(near, 4, 0)),
                    )
                    j = i * 2 + n
                    fr_ref[b, pl.ds(j, 8, stride=16), :] = feats
                    fr_ref[b, pl.ds(128 + j, 1), :] = last
            return carry

        lax.fori_loop(0, lax.div(chunks + 1, 2), gather, 0)

        for b in both:
            cx, cy = centre[b]
            for part in range(2):
                c0 = part * 8

                def got(f, b=b, c0=c0):
                    return fr_ref[b, f * 16 + c0 : f * 16 + c0 + 8, :]

                u = got(0) - cx
                v = got(1) - cy
                con_a, con_b, con_c = [got(f) for f in range(2, 5)]
                fr_ref[b, c0 : c0 + 8, :] = u
                fr_ref[b, 16 + c0 : 16 + c0 + 8, :] = v
                live = (lane_k + (sub + c0) * 16).astype(F32) < lengths[b]
                coefs = [
                    con_a * (-0.5 * LOG2_E),
                    con_b * -LOG2_E,
                    con_c * (-0.5 * LOG2_E),
                    (con_a * u + con_b * v) * LOG2_E,
                    (con_b * u + con_c * v) * LOG2_E,
                    jnp.where(
                        live,
                        (got(5) - 0.5 * (con_a * u * u + con_c * v * v) - con_b * u * v) * LOG2_E,
                        -1e30,
                    ),
                ]
                for f, value in enumerate(coefs):
                    hi, rest = split2(value)
                    mid, lo = split2(rest)
                    for p, piece in enumerate((hi, mid, lo)):
                        co_ref[b, pl.ds(c0 * 32 + p * 8 + f, 8, stride=32), :] = piece
                for channel, shade in enumerate((got(6), got(7), got(8))):
                    hi, lo = split2(shade)
                    cc_ref[b, pl.ds(c0 * 8 + channel, 8, stride=8), :] = hi
                    cc_ref[b, pl.ds(c0 * 8 + 3 + channel, 8, stride=8), :] = lo

        def colours_of(b, i):
            rows = cc_ref[b, pl.ds(pl.multiple_of(i * 16, 16), 16), :]
            return jnp.concatenate(
                [
                    jnp.concatenate(
                        [jnp.where(diag, rows[n * 8 + r : n * 8 + r + 1], 0.0) for r in range(6)],
                        axis=0,
                    )
                    for n in range(2)
                ],
                axis=1,
            ).astype(BF16)

        def fade(b, i):
            row0 = pl.multiple_of(i * 256, 256)
            pair = co_ref[b, pl.ds(pl.multiple_of(i * 64, 64), 64), :].astype(BF16)
            lhs = jnp.concatenate([pair[0:32], pair[32:64]], axis=1)
            al_ref[b, pl.ds(row0, 256), :] = jnp.exp2(dot(lhs, basis_b, TN))

        def weigh(b, i, through):
            row0 = pl.multiple_of(i * 256, 256)
            alphas = al_ref[b, pl.ds(row0, 256), :]
            weights = []
            for k in range(32):
                weight = through * alphas[k * 8 : k * 8 + 8]
                through = through - weight
                weights.append(weight)
            weight = jnp.concatenate(weights, axis=0)
            w_hi, w_lo = split2(weight)
            w_ref[b, pl.ds(row0, 256), :] = weight
            ww_ref[b, pl.ds(row0, 256), 0:256] = w_hi.astype(BF16)
            ww_ref[b, pl.ds(row0, 256), 256:512] = w_lo.astype(BF16)
            return through

        def shade(b, i, colour):
            row0 = pl.multiple_of(i * 256, 256)
            c_two = colours_of(b, i)
            prod = dot(c_two, ww_ref[b, pl.ds(row0, 256), 0:256], NN)
            prod_lo = dot(c_two, ww_ref[b, pl.ds(row0, 256), 256:512], NN)
            return colour + prod[0:24] + prod[24:48] + prod_lo[0:24] + prod_lo[24:48]

        def forward(i, carry):
            carry = list(carry)
            colours = [shade(b, i - 1, carry[b][1]) for b in both]
            through = [weigh(b, i, carry[b][0]) for b in both]
            for b in both:
                fade(b, i + 1)
            return tuple((through[b], colours[b]) for b in both)

        for b in both:
            fade(b, 0)
        start = [weigh(b, 0, jnp.ones((8, 256), F32)) for b in both]
        for b in both:
            fade(b, 1)
        dark = jnp.zeros((24, 256), F32)
        done = lax.fori_loop(1, chunks, forward, tuple((start[b], dark) for b in both))
        done = [(None, shade(b, chunks - 1, done[b][1])) for b in both]
        r_four = []
        for b in both:
            resid = done[b][1] - aim_ref[b, pl.ds(pl.multiple_of(group_no * 24, 8), 24), :]
            err_ref[b] += resid * resid
            r_hi, r_lo = split2(2.0 * resid)
            r_four.append(jnp.concatenate([r_hi, r_hi, r_lo, r_lo], axis=0).astype(BF16))
            r_t = jnp.transpose(
                jnp.concatenate([r_hi, r_lo, jnp.zeros((80, 256), F32)], axis=0)
            ).astype(BF16)
            rt_ref[b, 0:256, :] = r_t
            rt_ref[b, 256:512, :] = r_t

        def pull(b, i):
            c_two = colours_of(b, i)
            pl_ref[b] = dot(jnp.concatenate([c_two, c_two], axis=0), r_four[b], TN)

        def slope(b, i, behind):
            row0 = pl.multiple_of(i * 256, 256)
            pulls = pl_ref[b]
            alphas = al_ref[b, pl.ds(row0, 256), :]
            weight = w_ref[b, pl.ds(row0, 256), :]
            parts = []
            for k in range(31, -1, -1):
                diff = pulls[k * 8 : k * 8 + 8] - behind
                parts.append(weight[k * 8 : k * 8 + 8] * diff)
                behind = behind + alphas[k * 8 : k * 8 + 8] * diff
            d_hi, d_lo = split2(jnp.concatenate(parts[::-1], axis=0))
            dd_ref[b, :, 0:256] = d_hi.astype(BF16)
            dd_ref[b, :, 256:512] = d_lo.astype(BF16)
            return behind

        def collect(b, i):
            row0 = pl.multiple_of(i * 256, 256)
            mom = dot(basis_2, dd_ref[b], NT)
            sums = jnp.where(own, dot(ww_ref[b, pl.ds(row0, 256), :], rt_ref[b], NN), 0.0)
            for n in range(2):
                flip = jnp.transpose(sums[n * 128 : n * 128 + 128])
                j = i * 2 + n
                mo_ref[b, pl.ds(j, 8, stride=16), :] = mom[0:8, n * 128 : n * 128 + 128]
                for h in range(3):
                    mo_ref[b, pl.ds((8 + h) * 16 + j, 1), :] = jnp.sum(
                        flip[h * 8 : h * 8 + 8] + flip[24 + h * 8 : 32 + h * 8],
                        axis=0,
                        keepdims=True,
                    )

        def backward(step, carry):
            i = chunks - 1 - step
            for b in both:
                collect(b, i + 1)
            carry = tuple(slope(b, i, carry[b]) for b in both)
            for b in both:
                pull(b, jnp.maximum(i - 1, 0))
            return carry

        for b in both:
            pull(b, chunks - 1)
        start = tuple(slope(b, chunks - 1, jnp.zeros((8, 256), F32)) for b in both)
        for b in both:
            pull(b, jnp.maximum(chunks - 2, 0))
        lax.fori_loop(1, chunks, backward, start)
        for b in both:
            collect(b, 0)

        for b in both:
            for part in range(2):
                c0 = part * 8

                def moment(f, b=b, c0=c0):
                    return mo_ref[b, f * 16 + c0 : f * 16 + c0 + 8, :]

                u, v, con_a, con_b, con_c = [
                    fr_ref[b, f * 16 + c0 : f * 16 + c0 + 8, :] for f in range(5)
                ]
                m_xx, m_xy, m_yy, m_x, m_y, m_1 = [moment(f) for f in range(6)]
                s_x = m_x - u * m_1
                s_y = m_y - v * m_1
                grads = [
                    con_a * s_x + con_b * s_y,
                    con_b * s_x + con_c * s_y,
                    -0.5 * (m_xx - u * (m_x + s_x)),
                    -(m_xy - u * m_y - v * s_x),
                    -0.5 * (m_yy - v * (m_y + s_y)),
                    m_1,
                    moment(8),
                    moment(9),
                    moment(10),
                ]
                used = (sub + c0) < 2 * chunks
                for f, value in enumerate(grads):
                    hi, lo = split2(jnp.where(used, value, 0.0))
                    gr_ref[b, f * 16 + c0 : f * 16 + c0 + 8, :] = hi
                    gr_ref[b, 144 + f * 16 + c0 : 144 + f * 16 + c0 + 8, :] = lo

        def scatter(step, carry):
            for b in both:
                total = None
                for n in range(2):
                    j = step * 4 + n * 2
                    index = jnp.concatenate(
                        [ix_ref[b, pl.ds(unit0 + j + n, 1), :] for n in range(2)], axis=1
                    )
                    hit = row_a == (index >> 8)
                    rows = []
                    for f in range(18):
                        row = f * 16 + j
                        value = jnp.concatenate(
                            [gr_ref[b, pl.ds(row, 1), :], gr_ref[b, pl.ds(row + 1, 1), :]], axis=1
                        )
                        rows.append(jnp.where(hit, value, 0.0))
                    add = dot(jnp.concatenate(rows, axis=0).astype(BF16), scatter_rhs(index), NT)
                    add = add[0:144] + add[144:288]
                    total = add if total is None else total + add
                for half in range(2):
                    sg_ref[b, half, 0:144, :] += total[:, half * 128 : half * 128 + 128]
            return carry

        lax.fori_loop(0, lax.div(chunks + 1, 2), scatter, 0)
        return carry

    lax.fori_loop(0, GROUPS, group, 0)
    for b in both:
        total = jnp.sum(jnp.sum(err_ref[b], axis=0, keepdims=True), axis=1, keepdims=True)
        for half in range(2):
            sg_ref[b, half, 144:160, :] = view_ref[b, pl.ds(half, 16, stride=2), :]
            sg_ref[b, half, 240:256, :] = jnp.broadcast_to(total, (16, 128))

    for a in range(16):
        for half in range(2):
            parts = [
                sg_ref[b, half, pl.ds(q * 128 + a, 8, stride=16), :]
                for b in both
                for q in range(2)
            ]
            for r in range(4):
                out_ref[(a * 2 + half) * 4 + r] = by_quarter(
                    quarter, [turn(parts[q], q - r) for q in range(4)]
                )


def grads_kernel(
    cam_ref, params_ref, send_ref, grad_ref, out_ref, err_ref, flat_ref, res_ref, gg_ref, sems
):
    copies = fetch_params(params_ref, flat_ref, sems)
    row_a = lax.broadcasted_iota(jnp.int32, (16, 256), 0)
    quarter = lax.broadcasted_iota(jnp.int32, (8, 128), 1) >> 5
    gg_ref[...] = jnp.zeros(gg_ref.shape, F32)

    def place(step, total):
        tiles_of = [[grad_ref[step * 32 + n * 8 + i] for i in range(8)] for n in range(4)]
        for tile in sum(tiles_of, []):
            total = total + tile
        sums = [None] * BATCHES
        for part, batch_no in [(n, b) for n in range(4) for b in range(BATCHES)]:
            tiles = tiles_of[part]
            index = send_ref[batch_no, pl.ds(step * 4 + part, 1), :]
            hit = row_a == (index >> 8)
            rhs = scatter_rhs(index)
            high = []
            low = []
            for q in range(2):
                values = jnp.concatenate(
                    [
                        by_quarter(
                            quarter,
                            [turn(tiles[4 * n + i], i - 2 * batch_no - q) for i in range(4)],
                        )
                        for n in range(2)
                    ],
                    axis=1,
                )
                g_hi, g_lo = split2(values)
                for f in range(8 if q == 0 else 2):
                    high.append(jnp.where(hit, g_hi[f : f + 1], 0.0))
                    low.append(jnp.where(hit, g_lo[f : f + 1], 0.0))
            add = dot(jnp.concatenate(high + low, axis=0).astype(BF16), rhs, NT)
            add = add[0:160] + add[160:320]
            sums[batch_no] = add if part == 0 else sums[batch_no] + add
        for batch_no in range(BATCHES):
            gg_ref[batch_no] += sums[batch_no]
        return total

    total = lax.fori_loop(0, 4, place, jnp.zeros((8, 128), F32))
    for copy in copies:
        copy.wait()

    def block(block_no, carry):
        row0 = pl.multiple_of((block_no // 2) * 8, 8)
        half = block_no % 2
        lane0 = pl.multiple_of(half * 128, 128)
        cols = [param_rows(flat_ref, row0, half, p) for p in range(PARAMS)]
        geo = [0.0] * 10
        opac = 0.0
        shade = [0.0] * 48
        for batch_no in range(BATCHES):

            def feat(f, batch_no=batch_no):
                return gg_ref[batch_no, pl.ds(f * 16 + row0, 8), pl.ds(lane0, 128)]

            cam = pick_camera(cam_ref, batch_no, feat(9))
            _, pull_geo = jax.vjp(
                lambda c: screen_terms(c[0:3], shape_terms(c), cam), cols[0:10]
            )
            (d_geo,) = pull_geo(tuple(feat(f) for f in range(5)))
            basis, pull_ray = jax.vjp(lambda c: ray_basis(c, cam), cols[0:3])
            d_col = [feat(6 + h) for h in range(3)]
            (d_ray,) = pull_ray(
                [
                    d_col[0] * cols[11 + k] + d_col[1] * cols[27 + k] + d_col[2] * cols[43 + k]
                    for k in range(16)
                ]
            )
            for i in range(10):
                geo[i] = geo[i] + d_geo[i]
            for i in range(3):
                geo[i] = geo[i] + d_ray[i]
            opac = opac + feat(5)
            for h in range(3):
                for k in range(16):
                    shade[16 * h + k] = shade[16 * h + k] + d_col[h] * basis[k]
        opac = opac / (1.0 + jnp.exp(cols[10]))
        for p, value in enumerate(geo + [opac] + shade):
            res_ref[pl.ds((2 * row0 + half) * PITCH + p, 8, stride=2 * PITCH), :] = value
        return carry

    copies = [
        pltpu.make_async_copy(
            res_ref.at[pl.ds(j * PITCH, PARAMS), :],
            out_ref.at[:, pl.ds(j * 128, 128)],
            sems.at[j],
        )
        for j in range(32)
    ]
    for part in range(2):
        lax.fori_loop(part * 2, part * 2 + 2, block, 0)
        for copy in copies[part * 16 : part * 16 + 16]:
            copy.start()
    lane = lax.broadcasted_iota(jnp.int32, (1, 128), 1)
    errors = jnp.sum(
        jnp.where((lane == 32) | (lane == 96), total[7:8], 0.0), axis=1, keepdims=True
    )
    err_ref[...] = errors * (1.0 / (BATCHES * OWNERS * TILES_DEV * 3 * TILE_PX))
    for copy in copies:
        copy.wait()


def exchange(values):
    return lax.all_to_all(values, "dev", split_axis=0, concat_axis=0, tiled=True)


SMEM = pl.BlockSpec(memory_space=pltpu.SMEM)
VMEM = pl.BlockSpec(memory_space=pltpu.VMEM)
HBM = pl.BlockSpec(memory_space=pltpu.HBM)
CALL = pltpu.CompilerParams(vmem_limit_bytes=16 * 1024 * 1024)
OFFER_CALL = pltpu.CompilerParams(vmem_limit_bytes=60 * 1024 * 1024)
BLEND_CALL = pltpu.CompilerParams(vmem_limit_bytes=28 * 1024 * 1024)


def local(params, cameras, send_lists, tile_slots, tile_ids, tile_len, targets):
    lengths = tile_len[:, 0]
    tile_no = jnp.arange(TILES_DEV, dtype=jnp.int32)
    ahead = (lengths[:, None, :] > lengths[:, :, None]) | (
        (lengths[:, None, :] == lengths[:, :, None]) & (tile_no[None, None, :] < tile_no[None, :, None])
    )
    rank = jnp.sum(ahead.astype(jnp.int32), axis=2)
    order = jnp.sum(
        jnp.where(rank[:, None, :] == tile_no[None, :, None], tile_no[None, None, :], 0), axis=2
    )

    feats, cams, send = pl.pallas_call(
        offer_kernel,
        out_shape=(
            jax.ShapeDtypeStruct((OWNERS * 12, 128), F32),
            jax.ShapeDtypeStruct((CAM_ROWS * 8, 128), F32),
            jax.ShapeDtypeStruct((BATCHES, 16, 256), jnp.int32),
        ),
        in_specs=[VMEM, HBM, VMEM],
        out_specs=(VMEM, VMEM, VMEM),
        scratch_shapes=[
            pltpu.VMEM((32 * PITCH, 128), F32),
            pltpu.VMEM((BATCHES, 768, 128), F32),
            pltpu.VMEM((BATCHES, 512, 256), BF16),
            pltpu.SemaphoreType.DMA((32,)),
        ],
        compiler_params=OFFER_CALL,
        name="offer",
    )(cameras, params, jnp.transpose(send_lists, (0, 1, 3, 2)))
    feats = exchange(feats.reshape(OWNERS, 1, 1536)).reshape(OWNERS * 12, 128)

    views, slots, tiles, aims = pl.pallas_call(
        plan_kernel,
        out_shape=(
            jax.ShapeDtypeStruct((BATCHES, 32, 128), F32),
            jax.ShapeDtypeStruct((BATCHES, GROUPS * 16, 128), jnp.int32),
            jax.ShapeDtypeStruct((BATCHES, GROUPS * 8, 128), F32),
            jax.ShapeDtypeStruct((BATCHES, GROUPS * 24, 256), F32),
        ),
        in_specs=[SMEM, SMEM, SMEM, VMEM, VMEM],
        out_specs=(VMEM, VMEM, VMEM, VMEM),
        scratch_shapes=[pltpu.VMEM((BATCHES, 8, 256), jnp.int32)],
        compiler_params=CALL,
        name="plan",
    )(order, tile_ids, lengths, tile_slots, targets)

    rows = TILES_DEV // GROUPS * PAIRS
    slot_grads = pl.pallas_call(
        blend_kernel,
        out_shape=jax.ShapeDtypeStruct((OWNERS, 8, 128), F32),
        in_specs=[SMEM, SMEM, VMEM, VMEM, VMEM, VMEM, VMEM, VMEM],
        out_specs=VMEM,
        scratch_shapes=[
            pltpu.VMEM((BATCHES, 768, 128), F32),
            pltpu.VMEM((BATCHES, 288, 128), F32),
            pltpu.VMEM((BATCHES, 160, 256), BF16),
            pltpu.VMEM((BATCHES, 144, 128), F32),
            pltpu.VMEM((BATCHES, 576, 128), F32),
            pltpu.VMEM((BATCHES, 128, 128), F32),
            pltpu.VMEM((BATCHES, rows + 256, 256), F32),
            pltpu.VMEM((BATCHES, rows, 256), F32),
            pltpu.VMEM((BATCHES, rows, 512), BF16),
            pltpu.VMEM((BATCHES, 256, 256), F32),
            pltpu.VMEM((BATCHES, 256, 512), BF16),
            pltpu.VMEM((BATCHES, 512, 128), BF16),
            pltpu.VMEM((BATCHES, 176, 128), F32),
            pltpu.VMEM((BATCHES, 288, 128), F32),
            pltpu.VMEM((BATCHES, 2, 256, 128), F32),
            pltpu.VMEM((BATCHES, 24, 256), F32),
        ],
        compiler_params=BLEND_CALL,
        name="blend",
    )(order, lengths, cams, feats, views, slots, tiles, aims)
    slot_grads = exchange(slot_grads)

    grads, err = pl.pallas_call(
        grads_kernel,
        out_shape=(
            jax.ShapeDtypeStruct((PARAMS, 4096), F32),
            jax.ShapeDtypeStruct((1, 1), F32),
        ),
        in_specs=[VMEM, HBM, VMEM, VMEM],
        out_specs=(HBM, VMEM),
        scratch_shapes=[
            pltpu.VMEM((32 * PITCH, 128), F32),
            pltpu.VMEM((32 * PITCH, 128), F32),
            pltpu.VMEM((BATCHES, 160, 256), F32),
            pltpu.SemaphoreType.DMA((32,)),
        ],
        compiler_params=CALL,
        name="param_grads",
    )(cams, params, send, slot_grads)
    return (grads, err[0, 0])


def solution(mesh):
    placed = (
        P(None, "dev"),
        P(),
        P(None, "dev", None, None),
        P(None, "dev", None),
        P(None, "dev"),
        P(None, "dev", None),
        P(None, "dev", None, None),
    )
    return jax.shard_map(
        local, mesh=mesh, in_specs=placed, out_specs=(P(None, "dev"), P()), check_vma=False
    )
```
